32 devices in a mesh: dp: 16 (over z, y, x), tensor: 2 (over core).
Axes of the slice: x: 2, y: 2, z: 4, core: 2. Of those that a mesh axis runs over, the one named last changes fastest.
Arguments:
- tokens: bfloat16 [16384, 1536], P(('dp', 'tensor')), may hold values from -6 to 6
- routes: int32 [16384, 6], P('dp'), may hold values from 0 to 15, all different within a row; in each aligned block of 1024 rows (0 to 1023, 1024 to 2047, ...) at most 416 rows name the same one
- gain_in: float32 [1536], replicated, may hold values from 0.5 to 1.5
- w_zx: bfloat16 [1536, 2, 3072], P('dp', None, 'tensor'), may hold values from -0.15625 to 0.15625
- w_dt: bfloat16 [1536, 48], P('dp', 'tensor'), may hold values from -0.078125 to 0.078125
- w_bc: bfloat16 [1536, 256], P(('dp', 'tensor')), may hold values from -0.15625 to 0.15625
- conv_w: float32 [4, 3328], replicated, may hold values from -0.5 to 0.5
- conv_b: float32 [3328], replicated, may hold values from -2.5 to 2.5
- dt_bias: float32 [48], replicated, may hold values from -6.9 to -2.3
- a_log: float32 [48], replicated, may hold values from 0 to 2.7
- d_skip: float32 [48], replicated, may hold values from 0.5 to 1.5
- norm_gain: float32 [3072], replicated, may hold values from 0.5 to 1.5
- w_out: bfloat16 [3072, 1536], P('tensor', 'dp'), may hold values from -0.109375 to 0.109375
- gain_mid: float32 [1536], replicated, may hold values from 0.5 to 1.5
- router: bfloat16 [1536, 16], P(('dp', 'tensor')), may hold values from -0.078125 to 0.078125
- shared_gu: bfloat16 [1536, 2, 1024], P('dp', None, 'tensor'), may hold values from -0.15625 to 0.15625
- shared_down: bfloat16 [1024, 1536], P('tensor', 'dp'), may hold values from -0.25 to 0.25
- expert_gu: bfloat16 [16, 1536, 2, 512], P(None, 'dp', None, 'tensor'), may hold values from -0.15625 to 0.15625
- expert_down: bfloat16 [16, 512, 1536], P(None, 'tensor', 'dp'), may hold values from -0.5 to 0.5
- grad_out: bfloat16 [16384, 1536], P(('dp', 'tensor')), may hold values from -6 to 6
Outputs:
- output: bfloat16 [16384, 1536], P(('dp', 'tensor'))
- grad_tokens: bfloat16 [16384, 1536], P(('dp', 'tensor'))
- grad_gain_in: float32 [1536], replicated
- grad_w_zx: float32 [1536, 2, 3072], P('dp', None, 'tensor')
- grad_w_dt: float32 [1536, 48], P('dp', 'tensor')
- grad_w_bc: float32 [1536, 256], P(('dp', 'tensor'))
- grad_conv_w: float32 [4, 3328], replicated
- grad_conv_b: float32 [3328], replicated
- grad_dt_bias: float32 [48], replicated
- grad_a_log: float32 [48], replicated
- grad_d_skip: float32 [48], replicated
- grad_norm_gain: float32 [3072], replicated
- grad_w_out: float32 [3072, 1536], P('tensor', 'dp')
- grad_gain_mid: float32 [1536], replicated
- grad_router: float32 [1536, 16], P(('dp', 'tensor'))
- grad_shared_gu: float32 [1536, 2, 1024], P('dp', None, 'tensor')
- grad_shared_down: float32 [1024, 1536], P('tensor', 'dp')
- grad_expert_gu: float32 [16, 1536, 2, 512], P(None, 'dp', None, 'tensor')
- grad_expert_down: float32 [16, 512, 1536], P(None, 'tensor', 'dp')
The draws below stay inside these ranges and needn't reach their ends.
Inputs may be any that keep to these rules, and one draw needn't show every extreme that they name: `routes`: each row names 6 different experts; among the 1024 rows of one sequence no expert is named by more than 416 rows, a bound that some block reaches.
All inputs are finite; a program needn't handle non-finite values.
Results may differ from the reference program's by a relative error of at most 0.01.
Values may be sent and summed in bfloat16 or wider, within the bound.
No kernel may reach another device: no remote copies, remote signals or barrier semaphores. Data moves between devices by JAX's collectives and lax.ppermute only.
A program may use at most 576 MiB of HBM per device.

```python
import math
import jax
import jax.numpy as jnp
import numpy as np
from jax import lax

D = 1536
H = 48
P_SIZE = 64
NS = 128
CONV = 4
FE = 512
FS = 1024
TOPK = 6
EXPERTS = 16
BL = 128
SEQ = 1024
CAP = 416
TOKENS = 16384


def draw_dt_bias(key, part):
    key = jax.random.fold_in(key, 11)
    unit = jax.random.uniform(key, (H,), jnp.float32)
    return -6.9 + 4.6 * unit


def block_scale(own_key, dims, cuts, least, largest):
    gain, own = 1.0, jax.random.fold_in(own_key, 6)
    for dim, blocks in cuts:
        heights = jnp.exp(jax.random.uniform(jax.random.fold_in(own, dim), (blocks,), jnp.float32, least / len(cuts), largest / len(cuts)))
        gain = gain * jnp.repeat(heights, dims[dim] // blocks).reshape([-1 if axis == dim else 1 for axis in range(len(dims))])
    return gain


def assign_block(own_key, own, number, rows, count, top, limit, skew):
    ranking = jax.random.permutation(own_key, count)
    heavy_load, common = shares(count, rows * top, limit, skew, True), shares(count, rows * top, limit, skew, False)
    places = jnp.arange(count)

    def named(lengths, rotation):
        used = int((lengths > 0).sum())
        fixed = max(1, used // 4)
        passed = fixed + (places - fixed + rotation * (used - fixed)) % max(1, count - fixed)
        return jnp.zeros((count,), jnp.int32).at[ranking[jnp.where(places < fixed, places, passed)]].set(jnp.asarray(lengths, jnp.int32))

    lengths = jnp.where(number % 4 == 0, named(heavy_load, number // 4), named(common, number - number // 4 - 1))
    mixed = jax.random.permutation(jax.random.fold_in(own, 3), count)
    giver, receiver = mixed[0:count // 2 * 2:2], mixed[1:count // 2 * 2:2]
    slack = jnp.minimum(lengths[giver] - 1, limit - lengths[receiver]) // 2
    slack = jnp.where((giver == ranking[0]) | (receiver == ranking[0]) | (lengths[receiver] == 0), 0, jnp.maximum(slack, 0))
    passed = jax.random.randint(jax.random.fold_in(own, 4), (count // 2,), 0, 1 << 20) % (slack + 1)
    lengths = lengths.at[giver].add(-passed).at[receiver].add(passed)
    items = jnp.searchsorted(jnp.cumsum(lengths), jnp.arange(rows * top), side="right").astype(jnp.int32)
    table = items.reshape(top, rows).T
    table = table[jax.random.permutation(jax.random.fold_in(own, 1), rows)]
    rotation = jax.random.randint(jax.random.fold_in(own, 2), (rows, 1), 0, top)
    return jnp.take_along_axis(table, (jnp.arange(top)[None, :] + rotation) % top, axis=1)


def shares(number_of, total, limit, slope, full):
    portions = [(1 << 20) // math.isqrt(standing ** slope) + 1 for standing in range(1, number_of + 1)]
    largest = limit if full else min(limit, max(-(-total // number_of), total * portions[0] // sum(portions)))
    least = 1 if total - largest >= number_of - 1 else 0
    given, rest = [largest] + [least] * (number_of - 1), total - largest - least * (number_of - 1)
    while rest > 0:
        movable = [i for i in range(1, number_of) if given[i] < largest] or [i for i in range(1, number_of) if given[i] < limit]
        mass, left = sum([portions[i] for i in movable]), rest
        for i in movable:
            extra = min(limit - given[i], max(1, left * portions[i] // mass), rest)
            given[i] = given[i] + extra
            rest = rest - extra
    return np.array(given)


def gaussian(own_key, dims, width, reach, pieces=(), held_as=jnp.bfloat16):
    drawn = width * jax.random.normal(own_key, dims, jnp.float32)
    if pieces:
        drawn = drawn * block_scale(own_key, dims, pieces, -0.22, 0.18)
    return jnp.clip(drawn, -reach, reach).astype(held_as)


def setup_inputs(seed: int = 0) -> dict:
    seeds = jax.random.split(jax.random.key(seed), 21)
    tokens = gaussian(seeds[0], (TOKENS, D), 1.0, 6.0, ((0, 32),))
    routes_keys = jax.random.split(jax.random.fold_in(seeds[1], 1), TOKENS // SEQ)
    routes_turns = jax.random.permutation(jax.random.fold_in(seeds[1], 3), TOKENS // SEQ)
    routes = jax.vmap(lambda own, number: assign_block(jax.random.fold_in(seeds[1], 2), own, number, SEQ, EXPERTS, TOPK, CAP, 2))(routes_keys, routes_turns).reshape((TOKENS, TOPK))
    gain_in = jnp.clip(1.0 + 0.1 * jax.random.normal(seeds[2], (D,), jnp.float32), 0.5, 1.5)
    w_zx = gaussian(seeds[3], (D, 2, H * P_SIZE), D ** -0.5, 0.15625, ((0, 16), (2, 2)))
    w_dt = gaussian(seeds[4], (D, H), (4 * D) ** -0.5, 0.078125, ((0, 16), (1, 2)))
    w_bc = gaussian(seeds[5], (D, 2 * NS), D ** -0.5, 0.15625, ((0, 32),))
    conv_w = jnp.clip(jax.random.uniform(seeds[6], (CONV, H * P_SIZE + 2 * NS), jnp.float32, -0.5, 0.5), -0.5, 0.5)
    conv_b = gaussian(seeds[7], (H * P_SIZE + 2 * NS,), 0.3, 2.5, (), jnp.float32)
    dt_bias = draw_dt_bias(jax.random.fold_in(seeds[20], 71), 0)
    a_log = jnp.clip(jax.random.uniform(seeds[9], (H,), jnp.float32, 0.0, 2.7), 0.0, 2.7)
    d_skip = jnp.clip(jax.random.uniform(seeds[10], (H,), jnp.float32, 0.5, 1.5), 0.5, 1.5)
    norm_gain = jnp.clip(1.0 + 0.1 * jax.random.normal(seeds[11], (H * P_SIZE,), jnp.float32), 0.5, 1.5)
    w_out = gaussian(seeds[12], (H * P_SIZE, D), (H * P_SIZE) ** -0.5, 0.109375, ((0, 2), (1, 16)))
    gain_mid = jnp.clip(1.0 + 0.1 * jax.random.normal(seeds[13], (D,), jnp.float32), 0.5, 1.5)
    router = gaussian(seeds[14], (D, EXPERTS), (4 * D) ** -0.5, 0.078125, ((0, 32),))
    shared_gu = gaussian(seeds[15], (D, 2, FS), D ** -0.5, 0.15625, ((0, 16), (2, 2)))
    shared_down = gaussian(seeds[16], (FS, D), (FS // 2) ** -0.5, 0.25, ((0, 2), (1, 16)))
    expert_gu = gaussian(seeds[17], (EXPERTS, D, 2, FE), D ** -0.5, 0.15625, ((1, 16), (3, 2)))
    expert_down = gaussian(seeds[18], (EXPERTS, FE, D), (FE // 4) ** -0.5, 0.5, ((1, 2), (2, 16)))
    grad_out = gaussian(seeds[19], (TOKENS, D), 1.0, 6.0, ((0, 32),))
    return dict(tokens=tokens, routes=routes, gain_in=gain_in, w_zx=w_zx, w_dt=w_dt, w_bc=w_bc, conv_w=conv_w, conv_b=conv_b, dt_bias=dt_bias, a_log=a_log, d_skip=d_skip, norm_gain=norm_gain, w_out=w_out, gain_mid=gain_mid, router=router, shared_gu=shared_gu, shared_down=shared_down, expert_gu=expert_gu, expert_down=expert_down, grad_out=grad_out)


eps = 1e-05
highest = lax.Precision.HIGHEST

@jax.custom_vjp
def low(v):
    return lax.optimization_barrier(v.astype(jnp.bfloat16)).astype(jnp.float32)

@jax.custom_vjp
def low_back(v):
    return v

def low_keep(v):
    return (low(v), None)

def low_pass(kept, grad):
    return (grad,)

def back_keep(v):
    return (v, None)

def back_low(kept, grad):
    return (low(grad),)
low.defvjp(low_keep, low_pass)
low_back.defvjp(back_keep, back_low)

def full_dot(left_mat, right_mat):
    return jnp.dot(left_mat, right_mat, precision=highest)

def rms_norm(values, gain_vec):
    return values * lax.rsqrt(lax.optimization_barrier(jnp.mean(values * values, axis=-1, keepdims=True)) + eps) * gain_vec

def causal_conv(signal, kernel, bias_vec):
    conv_width = kernel.shape[0]
    length = signal.shape[0]
    padded = jnp.pad(signal, ((conv_width - 1, 0), (0, 0)))
    summed = jnp.zeros_like(signal) + bias_vec
    for offset in range(conv_width):
        summed = summed + kernel[offset] * padded[offset:offset + length]
    return summed

def ssd_block(carry_state, block_in):
    inputs, b_proj, c_proj, decay_log = block_in
    length = inputs.shape[0]
    cum_log = jnp.cumsum(decay_log, axis=0)
    row_pos = lax.broadcasted_iota(jnp.int32, (length, length), 0)
    col_pos = lax.broadcasted_iota(jnp.int32, (length, length), 1)
    causal = (col_pos <= row_pos)[:, :, None]
    log_gap = jnp.where(causal, cum_log[:, None, :] - cum_log[None, :, :], 0.0)
    scores = jnp.dot(c_proj, b_proj.T, precision=highest)
    weights = jnp.where(causal, jnp.exp(log_gap), 0.0) * scores[:, :, None]
    within = jnp.einsum('tsh,shp->thp', weights, inputs, precision=highest)
    across = jnp.einsum('tn,hnp->thp', c_proj, carry_state, precision=highest) * jnp.exp(cum_log)[:, :, None]
    to_end = jnp.exp(cum_log[-1][None, :] - cum_log)
    carried = carry_state * jnp.exp(cum_log[-1])[:, None, None]
    new_state = carried + jnp.einsum('sn,shp->hnp', b_proj, inputs * to_end[:, :, None], precision=highest)
    return (new_state, within + across)

def scan_heads(inputs, b_proj, c_proj, decay_log, block_fn):
    length, head_count, head_size = inputs.shape
    block_count = length // BL
    blocks = (inputs.reshape(block_count, BL, head_count, head_size), b_proj.reshape(block_count, BL, -1), c_proj.reshape(block_count, BL, -1), decay_log.reshape(block_count, BL, head_count))
    zero_state = jnp.zeros((head_count, b_proj.shape[1], head_size), jnp.float32)
    final_state, block_out = lax.scan(block_fn, zero_state, blocks)
    return block_out.reshape(length, head_count, head_size)

def mixer_front(normed, zx_w, dt_w, bc_w, conv_k, conv_bias, dt_shift, decay_rate, skip_gain, block_fn):
    local_width = zx_w.shape[2]
    head_count = dt_w.shape[1]
    state_size = bc_w.shape[1] // 2
    gate_z = low_back(full_dot(normed, zx_w[:, 0]))
    inner = low_back(full_dot(normed, zx_w[:, 1]))
    raw_dt = low_back(full_dot(normed, dt_w))
    proj_bc = full_dot(normed, bc_w)
    activated = jax.nn.silu(causal_conv(jnp.concatenate([inner, proj_bc], axis=1), conv_k, conv_bias))
    x_heads = activated[:, :local_width].reshape(-1, head_count, local_width // head_count)
    b_proj = activated[:, local_width:local_width + state_size]
    c_proj = activated[:, local_width + state_size:]
    step_size = jax.nn.softplus(raw_dt + dt_shift)
    decay_log = -step_size * jnp.exp(decay_rate)
    y_heads = scan_heads(x_heads * step_size[:, :, None], b_proj, c_proj, decay_log, block_fn)
    y_heads = y_heads + skip_gain[None, :, None] * x_heads
    gated_out = y_heads.reshape(-1, local_width) * jax.nn.silu(gate_z)
    return (gated_out, lax.optimization_barrier(jnp.sum(gated_out * gated_out, axis=1)))

def mixer_rear(gated_out, summed, gain_vec, out_w, full_width):
    scaled = low(gated_out * lax.rsqrt(summed[:, None] / full_width + eps) * gain_vec)
    return full_dot(scaled, out_w)

def slot_tables(routes):
    flat_ids = routes.reshape(-1)
    onehot = (flat_ids[:, None] == jnp.arange(EXPERTS, dtype=jnp.int32)[None, :]).astype(jnp.int32)
    before = jnp.cumsum(onehot, axis=0) - onehot
    place_in = lax.optimization_barrier(jnp.sum(before * onehot, axis=1)).astype(jnp.int32)
    slot_of = (flat_ids * CAP + place_in).astype(jnp.int32)
    token_of = jnp.arange(flat_ids.shape[0], dtype=jnp.int32) // routes.shape[1]
    slot_token = jnp.zeros((EXPERTS * CAP,), jnp.int32).at[slot_of].set(token_of)
    return (slot_of, slot_token)

def gate_values(normed, router_w, routes, slot_of):
    logits = full_dot(normed, router_w)
    picked = jnp.take_along_axis(logits, routes, axis=1)
    exp_vals = jnp.exp(picked - lax.optimization_barrier(jnp.max(picked, axis=1, keepdims=True)))
    gates = exp_vals / lax.optimization_barrier(jnp.sum(exp_vals, axis=1, keepdims=True))
    return jnp.zeros((EXPERTS * CAP,), jnp.float32).at[slot_of].set(gates.reshape(-1))

def experts_branch(mid_rows, routes, router_w, shared_gu, shared_down, expert_gu, expert_down):
    length = mid_rows.shape[0]
    slot_of, slot_token = slot_tables(routes)
    slot_gate = gate_values(mid_rows, router_w, routes, slot_of)
    buffers = mid_rows[slot_token].reshape(EXPERTS, CAP, D)
    gate_up = jnp.einsum('ecd,edkf->eckf', buffers, expert_gu, precision=highest)
    e_hidden = low(jax.nn.silu(low_back(gate_up[:, :, 0])) * low_back(gate_up[:, :, 1]))
    e_out = low_back(jnp.einsum('ecf,efd->ecd', e_hidden, expert_down, precision=highest))
    weighted = e_out.reshape(EXPERTS * CAP, D) * slot_gate[:, None]
    routed = jnp.zeros((length, D), jnp.float32).at[slot_token].add(weighted)
    shared_pre = full_dot(mid_rows, shared_gu.reshape(D, -1)).reshape(length, 2, -1)
    s_hidden = low(jax.nn.silu(low_back(shared_pre[:, 0])) * low_back(shared_pre[:, 1]))
    return routed + full_dot(s_hidden, shared_down)

def block_seq(seq_tokens, seq_routes, params):
    gain_in, w_zx, w_dt, w_bc, conv_w, conv_b, dt_bias, a_log, d_skip, norm_gain, w_out, gain_mid, router, shared_gu, shared_down, expert_gu, expert_down = params
    normed = low(rms_norm(seq_tokens, gain_in))
    gated_out, squares = mixer_front(normed, w_zx, w_dt, w_bc, conv_w, conv_b, dt_bias, a_log, d_skip, jax.checkpoint(ssd_block))
    resid = seq_tokens + low_back(mixer_rear(gated_out, squares, norm_gain, w_out, H * P_SIZE))
    mid_rows = low(rms_norm(resid, gain_mid))
    return resid + experts_branch(mid_rows, seq_routes, router, shared_gu, shared_down, expert_gu, expert_down)

def reference(tokens, routes, gain_in, w_zx, w_dt, w_bc, conv_w, conv_b, dt_bias, a_log, d_skip, norm_gain, w_out, gain_mid, router, shared_gu, shared_down, expert_gu, expert_down, grad_out):
    params = tuple((item.astype(jnp.float32) for item in (gain_in, w_zx, w_dt, w_bc, conv_w, conv_b, dt_bias, a_log, d_skip, norm_gain, w_out, gain_mid, router, shared_gu, shared_down, expert_gu, expert_down)))

    def forward(values, *weights):

        def one_seq(seq_pair):
            return block_seq(seq_pair[0], seq_pair[1], weights)
        seq_rows = values.reshape(-1, SEQ, D)
        seq_routes = routes.reshape(-1, SEQ, TOPK)
        return lax.map(jax.checkpoint(one_seq), (seq_rows, seq_routes)).reshape(-1, D)
    result, pull_back = jax.vjp(forward, tokens.astype(jnp.float32), *params)
    gradients = pull_back(grad_out.astype(jnp.float32))
    return (result.astype(jnp.bfloat16), gradients[0].astype(jnp.bfloat16), gradients[1], gradients[2], gradients[3], gradients[4], gradients[5], gradients[6], gradients[7], gradients[8], gradients[9], gradients[10], gradients[11], gradients[12], gradients[13], gradients[14], gradients[15], gradients[16], gradients[17])
```

```python
import functools

import jax
import jax.numpy as jnp
from jax import lax
from jax.experimental import pallas as pl
from jax.experimental.pallas import tpu as pltpu
from jax.sharding import PartitionSpec as P

F32 = jnp.float32
BF = jnp.bfloat16
EPS = 1e-05
H = 48
P_SIZE = 64
NS = 128
EXPERTS = 16
BL = 128
GROUP = 4
LANES = 128
VMEM = 60 * 1024 * 1024
highest = lax.Precision.HIGHEST


def nn(left, right):
    return lax.dot_general(left, right, (((1,), (0,)), ((), ())), preferred_element_type=F32)


def nt(left, right):
    return lax.dot_general(left, right, (((1,), (1,)), ((), ())), preferred_element_type=F32)


def tn(left, right, kind=F32):
    return lax.dot_general(left, right, (((0,), (0,)), ((), ())), preferred_element_type=kind)


def hop(values, bits):
    count = lax.axis_size("dp")
    return lax.ppermute(values, "dp", [(i, i ^ bits) for i in range(count)])


def next_line(values):
    count = lax.axis_size("dp")
    return lax.ppermute(values, "dp", [(i, (i + GROUP) % count) for i in range(count)])


def swap(values):
    return lax.ppermute(values, "tensor", [(0, 1), (1, 0)])


def pick(values, index, axis=0):
    return lax.dynamic_index_in_dim(values, index, axis, keepdims=False)


def in_order(mine, theirs, core):
    return jnp.where(
        core == 0, jnp.concatenate([mine, theirs]), jnp.concatenate([theirs, mine])
    )


def ring(block, lines):
    blocks = [block]
    for _ in range(lines - 1):
        blocks.append(next_line(blocks[-1]))
    return blocks


def gather_blocks(block, first, lines):
    own = jnp.stack(ring(block, lines))
    second = 3 - first
    near = hop(own, first)
    found = {0: own, first: near, second: hop(own, second), 3: hop(near, second)}
    return [found[k] for k in range(GROUP)]


def assemble(parts, targets):
    inner, height, width = parts[0].shape
    total = len(parts) * inner
    if height % 32:
        flat = jnp.concatenate(parts)
        source = jnp.zeros((total,), jnp.int32).at[targets].set(jnp.arange(total, dtype=jnp.int32))
        return flat[source].reshape(total * height, width)

    def body(target_ref, *refs):
        out_ref, sems = refs[-2], refs[-1]
        copies = []
        for i in range(len(parts)):
            for j in range(inner):
                number = i * inner + j
                start = pl.multiple_of(target_ref[number] * height, height)
                copies.append(
                    pltpu.make_async_copy(
                        refs[i].at[j], out_ref.at[pl.ds(start, height)], sems.at[number]
                    )
                )
        for copy in copies:
            copy.start()
        for copy in copies:
            copy.wait()

    return pl.pallas_call(
        body,
        out_shape=jax.ShapeDtypeStruct((total * height, width), parts[0].dtype),
        in_specs=[pl.BlockSpec(memory_space=pltpu.SMEM)]
        + [pl.BlockSpec(memory_space=pl.ANY)] * len(parts),
        out_specs=pl.BlockSpec(memory_space=pltpu.VMEM),
        scratch_shapes=[pltpu.SemaphoreType.DMA((total,))],
        compiler_params=pltpu.CompilerParams(vmem_limit_bytes=VMEM),
        cost_estimate=pl.CostEstimate(
            flops=0, bytes_accessed=4 * total * height * width, transcendentals=0
        ),
        name="assemble",
    )(targets, *parts)


def line_sum(blocks, line, lines):
    if lines == 1:
        return blocks[0].astype(F32)
    held = pick(blocks, lax.rem(line - 1 + lines, lines))
    for step in range(1, lines):
        came = next_line(held.astype(BF))
        mine = pick(blocks, lax.rem(line - 1 - step + 2 * lines, lines))
        held = came.astype(F32) + mine.astype(F32)
    return held


def block_sum(values, first, place, line, lines):
    rows, width = values.shape
    parts = values.reshape(lines, 2, 2, rows // (lines * GROUP), width)
    axes = {1: (2, lax.rem(place, 2)), 2: (1, place // 2)}
    axis, own = axes[first]
    sent = hop(pick(parts, 1 - own, axis).astype(BF), first)
    parts = pick(parts, own, axis).astype(F32) + sent.astype(F32)
    second = 3 - first
    own = axes[second][1]
    sent = hop(pick(parts, 1 - own, 1).astype(BF), second)
    parts = pick(parts, own, 1) + sent.astype(F32)
    return line_sum(parts, line, lines)


def share_group(piece):
    half = piece.shape[0] // 2
    along_x, along_y = hop(piece, 1), hop(piece, 2)
    across = jnp.concatenate([hop(along_x[:half], 2), hop(along_y[half:], 1)])
    return [piece, along_x, along_y, across]


def sum_group(parts):
    half = parts[3].shape[0] // 2
    over_x = hop(parts[3][:half].astype(BF), 1).astype(F32)
    over_y = hop(parts[3][half:].astype(BF), 2).astype(F32)
    to_y = jnp.concatenate([parts[2][:half] + over_x, parts[2][half:]])
    to_x = jnp.concatenate([parts[1][:half], parts[1][half:] + over_y])
    return (
        parts[0] + hop(to_x.astype(BF), 1).astype(F32) + hop(to_y.astype(BF), 2).astype(F32)
    )


def total_sum(values):
    values = values + swap(values)
    bits = 1
    while bits < lax.axis_size("dp"):
        values = values + hop(values, bits)
        bits *= 2
    return values


def sigmoid(values):
    return 1.0 / (1.0 + jnp.exp(-values))


def split_two(values):
    high = values.astype(BF)
    return high, (values - high.astype(F32)).astype(BF)


def spread_heads(values, spread):
    high, low = split_two(values)
    packed = high.astype(F32) + pltpu.roll(low.astype(F32), LANES // 2, 1)
    return nn(packed.astype(BF), spread)


def gather_heads(values, spread, heads_on):
    high, low = split_two(values)
    return jnp.where(heads_on, nt(high, spread) + nt(low, spread), 0.0)


def conv_rows(ext, kern, low, high, offset):
    summed = kern[4:5, low:high]
    for j in range(4):
        summed = summed + kern[j : j + 1, low:high] * ext[offset + j : offset + j + BL, low:high]
    return summed


def step_terms(raw, head_par, heads_on):
    shifted = raw + head_par[0:1]
    soft = jnp.maximum(shifted, 0.0) + jnp.log1p(jnp.exp(-jnp.abs(shifted)))
    step = jnp.where(heads_on, soft, 0.0)
    return shifted, step, -step * head_par[1:2]


def front_body(gate_ref, zi_ref, kern_ref, head_ref, spread_ref, y_ref, sq_ref, state_ref, ext, state):
    width = gate_ref.shape[1]
    first = pl.program_id(0) == 0

    @pl.when(first)
    def _():
        ext[0:8, :] = jnp.zeros((8, ext.shape[1]), F32)
        state[...] = jnp.zeros(state.shape, F32)

    @pl.when(jnp.logical_not(first))
    def _():
        ext[0:8, :] = ext[BL : BL + 8, :]

    ext[8 : BL + 8, :] = zi_ref[...]
    rows = lax.broadcasted_iota(jnp.int32, (BL, LANES), 0)
    cols = lax.broadcasted_iota(jnp.int32, (BL, LANES), 1)
    causal = cols <= rows
    heads_on = cols < width // P_SIZE
    spread = spread_ref[...]
    state_ref[0] = state[...]
    pre = conv_rows(ext, kern_ref, 0, width, 5)
    x = pre * sigmoid(pre)
    pre = conv_rows(ext, kern_ref, width + LANES, ext.shape[1], 5)
    maps = pre * sigmoid(pre)
    b, c = maps[:, :NS], maps[:, NS:]
    shifted, step, decay = step_terms(zi_ref[:, width : width + LANES], head_ref, heads_on)
    cum = jnp.dot(causal.astype(F32), decay, precision=highest, preferred_element_type=F32)
    cum_t = cum.T
    last = cum[BL - 1 : BL]
    scores = nt(c.astype(BF), b.astype(BF))
    u = x * spread_heads(step, spread)
    from_start = spread_heads(jnp.where(heads_on, jnp.exp(cum), 0.0), spread)
    to_end = spread_heads(jnp.where(heads_on, jnp.exp(last - cum), 0.0), spread)
    u_low = u.astype(BF)
    left = cols < P_SIZE
    within = []
    for pair in range(width // LANES):
        mats = []
        for head in (2 * pair, 2 * pair + 1):
            gap = cum[:, head : head + 1] - cum_t[head : head + 1, :]
            mats.append((jnp.where(causal, jnp.exp(gap), 0.0) * scores).astype(BF))
        cut = u_low[:, pair * LANES : (pair + 1) * LANES]
        zero = jnp.zeros_like(cut)
        stacked = jnp.concatenate([jnp.where(left, cut, zero), jnp.where(left, zero, cut)], axis=0)
        within.append(nn(jnp.concatenate(mats, axis=1), stacked))
    before = state[...]
    across = nn(c.astype(BF), before.astype(BF)) * from_start
    y = jnp.concatenate(within, axis=1) + across + kern_ref[5:6, :width] * x
    y_ref[...] = y
    gate = gate_ref[...]
    gated = y * gate * sigmoid(gate)
    sq_ref[...] = jnp.broadcast_to(jnp.sum(gated * gated, axis=1, keepdims=True), sq_ref.shape)
    grown = nn(b.T.astype(BF), (u * to_end).astype(BF))
    state[...] = before * from_start[BL - 1 : BL] + grown


def front_scan(gate, zi, kern, head_par, spread):
    length, width = gate.shape
    steps = length // BL
    return pl.pallas_call(
        front_body,
        grid=(steps,),
        out_shape=(
            jax.ShapeDtypeStruct((length, width), F32),
            jax.ShapeDtypeStruct((length, LANES), F32),
            jax.ShapeDtypeStruct((steps, NS, width), F32),
        ),
        in_specs=[
            pl.BlockSpec((BL, width), lambda i: (i, 0)),
            pl.BlockSpec((BL, zi.shape[1]), lambda i: (i, 0)),
            pl.BlockSpec(kern.shape, lambda i: (0, 0)),
            pl.BlockSpec(head_par.shape, lambda i: (0, 0)),
            pl.BlockSpec(spread.shape, lambda i: (0, 0)),
        ],
        out_specs=(
            pl.BlockSpec((BL, width), lambda i: (i, 0)),
            pl.BlockSpec((BL, LANES), lambda i: (i, 0)),
            pl.BlockSpec((1, NS, width), lambda i: (i, 0, 0)),
        ),
        scratch_shapes=[pltpu.VMEM((BL + 8, zi.shape[1]), F32), pltpu.VMEM((NS, width), F32)],
        compiler_params=pltpu.CompilerParams(
            dimension_semantics=("arbitrary",), vmem_limit_bytes=VMEM
        ),
        cost_estimate=pl.CostEstimate(
            flops=40_000_000_000, bytes_accessed=30_000_000, transcendentals=8_000_000
        ),
        name="front_scan",
    )(gate, zi, kern, head_par, spread)


def back_body(
    dsc_ref, y_ref, gate_ref, zi_ref, prev_ref, state_ref, rows_ref, kern_ref, head_ref, spread_ref,
    dz_ref, di_ref, par_ref, hg_ref, ext, ext_d, d_state,
):
    width = gate_ref.shape[1]
    wide = zi_ref.shape[1]
    number = pl.program_id(0)
    steps = pl.num_programs(0)

    @pl.when(number == 0)
    def _():
        ext_d[BL : BL + 8, :] = jnp.zeros((8, wide), F32)
        d_state[...] = jnp.zeros(d_state.shape, F32)
        par_ref[...] = jnp.zeros(par_ref.shape, F32)
        hg_ref[...] = jnp.zeros(hg_ref.shape, F32)

    @pl.when(number > 0)
    def _():
        ext_d[BL : BL + 8, :] = ext_d[0:8, :]

    ext[0:8, :] = jnp.where(number == steps - 1, 0.0, prev_ref[...])
    ext[8 : BL + 8, :] = zi_ref[...]
    rows = lax.broadcasted_iota(jnp.int32, (BL, LANES), 0)
    cols = lax.broadcasted_iota(jnp.int32, (BL, LANES), 1)
    upper = rows <= cols
    strict = rows < cols
    heads_on = cols < width // P_SIZE
    left = cols < P_SIZE
    spread = spread_ref[...]
    pre_x = conv_rows(ext, kern_ref, 0, width, 5)
    sig_x = sigmoid(pre_x)
    x = pre_x * sig_x
    pre_m = conv_rows(ext, kern_ref, width + LANES, wide, 5)
    sig_m = sigmoid(pre_m)
    maps = pre_m * sig_m
    b, c = maps[:, :NS], maps[:, NS:]
    b_low, c_low = b.astype(BF), c.astype(BF)
    shifted, step, decay = step_terms(zi_ref[:, width : width + LANES], head_ref, heads_on)
    cum = jnp.dot(
        (cols <= rows).astype(F32), decay, precision=highest, preferred_element_type=F32
    )
    cum_t = cum.T
    last = cum[BL - 1 : BL]
    step_wide = spread_heads(step, spread)
    from_start = spread_heads(jnp.where(heads_on, jnp.exp(cum), 0.0), spread)
    to_end = spread_heads(jnp.where(heads_on, jnp.exp(last - cum), 0.0), spread)
    whole = from_start[BL - 1 : BL]
    y, gate, d_scaled = y_ref[...], gate_ref[...], dsc_ref[...]
    sig_g = sigmoid(gate)
    silu_g = gate * sig_g
    gated = y * silu_g
    scale, pull = rows_ref[:, 0:1], rows_ref[:, 1:2]
    scaled_in = d_scaled * scale
    d_gated = scaled_in * kern_ref[6:7, :width] - gated * pull
    par_ref[6:7, :width] += jnp.sum(scaled_in * gated, axis=0, keepdims=True)
    d_y = d_gated * silu_g
    dz_ref[...] = (d_gated * y * sig_g * (1.0 + gate * (1.0 - sig_g))).astype(BF)
    par_ref[5:6, :width] += jnp.sum(d_y * x, axis=0, keepdims=True)
    u = x * step_wide
    u_low, dy_low = u.astype(BF), d_y.astype(BF)
    scores_t = nt(b_low, c_low)
    d_scores_t = jnp.zeros((BL, BL), F32)
    du_parts = []
    gap_rows = jnp.zeros((BL, LANES), F32)
    gap_cols = []
    for pair in range(width // LANES):
        lanes = slice(pair * LANES, (pair + 1) * LANES)
        cut_u, cut_d = u_low[:, lanes], dy_low[:, lanes]
        zero = jnp.zeros_like(cut_u)
        stack_u = jnp.concatenate([jnp.where(left, cut_u, zero), jnp.where(left, zero, cut_u)], axis=0)
        stack_d = jnp.concatenate([jnp.where(left, cut_d, zero), jnp.where(left, zero, cut_d)], axis=0)
        d_weights = nt(stack_u, cut_d)
        mats = []
        for place, head in enumerate((2 * pair, 2 * pair + 1)):
            gap = cum_t[head : head + 1, :] - cum[:, head : head + 1]
            decays = jnp.where(upper, jnp.exp(gap), 0.0)
            weight = decays * scores_t
            mats.append(weight.astype(BF))
            d_weight = d_weights[place * BL : (place + 1) * BL]
            d_scores_t = d_scores_t + decays * d_weight
            moved = jnp.where(strict, weight * d_weight, 0.0)
            gap_rows = jnp.where(cols == head, jnp.sum(moved, axis=1, keepdims=True), gap_rows)
            gap_cols.append(jnp.sum(moved, axis=0, keepdims=True))
        du_parts.append(nn(jnp.concatenate(mats, axis=1), stack_d))
    gap_cols.append(jnp.zeros((LANES - width // P_SIZE, BL), F32))
    gap_cols = jnp.concatenate(gap_cols, axis=0).T
    before, d_after = state_ref[0], d_state[...]
    before_low, d_after_low = before.astype(BF), d_after.astype(BF)
    dy_start = d_y * from_start
    dy_start_low = dy_start.astype(BF)
    reach = gather_heads(dy_start * nn(c_low, before_low), spread, heads_on)
    u_end = u * to_end
    d_from_state = nn(b_low, d_after_low)
    kept = gather_heads(u_end * d_from_state, spread, heads_on)
    carried = jnp.sum(before * d_after, axis=0, keepdims=True) * whole
    carried = gather_heads(jnp.broadcast_to(carried, (8, width)), spread, heads_on[:8])[0:1]
    d_c = nt(dy_start_low, before_low) + nn(d_scores_t.T.astype(BF), b_low)
    d_b = nt(u_end.astype(BF), d_after_low) + nn(d_scores_t.astype(BF), c_low)
    d_state[...] = d_after * whole + nn(c.T.astype(BF), dy_start_low)
    d_u = jnp.concatenate(du_parts, axis=1) + to_end * d_from_state
    d_decay = (
        jnp.dot(
            upper.astype(F32), reach + gap_cols - gap_rows, precision=highest,
            preferred_element_type=F32,
        )
        + jnp.dot(
            (cols < rows).astype(F32), kept, precision=highest, preferred_element_type=F32
        )
        + carried
    )
    d_step = gather_heads(x * d_u, spread, heads_on)
    rate = head_ref[1:2]
    d_raw = jnp.where(heads_on, (d_step - rate * d_decay) * sigmoid(shifted), 0.0)
    hg_ref[0:1, :] += jnp.sum(d_raw, axis=0, keepdims=True)
    hg_ref[1:2, :] += jnp.sum(jnp.where(heads_on, d_decay * decay, 0.0), axis=0, keepdims=True)
    d_x = step_wide * d_u + kern_ref[5:6, :width] * d_y
    ext_d[0:BL, :width] = d_x * sig_x * (1.0 + pre_x * (1.0 - sig_x))
    ext_d[0:BL, width : width + LANES] = jnp.zeros((BL, LANES), F32)
    ext_d[0:BL, width + LANES :] = (
        jnp.concatenate([d_b, d_c], axis=1) * sig_m * (1.0 + pre_m * (1.0 - sig_m))
    )
    for low, high in ((0, width), (width + LANES, wide)):
        d_act = ext_d[0:BL, low:high]
        d_in = jnp.zeros((BL, high - low), F32)
        for j in range(4):
            d_in = d_in + kern_ref[j : j + 1, low:high] * ext_d[3 - j : 3 - j + BL, low:high]
            par_ref[j : j + 1, low:high] += jnp.sum(
                d_act * ext[5 + j : 5 + j + BL, low:high], axis=0, keepdims=True
            )
        par_ref[4:5, low:high] += jnp.sum(d_act, axis=0, keepdims=True)
        di_ref[:, low:high] = d_in.astype(BF)
    di_ref[:, width : width + LANES] = d_raw.astype(BF)


def back_scan(d_scaled, y, gate, zi, states, row_par, kern, head_par, spread):
    length, width = gate.shape
    wide = zi.shape[1]
    steps = length // BL
    per = BL // 8

    def back(i):
        return (steps - 1 - i, 0)

    def fixed(i):
        return (0, 0)

    return pl.pallas_call(
        back_body,
        grid=(steps,),
        out_shape=(
            jax.ShapeDtypeStruct((length, width), BF),
            jax.ShapeDtypeStruct((length, wide), BF),
            jax.ShapeDtypeStruct((8, wide), F32),
            jax.ShapeDtypeStruct((8, LANES), F32),
        ),
        in_specs=[
            pl.BlockSpec((BL, width), back),
            pl.BlockSpec((BL, width), back),
            pl.BlockSpec((BL, width), back),
            pl.BlockSpec((BL, wide), back),
            pl.BlockSpec((8, wide), lambda i: (jnp.maximum((steps - 1 - i) * per - 1, 0), 0)),
            pl.BlockSpec((1, NS, width), lambda i: (steps - 1 - i, 0, 0)),
            pl.BlockSpec((BL, LANES), back),
            pl.BlockSpec(kern.shape, fixed),
            pl.BlockSpec(head_par.shape, fixed),
            pl.BlockSpec(spread.shape, fixed),
        ],
        out_specs=(
            pl.BlockSpec((BL, width), back),
            pl.BlockSpec((BL, wide), back),
            pl.BlockSpec((8, wide), fixed),
            pl.BlockSpec((8, LANES), fixed),
        ),
        scratch_shapes=[
            pltpu.VMEM((BL + 8, wide), F32),
            pltpu.VMEM((BL + 8, wide), F32),
            pltpu.VMEM((NS, width), F32),
        ],
        compiler_params=pltpu.CompilerParams(
            dimension_semantics=("arbitrary",), vmem_limit_bytes=VMEM
        ),
        cost_estimate=pl.CostEstimate(
            flops=80_000_000_000, bytes_accessed=60_000_000, transcendentals=12_000_000
        ),
        name="back_scan",
    )(d_scaled, y, gate, zi, zi, states, row_par, kern, head_par, spread)


def expert_body(hidden, units, x_ref, ym_ref, router_ref, w_ref, acts_ref, out_ref, dx_ref, dl_ref, w, sem):
    width = x_ref.shape[1]
    tile = x_ref.shape[0]

    @pl.when(pl.program_id(0) == 0)
    def _():
        copy = pltpu.make_async_copy(w_ref, w, sem)
        copy.start()
        copy.wait()

    lane = lax.broadcasted_iota(jnp.int32, (tile, LANES), 1)
    routed = ym_ref[:, width:].astype(F32) > 0.5
    logits = nn(x_ref[...], router_ref[...])
    top = jnp.max(jnp.where(routed, logits, -1e30), axis=1, keepdims=True)
    powers = jnp.where(routed, jnp.exp(jnp.where(routed, logits - top, 0.0)), 0.0)
    gates = powers / jnp.sum(powers, axis=1, keepdims=True)

    def hidden_part(start, size, gate):
        def columns(which):
            return pl.ds(pl.multiple_of(which * hidden + start, LANES), size)

        x = x_ref[...]
        pre = nn(x, w[:, columns(0)])
        up = nn(x, w[:, columns(1)])
        d_act = nn(ym_ref[:, :width], w[:, columns(2)])
        sig = sigmoid(pre)
        silu = pre * sig
        act = (silu * up).astype(BF).astype(F32)
        d_gate = jnp.sum(act * d_act, axis=1, keepdims=True)
        d_hid = d_act if gate is None else d_act * gate
        acts_ref[:, columns(0)] = (d_hid * up * sig * (1.0 + pre * (1.0 - sig))).astype(BF)
        acts_ref[:, columns(1)] = (d_hid * silu).astype(BF)
        acts_ref[:, columns(2)] = (act if gate is None else act * gate).astype(BF)
        return d_gate

    def one_expert(e, d_gates):
        gate = jnp.sum(jnp.where(lane == e, gates, 0.0), axis=1, keepdims=True)
        return jnp.where(lane == e, hidden_part(e * units, units, gate), d_gates)

    own = EXPERTS // GROUP
    d_gates = lax.fori_loop(0, own, one_expert, jnp.zeros((tile, LANES), F32))
    hidden_part(own * units, hidden - own * units, None)
    mean = jnp.sum(gates * d_gates, axis=1, keepdims=True)
    d_logits = (gates * (d_gates - mean)).astype(BF)
    dl_ref[...] = d_logits
    step = 256

    def one_slice(number, carry):
        rows = pl.ds(pl.multiple_of(number * step, step), step)
        out_ref[:, rows] = nt(acts_ref[:, 2 * hidden :], w[rows, 2 * hidden :]).astype(BF)
        dx_ref[:, rows] = (
            nt(acts_ref[:, : 2 * hidden], w[rows, : 2 * hidden]) + nt(d_logits, router_ref[rows, :])
        ).astype(BF)
        return carry

    lax.fori_loop(0, width // step, one_slice, 0)


def expert_rows(x, ym, router, w, units):
    rows, width = x.shape
    hidden = w.shape[1] // 3
    tile = min(512, rows)
    return pl.pallas_call(
        functools.partial(expert_body, hidden, units),
        grid=(rows // tile,),
        out_shape=(
            jax.ShapeDtypeStruct((rows, 3 * hidden), BF),
            jax.ShapeDtypeStruct((rows, width), BF),
            jax.ShapeDtypeStruct((rows, width), BF),
            jax.ShapeDtypeStruct((rows, LANES), BF),
        ),
        in_specs=[
            pl.BlockSpec((tile, width), lambda i: (i, 0)),
            pl.BlockSpec((tile, ym.shape[1]), lambda i: (i, 0)),
            pl.BlockSpec(router.shape, lambda i: (0, 0)),
            pl.BlockSpec(memory_space=pl.ANY),
        ],
        out_specs=(
            pl.BlockSpec((tile, 3 * hidden), lambda i: (i, 0)),
            pl.BlockSpec((tile, width), lambda i: (i, 0)),
            pl.BlockSpec((tile, width), lambda i: (i, 0)),
            pl.BlockSpec((tile, LANES), lambda i: (i, 0)),
        ),
        scratch_shapes=[pltpu.VMEM(w.shape, BF), pltpu.SemaphoreType.DMA],
        compiler_params=pltpu.CompilerParams(
            dimension_semantics=("arbitrary",), vmem_limit_bytes=VMEM
        ),
        cost_estimate=pl.CostEstimate(
            flops=4 * rows * width * 3 * hidden, bytes_accessed=30_000_000, transcendentals=0
        ),
        name="expert_rows",
    )(x, ym, router, w)


def norm_rows(values):
    return lax.rsqrt(jnp.mean(values * values, axis=-1, keepdims=True) + EPS)


def norm_back(d_rows, values, scale, gain):
    grad_gain = jnp.sum(d_rows * values * scale, axis=0)
    pulled = d_rows * gain
    mean = jnp.mean(values * pulled, axis=-1, keepdims=True)
    return scale * pulled - values * (scale * scale * scale) * mean, grad_gain


def shards(
    tokens, routes, gain_in, w_zx, w_dt, w_bc, conv_w, conv_b, dt_bias, a_log, d_skip, norm_gain,
    w_out, gain_mid, router, shared_gu, shared_down, expert_gu, expert_down, grad_out,
):
    core = lax.axis_index("tensor")
    me = lax.axis_index("dp")
    lines = lax.axis_size("dp") // GROUP
    line, place = me // GROUP, lax.rem(me, GROUP)
    piece, width_d = tokens.shape
    local = w_zx.shape[2]
    heads = w_dt.shape[1]
    units = expert_gu.shape[3]
    own = EXPERTS // GROUP
    inner_all = norm_gain.shape[0]
    height = w_zx.shape[0]

    lines_back = lax.rem(line - jnp.arange(lines, dtype=jnp.int32) + lines, lines)
    members = place ^ jnp.arange(GROUP, dtype=jnp.int32)
    mixer_order = (members[:, None] + GROUP * lines_back[None, :]).reshape(-1)
    expert_order = (members[None, :] + GROUP * lines_back[:, None]).reshape(-1)

    tokens_full = in_order(tokens, swap(tokens), core).astype(F32)
    joint = jnp.concatenate([w_bc, router], axis=1)
    joint = in_order(joint, swap(joint), core)
    bc_cols, router_cols = joint[:, : 2 * NS], joint[:, 2 * NS :]
    pad = jnp.zeros((height, LANES - heads - EXPERTS), BF)
    inner_block = jnp.concatenate([w_zx[:, 1], w_dt, router_cols, pad, bc_cols], axis=1)
    gate_w = assemble(gather_blocks(w_zx[:, 0], 1, lines), mixer_order)
    inner_w = assemble(gather_blocks(inner_block, 2, lines), mixer_order)
    out_w = assemble(gather_blocks(w_out.T, 1, lines), mixer_order)

    by_member = expert_gu.reshape(GROUP, own, height, 2, units).transpose(0, 2, 3, 1, 4)
    by_member = by_member.reshape(GROUP, height, 2, own * units)
    down_member = expert_down.reshape(GROUP, own, units, height).transpose(0, 3, 1, 2)
    down_member = down_member.reshape(GROUP, height, own * units)
    shared_units = shared_gu.shape[2] // GROUP
    sgu_member = shared_gu.reshape(height, 2, GROUP, shared_units).transpose(2, 0, 1, 3)
    sdown_member = shared_down.reshape(GROUP, shared_units, height).transpose(0, 2, 1)
    hidden = own * units + shared_units
    packed = jnp.concatenate(
        [
            by_member[:, :, 0], sgu_member[:, :, 0], by_member[:, :, 1], sgu_member[:, :, 1],
            down_member, sdown_member,
        ],
        axis=2,
    )
    group_block = jnp.stack(
        [pick(packed, members[0])] + [hop(pick(packed, members[k]), k) for k in range(1, GROUP)]
    )
    expert_w = assemble(ring(group_block, lines), expert_order)

    own_routes = lax.dynamic_slice_in_dim(routes, core * piece, piece, 0)
    lane = jnp.arange(LANES, dtype=jnp.int32)
    mask = jnp.any(own_routes[:, :, None] == lane[None, None, :], axis=1).astype(BF)
    back_rows = [
        jnp.concatenate([mine, swap(mine)])
        for mine in share_group(jnp.concatenate([grad_out, mask], axis=1))
    ]

    def own_mask(rows):
        marks = rows[:, width_d : width_d + EXPERTS]
        return jnp.pad(
            jnp.roll(marks, -own * place, axis=1), ((0, 0), (0, LANES - EXPERTS))
        )

    back_rows = [
        jnp.concatenate([rows[:, :width_d], own_mask(rows)], axis=1) for rows in back_rows
    ]

    cut = functools.partial(lax.dynamic_slice_in_dim, start_index=core * local, slice_size=local)
    cut_heads = functools.partial(lax.dynamic_slice_in_dim, start_index=core * heads, slice_size=heads)
    between = jnp.zeros((5, LANES), F32)
    conv_all = jnp.concatenate([conv_w, conv_b[None]])
    kern = jnp.concatenate([cut(conv_all, axis=1), between, conv_all[:, inner_all:]], axis=1)
    tail = jnp.zeros((1, kern.shape[1] - local), F32)
    skip_wide = jnp.repeat(cut_heads(d_skip, axis=0), P_SIZE)[None]
    gain_loc = cut(norm_gain, axis=0)
    kern = jnp.concatenate(
        [
            kern,
            jnp.concatenate([skip_wide, tail], axis=1),
            jnp.concatenate([gain_loc[None], tail], axis=1),
            jnp.zeros((1, kern.shape[1]), F32),
        ]
    )
    head_par = jnp.pad(
        jnp.stack([cut_heads(dt_bias, axis=0), jnp.exp(cut_heads(a_log, axis=0))]),
        ((0, 6), (0, LANES - heads)),
    )
    head_of = jnp.arange(local, dtype=jnp.int32) // P_SIZE
    half_lane = lax.rem(lane, LANES // 2)
    spread = (half_lane[:, None] == head_of[None, :]).astype(BF)

    normed = (tokens_full * norm_rows(tokens_full) * gain_in).astype(BF)
    gate = nn(normed, gate_w)
    zi = nn(normed, inner_w)
    y, squares, states = front_scan(gate, zi, kern, head_par, spread)
    squares = squares[:, 0:1]
    squares = squares + swap(squares)
    row_scale = lax.rsqrt(squares / inner_all + EPS)
    scaled = (y * gate * sigmoid(gate) * row_scale * gain_loc).astype(BF)
    mixed = nt(scaled, out_w)
    mixed_mine = lax.dynamic_slice_in_dim(mixed, core * piece, piece, 0)
    mixed_mine = mixed_mine + swap(lax.dynamic_slice_in_dim(mixed, (1 - core) * piece, piece, 0))
    resid_in = tokens.astype(F32)
    resid = resid_in + mixed_mine
    mid_scale = norm_rows(resid)
    mid = (resid * mid_scale * gain_mid).astype(BF)

    mid_rows = [jnp.concatenate([mine, swap(mine)]) for mine in share_group(mid)]
    router_all = inner_w[:, local + heads : local + heads + EXPERTS]
    router_own = jnp.pad(
        jnp.roll(router_all, -own * place, axis=1), ((0, 0), (0, LANES - EXPERTS))
    )
    done = [expert_rows(x, ym, router_own, expert_w, units) for x, ym in zip(mid_rows, back_rows)]

    def both_cores(rows):
        return rows[:piece].astype(F32) + swap(rows[piece:]).astype(F32)

    d_mid = sum_group([both_cores(item[2]) for item in done])
    branch = sum_group([both_cores(item[1]) for item in done])
    output = (resid + branch).astype(BF)
    x_all = jnp.concatenate(mid_rows)
    dy_all = jnp.concatenate([rows[:, :width_d] for rows in back_rows])
    acts = jnp.concatenate([item[0] for item in done])
    d_logits = jnp.concatenate([item[3] for item in done])
    grad_gu = tn(x_all, acts[:, : 2 * hidden], BF)
    grad_down = tn(dy_all, acts[:, 2 * hidden :], BF)
    grad_router = tn(x_all, d_logits)[:, :EXPERTS]
    grad_router = jnp.roll(grad_router, own * place, axis=1)

    def to_members(grad):
        summed = line_sum(grad.reshape(lines, GROUP, height, -1), line, lines)
        low = summed.astype(BF)
        came = [pick(summed, members[0])] + [
            hop(pick(low, members[k]), k).astype(F32) for k in range(1, GROUP)
        ]
        stacked = jnp.stack(came)
        return jnp.stack([pick(stacked, place ^ k) for k in range(GROUP)])

    g_gu = to_members(grad_gu).reshape(GROUP, height, 2, hidden)
    g_down = to_members(grad_down)
    routed = own * units
    g_egu = g_gu[..., :routed].reshape(GROUP, height, 2, own, units).transpose(0, 3, 1, 2, 4)
    g_egu = g_egu.reshape(EXPERTS, height, 2, units)
    g_edown = g_down[..., :routed].reshape(GROUP, height, own, units).transpose(0, 2, 3, 1)
    g_edown = g_edown.reshape(EXPERTS, units, height)
    g_sgu = g_gu[..., routed:].transpose(1, 2, 0, 3).reshape(height, 2, -1)
    g_sdown = g_down[..., routed:].transpose(0, 2, 1).reshape(-1, height)

    d_extra, grad_gain_mid = norm_back(d_mid, resid, mid_scale, gain_mid)
    d_resid = grad_out.astype(F32) + d_extra
    d_mix = d_resid.astype(BF)
    pulls = jnp.sum(d_mix.astype(F32) * (resid - resid_in), axis=1, keepdims=True)
    pulls = in_order(pulls, swap(pulls), core)
    d_mix = in_order(d_mix, swap(d_mix), core)
    row_par = jnp.concatenate(
        [row_scale, row_scale * row_scale * pulls / inner_all], axis=1
    )
    row_par = jnp.pad(row_par, ((0, 0), (0, LANES - 2)))
    d_scaled = nn(d_mix, out_w)
    grad_out_w = tn(d_mix, scaled, BF)
    dz, di, par_grads, head_grads = back_scan(
        d_scaled, y, gate, zi, states, row_par, kern, head_par, spread
    )
    d_normed = nt(dz, gate_w) + nt(di, inner_w)
    d_mine = lax.dynamic_slice_in_dim(d_normed, core * piece, piece, 0)
    d_mine = d_mine + swap(lax.dynamic_slice_in_dim(d_normed, (1 - core) * piece, piece, 0))
    d_extra, grad_gain_in = norm_back(d_mine, resid_in, norm_rows(resid_in), gain_in)
    grad_tokens = (d_resid + d_extra).astype(BF)

    grad_inner = tn(normed, di)
    grad_inner = lax.dynamic_update_slice(grad_inner, grad_router, (0, local + heads))
    g_out = block_sum(grad_out_w, 1, place, line, lines).T
    g_gate = block_sum(tn(normed, dz, BF), 2, place, line, lines)
    g_inner = block_sum(grad_inner.astype(BF), 1, place, line, lines)
    g_zx = jnp.stack([g_gate, g_inner[:, :local]], axis=1)
    g_dt = g_inner[:, local : local + heads]
    g_joint = jnp.concatenate(
        [g_inner[:, local + heads : local + heads + EXPERTS], g_inner[:, local + LANES :]], axis=1
    )
    joint_rows = height // 2
    g_joint = lax.dynamic_slice_in_dim(g_joint, core * joint_rows, joint_rows, 0) + swap(
        lax.dynamic_slice_in_dim(g_joint, (1 - core) * joint_rows, joint_rows, 0)
    )

    def widen(part, full):
        start = (0,) * (part.ndim - 1) + (core * part.shape[-1],)
        return lax.dynamic_update_slice(jnp.zeros(part.shape[:-1] + (full,), F32), part, start)

    conv_full = jnp.concatenate(
        [widen(par_grads[:5, :local], inner_all), par_grads[:5, local + LANES :]], axis=1
    )
    skip_loc = par_grads[5, :local].reshape(heads, P_SIZE).sum(axis=1)
    small = [
        grad_gain_in,
        grad_gain_mid,
        conv_full.reshape(-1),
        widen(head_grads[0, :heads], H),
        widen(head_grads[1, :heads], H),
        widen(skip_loc, H),
        widen(par_grads[6, :local], inner_all),
    ]
    flat = jnp.concatenate(small)
    count = -(-flat.shape[0] // 1024) * 1024
    flat = total_sum(jnp.pad(flat, (0, count - flat.shape[0])).reshape(-1, LANES)).reshape(-1)
    sums = []
    start = 0
    for item in small:
        sums.append(flat[start : start + item.shape[0]])
        start += item.shape[0]
    conv_sums = sums[2].reshape(5, -1)
    return (
        output, grad_tokens, sums[0], g_zx, g_dt, g_joint[:, EXPERTS:], conv_sums[:4],
        conv_sums[4], sums[3], sums[4], sums[5], sums[6], g_out, sums[1], g_joint[:, :EXPERTS],
        g_sgu, g_sdown, g_egu, g_edown,
    )


def solution(mesh):
    both = P(("dp", "tensor"), None)
    rows = P("dp", None, "tensor")
    cols = P("tensor", "dp")
    return jax.shard_map(
        shards,
        mesh=mesh,
        in_specs=(
            both, P("dp", None), P(), rows, P("dp", "tensor"), both, P(), P(), P(), P(), P(), P(),
            cols, P(), both, rows, cols, P(None, "dp", None, "tensor"), P(None, "tensor", "dp"),
            both,
        ),
        out_specs=(
            both, both, P(), rows, P("dp", "tensor"), both, P(), P(), P(), P(), P(), P(),
            cols, P(), both, rows, cols, P(None, "dp", None, "tensor"), P(None, "tensor", "dp"),
        ),
        check_vma=False,
    )
```

```python
import functools

import jax
import jax.numpy as jnp
from jax import lax
from jax.experimental import pallas as pl
from jax.experimental.pallas import tpu as pltpu
from jax.sharding import PartitionSpec as P

F32 = jnp.float32
BF = jnp.bfloat16
EPS = 1e-05
H = 48
P_SIZE = 64
NS = 128
EXPERTS = 16
BL = 128
GROUP = 4
LANES = 128
VMEM = 60 * 1024 * 1024
SMALL = pl.CostEstimate(flops=1000, bytes_accessed=1000, transcendentals=0)
highest = lax.Precision.HIGHEST


def nn(left, right):
    return lax.dot_general(left, right, (((1,), (0,)), ((), ())), preferred_element_type=F32)


def nt(left, right):
    return lax.dot_general(left, right, (((1,), (1,)), ((), ())), preferred_element_type=F32)


def tn(left, right, kind=F32):
    return lax.dot_general(left, right, (((0,), (0,)), ((), ())), preferred_element_type=kind)


def hop(values, bits):
    count = lax.axis_size("dp")
    return lax.ppermute(values, "dp", [(i, i ^ bits) for i in range(count)])


def next_line(values):
    count = lax.axis_size("dp")
    return lax.ppermute(values, "dp", [(i, (i + GROUP) % count) for i in range(count)])


def swap(values):
    return lax.ppermute(values, "tensor", [(0, 1), (1, 0)])


def pick(values, index, axis=0):
    return lax.dynamic_index_in_dim(values, index, axis, keepdims=False)


def in_order(mine, theirs, core):
    return jnp.where(
        core == 0, jnp.concatenate([mine, theirs]), jnp.concatenate([theirs, mine])
    )


def tie(values, *others):
    flat, tree = jax.tree.flatten(values)
    held = lax.optimization_barrier((flat, others))
    return jax.tree.unflatten(tree, held[0])


class Order:
    def __init__(self):
        self.marks = self.last = ()

    def __call__(self, values):
        return tie(values, *self.marks)

    def set(self, *marks):
        self.marks, self.last = marks + self.last, marks

    def take(self, *values):
        values = self(values)
        self.set(*values)
        return values if len(values) > 1 else values[0]


def ring_on(blocks, order, low, high, lines):
    for _ in range(low, min(high, lines)):
        blocks.append(order(next_line(blocks[-1])))


def pieces_of(parts, targets, cut):
    inner, height, width = parts[0].shape
    starts = [0] * len(parts)
    if cut:
        starts[-1] = cut
    if height % 32 == 0:
        return parts, starts, targets
    if cut:
        parts = parts[:3] + [jnp.concatenate(parts[3:], axis=-1)]
    flat = jnp.concatenate(parts)
    total = flat.shape[0]
    source = jnp.zeros((total,), jnp.int32)
    source = source.at[targets[:total]].set(jnp.arange(total, dtype=jnp.int32))
    whole = flat[source].reshape(1, total * height, width)
    return [whole], [0], jnp.zeros((1,), jnp.int32)


def load_pieces(target_ref, part_refs, starts, held, base, sems):
    copies = []
    for ref, start in zip(part_refs, starts):
        inner, height, width = ref.shape
        for j in range(inner):
            row = pl.multiple_of(target_ref[len(copies)] * height, height)
            copies.append(
                pltpu.make_async_copy(
                    ref.at[j],
                    held.at[pl.ds(row, height), base + start : base + start + width],
                    sems.at[len(copies)],
                )
            )
    return copies


def run_copies(copies):
    for copy in copies:
        copy.start()
    for copy in copies:
        copy.wait()


def norm_rows(values):
    return lax.rsqrt(jnp.mean(values * values, axis=-1, keepdims=True) + EPS)


def sigmoid(values):
    return 1.0 / (1.0 + jnp.exp(-values))


def split_two(values):
    high = values.astype(BF)
    return high, (values - high.astype(F32)).astype(BF)


def spread_heads(values, spread):
    high, low = split_two(values)
    packed = high.astype(F32) + pltpu.roll(low.astype(F32), LANES // 2, 1)
    return nn(packed.astype(BF), spread)


def gather_heads(values, spread, heads_on):
    high, low = split_two(values)
    return jnp.where(heads_on, nt(high, spread) + nt(low, spread), 0.0)


def conv_rows(ext, kern, low, high, offset):
    summed = kern[4:5, low:high]
    for j in range(4):
        summed = summed + kern[j : j + 1, low:high] * ext[offset + j : offset + j + BL, low:high]
    return summed


def step_terms(raw, head_par, heads_on):
    shifted = raw + head_par[0:1]
    soft = jnp.maximum(shifted, 0.0) + jnp.log1p(jnp.exp(-jnp.abs(shifted)))
    step = jnp.where(heads_on, soft, 0.0)
    return shifted, step, -step * head_par[1:2]


def front_body(zi_ref, kern_ref, head_ref, spread_ref, y_ref, state_ref, ext, state):
    width = y_ref.shape[1]
    first = pl.program_id(0) == 0

    @pl.when(first)
    def _():
        ext[0:8, :] = jnp.zeros((8, ext.shape[1]), F32)
        state[...] = jnp.zeros(state.shape, F32)

    @pl.when(jnp.logical_not(first))
    def _():
        ext[0:8, :] = ext[BL : BL + 8, :]

    ext[8 : BL + 8, :] = zi_ref[...]
    rows = lax.broadcasted_iota(jnp.int32, (BL, LANES), 0)
    cols = lax.broadcasted_iota(jnp.int32, (BL, LANES), 1)
    causal = cols <= rows
    heads_on = cols < width // P_SIZE
    spread = spread_ref[...]
    state_ref[0] = state[...]
    pre = conv_rows(ext, kern_ref, 0, width, 5)
    x = pre * sigmoid(pre)
    pre = conv_rows(ext, kern_ref, width + LANES, ext.shape[1], 5)
    maps = pre * sigmoid(pre)
    b, c = maps[:, :NS], maps[:, NS:]
    shifted, step, decay = step_terms(zi_ref[:, width : width + LANES], head_ref, heads_on)
    cum = jnp.dot(causal.astype(F32), decay, precision=highest, preferred_element_type=F32)
    cum_t = cum.T
    last = cum[BL - 1 : BL]
    scores = nt(c.astype(BF), b.astype(BF))
    u = x * spread_heads(step, spread)
    from_start = spread_heads(jnp.where(heads_on, jnp.exp(cum), 0.0), spread)
    to_end = spread_heads(jnp.where(heads_on, jnp.exp(last - cum), 0.0), spread)
    u_low = u.astype(BF)
    left = cols < P_SIZE
    within = []
    for pair in range(width // LANES):
        mats = []
        for head in (2 * pair, 2 * pair + 1):
            gap = cum[:, head : head + 1] - cum_t[head : head + 1, :]
            mats.append((jnp.where(causal, jnp.exp(gap), 0.0) * scores).astype(BF))
        cut = u_low[:, pair * LANES : (pair + 1) * LANES]
        zero = jnp.zeros_like(cut)
        stacked = jnp.concatenate([jnp.where(left, cut, zero), jnp.where(left, zero, cut)], axis=0)
        within.append(nn(jnp.concatenate(mats, axis=1), stacked))
    before = state[...]
    across = nn(c.astype(BF), before.astype(BF)) * from_start
    y_ref[...] = jnp.concatenate(within, axis=1) + across + kern_ref[5:6, :width] * x
    grown = nn(b.T.astype(BF), (u * to_end).astype(BF))
    state[...] = before * from_start[BL - 1 : BL] + grown


def front_scan(zi, kern, head_par, spread):
    length, width = zi.shape[0], spread.shape[1]
    steps = length // BL
    return pl.pallas_call(
        front_body,
        grid=(steps,),
        out_shape=(
            jax.ShapeDtypeStruct((length, width), F32),
            jax.ShapeDtypeStruct((steps, NS, width), F32),
        ),
        in_specs=[
            pl.BlockSpec((BL, zi.shape[1]), lambda i: (i, 0)),
            pl.BlockSpec(kern.shape, lambda i: (0, 0)),
            pl.BlockSpec(head_par.shape, lambda i: (0, 0)),
            pl.BlockSpec(spread.shape, lambda i: (0, 0)),
        ],
        out_specs=(
            pl.BlockSpec((BL, width), lambda i: (i, 0)),
            pl.BlockSpec((1, NS, width), lambda i: (i, 0, 0)),
        ),
        scratch_shapes=[pltpu.VMEM((BL + 8, zi.shape[1]), F32), pltpu.VMEM((NS, width), F32)],
        compiler_params=pltpu.CompilerParams(
            dimension_semantics=("arbitrary",), vmem_limit_bytes=VMEM
        ),
        cost_estimate=SMALL,
        name="front_scan",
    )(zi, kern, head_par, spread)


def back_body(
    dy_ref, zi_ref, prev_ref, state_ref, kern_ref, head_ref, spread_ref,
    dia_ref, dib_ref, par_ref, hg_ref, ext, ext_d, d_state,
):
    width = dy_ref.shape[1]
    wide = zi_ref.shape[1]
    cut_at = dia_ref.shape[1]
    number = pl.program_id(0)
    steps = pl.num_programs(0)

    @pl.when(number == 0)
    def _():
        ext_d[BL : BL + 8, :] = jnp.zeros((8, wide), F32)
        d_state[...] = jnp.zeros(d_state.shape, F32)
        par_ref[...] = jnp.zeros(par_ref.shape, F32)
        hg_ref[...] = jnp.zeros(hg_ref.shape, F32)

    @pl.when(number > 0)
    def _():
        ext_d[BL : BL + 8, :] = ext_d[0:8, :]

    ext[0:8, :] = jnp.where(number == steps - 1, 0.0, prev_ref[...])
    ext[8 : BL + 8, :] = zi_ref[...]
    rows = lax.broadcasted_iota(jnp.int32, (BL, LANES), 0)
    cols = lax.broadcasted_iota(jnp.int32, (BL, LANES), 1)
    upper = rows <= cols
    strict = rows < cols
    heads_on = cols < width // P_SIZE
    left = cols < P_SIZE
    spread = spread_ref[...]
    pre_x = conv_rows(ext, kern_ref, 0, width, 5)
    sig_x = sigmoid(pre_x)
    x = pre_x * sig_x
    pre_m = conv_rows(ext, kern_ref, width + LANES, wide, 5)
    sig_m = sigmoid(pre_m)
    maps = pre_m * sig_m
    b, c = maps[:, :NS], maps[:, NS:]
    b_low, c_low = b.astype(BF), c.astype(BF)
    shifted, step, decay = step_terms(zi_ref[:, width : width + LANES], head_ref, heads_on)
    cum = jnp.dot(
        (cols <= rows).astype(F32), decay, precision=highest, preferred_element_type=F32
    )
    cum_t = cum.T
    last = cum[BL - 1 : BL]
    step_wide = spread_heads(step, spread)
    from_start = spread_heads(jnp.where(heads_on, jnp.exp(cum), 0.0), spread)
    to_end = spread_heads(jnp.where(heads_on, jnp.exp(last - cum), 0.0), spread)
    whole = from_start[BL - 1 : BL]
    d_y = dy_ref[...]
    par_ref[5:6, :width] += jnp.sum(d_y * x, axis=0, keepdims=True)
    u = x * step_wide
    u_low, dy_low = u.astype(BF), d_y.astype(BF)
    scores_t = nt(b_low, c_low)
    d_scores_t = jnp.zeros((BL, BL), F32)
    du_parts = []
    gap_rows = jnp.zeros((BL, LANES), F32)
    gap_cols = []
    for pair in range(width // LANES):
        lanes = slice(pair * LANES, (pair + 1) * LANES)
        cut_u, cut_d = u_low[:, lanes], dy_low[:, lanes]
        zero = jnp.zeros_like(cut_u)
        stack_u = jnp.concatenate([jnp.where(left, cut_u, zero), jnp.where(left, zero, cut_u)], axis=0)
        stack_d = jnp.concatenate([jnp.where(left, cut_d, zero), jnp.where(left, zero, cut_d)], axis=0)
        d_weights = nt(stack_u, cut_d)
        mats = []
        for place, head in enumerate((2 * pair, 2 * pair + 1)):
            gap = cum_t[head : head + 1, :] - cum[:, head : head + 1]
            decays = jnp.where(upper, jnp.exp(gap), 0.0)
            weight = decays * scores_t
            mats.append(weight.astype(BF))
            d_weight = d_weights[place * BL : (place + 1) * BL]
            d_scores_t = d_scores_t + decays * d_weight
            moved = jnp.where(strict, weight * d_weight, 0.0)
            gap_rows = jnp.where(cols == head, jnp.sum(moved, axis=1, keepdims=True), gap_rows)
            gap_cols.append(jnp.sum(moved, axis=0, keepdims=True))
        du_parts.append(nn(jnp.concatenate(mats, axis=1), stack_d))
    gap_cols.append(jnp.zeros((LANES - width // P_SIZE, BL), F32))
    gap_cols = jnp.concatenate(gap_cols, axis=0).T
    before, d_after = state_ref[0], d_state[...]
    before_low, d_after_low = before.astype(BF), d_after.astype(BF)
    dy_start = d_y * from_start
    dy_start_low = dy_start.astype(BF)
    reach = gather_heads(dy_start * nn(c_low, before_low), spread, heads_on)
    u_end = u * to_end
    d_from_state = nn(b_low, d_after_low)
    kept = gather_heads(u_end * d_from_state, spread, heads_on)
    carried = jnp.sum(before * d_after, axis=0, keepdims=True) * whole
    carried = gather_heads(jnp.broadcast_to(carried, (8, width)), spread, heads_on[:8])[0:1]
    d_c = nt(dy_start_low, before_low) + nn(d_scores_t.T.astype(BF), b_low)
    d_b = nt(u_end.astype(BF), d_after_low) + nn(d_scores_t.astype(BF), c_low)
    d_state[...] = d_after * whole + nn(c.T.astype(BF), dy_start_low)
    d_u = jnp.concatenate(du_parts, axis=1) + to_end * d_from_state
    d_decay = (
        jnp.dot(
            upper.astype(F32), reach + gap_cols - gap_rows, precision=highest,
            preferred_element_type=F32,
        )
        + jnp.dot(
            (cols < rows).astype(F32), kept, precision=highest, preferred_element_type=F32
        )
        + carried
    )
    d_step = gather_heads(x * d_u, spread, heads_on)
    rate = head_ref[1:2]
    d_raw = jnp.where(heads_on, (d_step - rate * d_decay) * sigmoid(shifted), 0.0)
    hg_ref[0:1, :] += jnp.sum(d_raw, axis=0, keepdims=True)
    hg_ref[1:2, :] += jnp.sum(jnp.where(heads_on, d_decay * decay, 0.0), axis=0, keepdims=True)
    d_x = step_wide * d_u + kern_ref[5:6, :width] * d_y
    ext_d[0:BL, :width] = d_x * sig_x * (1.0 + pre_x * (1.0 - sig_x))
    ext_d[0:BL, width : width + LANES] = jnp.zeros((BL, LANES), F32)
    ext_d[0:BL, width + LANES :] = (
        jnp.concatenate([d_b, d_c], axis=1) * sig_m * (1.0 + pre_m * (1.0 - sig_m))
    )
    for low, high in ((0, cut_at), (cut_at, width), (width + LANES, wide)):
        d_act = ext_d[0:BL, low:high]
        d_in = jnp.zeros((BL, high - low), F32)
        for j in range(4):
            d_in = d_in + kern_ref[j : j + 1, low:high] * ext_d[3 - j : 3 - j + BL, low:high]
            par_ref[j : j + 1, low:high] += jnp.sum(
                d_act * ext[5 + j : 5 + j + BL, low:high], axis=0, keepdims=True
            )
        par_ref[4:5, low:high] += jnp.sum(d_act, axis=0, keepdims=True)
        if low < cut_at:
            dia_ref[...] = d_in.astype(BF)
        else:
            dib_ref[:, low - cut_at : high - cut_at] = d_in.astype(BF)
    dib_ref[:, width - cut_at : width - cut_at + LANES] = d_raw.astype(BF)


def back_scan(d_y, zi, states, kern, head_par, spread, cut_at):
    length, width = d_y.shape
    wide = zi.shape[1]
    steps = length // BL
    per = BL // 8

    def back(i):
        return (steps - 1 - i, 0)

    def fixed(i):
        return (0, 0)

    return pl.pallas_call(
        back_body,
        grid=(steps,),
        out_shape=(
            jax.ShapeDtypeStruct((length, cut_at), BF),
            jax.ShapeDtypeStruct((length, wide - cut_at), BF),
            jax.ShapeDtypeStruct((8, wide), F32),
            jax.ShapeDtypeStruct((8, LANES), F32),
        ),
        in_specs=[
            pl.BlockSpec((BL, width), back),
            pl.BlockSpec((BL, wide), back),
            pl.BlockSpec((8, wide), lambda i: (jnp.maximum((steps - 1 - i) * per - 1, 0), 0)),
            pl.BlockSpec((1, NS, width), lambda i: (steps - 1 - i, 0, 0)),
            pl.BlockSpec(kern.shape, fixed),
            pl.BlockSpec(head_par.shape, fixed),
            pl.BlockSpec(spread.shape, fixed),
        ],
        out_specs=(
            pl.BlockSpec((BL, cut_at), back),
            pl.BlockSpec((BL, wide - cut_at), back),
            pl.BlockSpec((8, wide), fixed),
            pl.BlockSpec((8, LANES), fixed),
        ),
        scratch_shapes=[
            pltpu.VMEM((BL + 8, wide), F32),
            pltpu.VMEM((BL + 8, wide), F32),
            pltpu.VMEM((NS, width), F32),
        ],
        compiler_params=pltpu.CompilerParams(
            dimension_semantics=("arbitrary",), vmem_limit_bytes=VMEM
        ),
        cost_estimate=SMALL,
        name="back_scan",
    )(d_y, zi, zi, states, kern, head_par, spread)


def small_call(body, outs, args, name, scalars=0):
    vmem, smem = pl.BlockSpec(memory_space=pltpu.VMEM), pl.BlockSpec(memory_space=pltpu.SMEM)
    return pl.pallas_call(
        body,
        out_shape=tuple(jax.ShapeDtypeStruct(shape, kind) for shape, kind in outs),
        in_specs=[smem] * scalars + [vmem] * (len(args) - scalars),
        out_specs=tuple(vmem for _ in outs),
        compiler_params=pltpu.CompilerParams(vmem_limit_bytes=VMEM),
        cost_estimate=SMALL,
        name=name,
    )(*args)


def stack_columns(blocks, start, width):
    height = blocks[0].shape[0]

    def body(*refs):
        for number, ref in enumerate(refs[:-1]):
            refs[-1][number] = ref[:, start : start + width]

    shape = (len(blocks), height, width)
    return small_call(body, [(shape, blocks[0].dtype)], blocks, "stack_columns")[0]


def stack_pairs(first, second):
    height, low = first[0].shape
    high = second[0].shape[1]

    def body(*refs):
        for number in range(len(first)):
            refs[-1][number, :, :low] = refs[number][...]
            refs[-1][number, :, low:] = refs[len(first) + number][...]

    shape = (len(first), height, low + high)
    return small_call(body, [(shape, first[0].dtype)], [*first, *second], "stack_pairs")[0]


def cut_columns(values, start, width):
    def body(values_ref, out_ref):
        out_ref[...] = values_ref[:, :, start : start + width]

    return small_call(
        body, [(values.shape[:2] + (width,), values.dtype)], [values], "cut_columns"
    )[0]


def cut_rows_of(values, start, rows):
    def body(values_ref, out_ref):
        out_ref[...] = values_ref[start : start + rows]

    return small_call(body, [((rows, values.shape[1]), values.dtype)], [values], "cut_rows")[0]


def pair_rows(pairs, core):
    def body(core_ref, *refs):
        for number in range(len(pairs)):
            mine_ref, other_ref = refs[2 * number : 2 * number + 2]
            out_ref = refs[2 * len(pairs) + number]
            out_ref[core_ref[0]] = mine_ref[...]
            out_ref[1 - core_ref[0]] = other_ref[...]

    outs = [((2,) + mine.shape, mine.dtype) for mine, _ in pairs]
    args = [core] + [item for pair in pairs for item in pair]
    done = small_call(body, outs, args, "pair_rows", 1)
    return [item.reshape(-1, item.shape[2]) for item in done]


def add_blocks(groups, height, count, kind, where, name):
    total = sum(width for width, _, _ in groups)
    flat = [(width, item) for width, items, _ in groups for item in items]
    overs = []
    for _, _, over in groups:
        if over is not None and not any(over[0] is array for array in overs):
            overs.append(over[0])

    if height % 32:
        columns = []
        for width, items, over in groups:
            term = 0.0
            for array, number, spot in items:
                part = array[:, number * width : (number + 1) * width].reshape(-1, height, width)
                picked = [pick(part, spot(i, where)) for i in range(count)]
                term = term + jnp.concatenate(picked).astype(F32)
            if over is not None:
                term = term + over[0][:, over[1] : over[1] + width].astype(F32)
            columns.append(term)
        return jnp.concatenate(columns, axis=1).astype(kind)

    def body(where_ref, *refs):
        item_refs = refs[: len(flat)]
        over_refs = refs[len(flat) : len(flat) + len(overs)]
        out_ref, sems = refs[len(flat) + len(overs)], refs[-1]
        helds = refs[len(flat) + len(overs) + 1 : -1]
        copies = []
        for row, (ref, held, (width, (_, number, spot))) in enumerate(zip(item_refs, helds, flat)):
            for i in range(count):
                start = pl.multiple_of(spot(i, where_ref) * height, height)
                copies.append(
                    pltpu.make_async_copy(
                        ref.at[pl.ds(start, height), number * width : (number + 1) * width],
                        held.at[i * height : (i + 1) * height],
                        sems.at[row, i],
                    )
                )
        run_copies(copies)
        at = start = 0
        for width, items, over in groups:
            term = helds[at][...]
            if len(items) > 1 or over is not None:
                term = term.astype(F32)
            for held in helds[at + 1 : at + len(items)]:
                term = term + held[...].astype(F32)
            if over is not None:
                (number,) = [i for i, array in enumerate(overs) if array is over[0]]
                term = term + over_refs[number][:, over[1] : over[1] + width].astype(F32)
            out_ref[:, start : start + width] = term.astype(kind)
            at += len(items)
            start += width

    vmem, any_ref = pl.BlockSpec(memory_space=pltpu.VMEM), pl.BlockSpec(memory_space=pl.ANY)
    return pl.pallas_call(
        body,
        out_shape=jax.ShapeDtypeStruct((count * height, total), kind),
        in_specs=[pl.BlockSpec(memory_space=pltpu.SMEM)]
        + [any_ref] * len(flat)
        + [vmem] * len(overs),
        out_specs=vmem,
        scratch_shapes=[
            pltpu.VMEM((count * height, width), item[0].dtype) for width, item in flat
        ]
        + [pltpu.SemaphoreType.DMA((len(flat), count))],
        compiler_params=pltpu.CompilerParams(vmem_limit_bytes=VMEM),
        cost_estimate=SMALL,
        name=name,
    )(where, *[item[0] for _, item in flat], *overs)


class Plane:
    def __init__(self, values, bits, where, lines):
        self.values, self.bits, self.where, self.lines = values, bits, where, lines
        self.height = values[0][0].shape[0] // (lines * GROUP)
        self.came = self.came_last = None

    def _spot(self, i, first, second):
        x, y = (first, second) if self.bits == 1 else (second, first)
        return i * GROUP + y * 2 + x

    def _own(self, where, axis):
        return lax.rem(where[0], 2) if axis == 1 else where[0] // 2

    def start(self, order):
        def spot(i, where):
            return self._spot(i // 2, 1 - self._own(where, self.bits), i % 2)

        groups = [
            (width, [(order(array), number, spot)], None) for array, number, width in self.values
        ]
        return add_blocks(groups, self.height, 2 * self.lines, BF, self.where, "plane_start")

    def _groups(self, keep, line_at, last):
        def which(where):
            own = self._own(where, 3 - self.bits)
            return own if keep else 1 - own

        def in_came(i, where):
            return 2 * line_at(i, where) + which(where)

        def in_values(i, where):
            return self._spot(line_at(i, where), self._own(where, self.bits), which(where))

        width = sum(item[2] for item in self.values)
        groups = []
        start = 0
        for array, number, wide in self.values:
            items = [(array, number, in_values), (self.came, start, in_came)]
            if last:
                items.append((self.came_last, start, line_at))
            groups.append((wide, items, None))
            start += 1
        return groups

    def turn(self):
        return add_blocks(
            self._groups(False, lambda i, where: i, False), self.height, self.lines, BF,
            self.where, "plane_turn",
        )

    def groups(self, line_at):
        return self._groups(True, line_at, True)


class LineSums:
    def __init__(self, parts, order, lines, height, where):
        self.parts, self.order, self.lines = parts, order, lines
        self.height, self.where = height, where
        self.steps, self.final, self.names = {}, {}, []
        self.sent = None

    def _step(self, names, overs, kind):
        groups = []
        for name in names:
            back = self.steps[name] + 1

            def line_at(i, spots, back=back):
                return lax.rem(spots[1] - back + 2 * self.lines, self.lines)

            over = overs.get(name)
            start = 0
            for width, items, _ in self.parts[name](line_at):
                groups.append((width, items, None if over is None else (over[0], over[1] + start)))
                start += width
        return add_blocks(groups, self.height, 1, kind, self.where, "line_step")

    def _send(self, names, overs):
        self.names = names
        self.sent = self._step(names, overs, BF) if names else None

    def start(self, *names):
        for name in names:
            self.steps[name] = 0
        self._send(list(names), {})

    def run(self, count, *new):
        for number in range(count):
            joining = list(new) if number + 1 == count else []
            overs = {}
            if self.names:
                came = self.order(next_line(self.sent))
                start = 0
                for name in self.names:
                    overs[name] = (came, start)
                    start += sum(width for width, _, _ in self.parts[name](None))
                    self.steps[name] += 1
                    if self.steps[name] + 1 == self.lines:
                        self.final[name] = self._step([name], overs, F32)
            staying = [name for name in self.names if name not in self.final]
            for name in joining:
                self.steps[name] = 0
            if staying or joining or self.names:
                self._send(staying + joining, overs)


def member_pieces(gu, down, where, height):
    wide, narrow = gu.shape[1], down.shape[1]

    def spot_of(k, spots):
        bit_0 = lax.rem(spots[0] + k % 2, 2)
        return bit_0 + 2 * lax.rem(spots[0] // 2 + k // 2, 2)

    if height % 32:
        return [
            jnp.concatenate(
                [pick(item.reshape(GROUP, height, -1), spot_of(k, where)) for item in (gu, down)],
                axis=1,
            ).astype(BF)
            for k in range(GROUP)
        ]

    def body(where_ref, gu_ref, down_ref, *out_refs):
        for k, out_ref in enumerate(out_refs):
            rows = pl.ds(pl.multiple_of(spot_of(k, where_ref) * height, height), height)
            out_ref[:, :wide] = gu_ref[rows, :].astype(BF)
            out_ref[:, wide:] = down_ref[rows, :].astype(BF)

    return list(
        small_call(
            body, [((height, wide + narrow), BF)] * GROUP, [where, gu, down], "member_pieces", 1
        )
    )


def gathered_call(body, tile, row_args, fixed_args, matrices, shift, outs, name):
    depth = sum(part.shape[0] * part.shape[1] for part in matrices[0][0][:4])
    widths = [parts[0].shape[2] for parts, _, _ in matrices]
    counts = [len(parts) for parts, _, _ in matrices]
    targets = matrices[0][2]
    rows = row_args[0].shape[0]
    steps = rows // tile
    row_count, fixed_count = len(row_args), len(fixed_args)

    def whole(*refs):
        order_ref = refs[0]
        at = 2
        row_refs = refs[at : at + row_count]
        at += row_count
        fixed_refs = refs[at : at + fixed_count]
        at += fixed_count
        part_refs = refs[at : at + sum(counts)]
        at += sum(counts)
        out_refs = refs[at : at + len(outs)]
        held, sems = refs[-2], refs[-1]

        @pl.when(pl.program_id(0) == 0)
        def _():
            copies = []
            used = base = 0
            for number, (count, width) in enumerate(zip(counts, widths)):
                copies += load_pieces(
                    order_ref, part_refs[used : used + count], matrices[number][1], held, base,
                    sems.at[number],
                )
                used += count
                base += width
            run_copies(copies)

        body(row_refs, fixed_refs, held, out_refs, pl.program_id(0))

    def rows_map(i, order_ref, shift_ref):
        return (lax.rem(i + shift_ref[0], steps), 0)

    def fixed_map(i, order_ref, shift_ref):
        return (0, 0)

    def low_map(i, order_ref, shift_ref):
        return (jnp.minimum(i, steps // 2 - 1), 0)

    def high_map(i, order_ref, shift_ref):
        return (jnp.maximum(i - steps // 2, 0), 0)

    maps = {"rows": rows_map, "low": low_map, "high": high_map}

    def out_spec(shape, kind):
        if kind == "one":
            return pl.BlockSpec(shape, fixed_map)
        return pl.BlockSpec((tile, shape[1]), maps[kind])

    return pl.pallas_call(
        whole,
        grid_spec=pltpu.PrefetchScalarGridSpec(
            num_scalar_prefetch=2,
            grid=(steps,),
            in_specs=[pl.BlockSpec((tile, arg.shape[1]), rows_map) for arg in row_args]
            + [pl.BlockSpec(arg.shape, fixed_map) for arg in fixed_args]
            + [pl.BlockSpec(memory_space=pl.ANY)] * sum(counts),
            out_specs=tuple(out_spec(shape, kind) for shape, _, kind in outs),
            scratch_shapes=[
                pltpu.VMEM((depth, sum(widths)), BF),
                pltpu.SemaphoreType.DMA((len(matrices), targets.shape[0])),
            ],
        ),
        out_shape=tuple(jax.ShapeDtypeStruct(shape, kind) for shape, kind, _ in outs),
        compiler_params=pltpu.CompilerParams(
            dimension_semantics=("arbitrary",), vmem_limit_bytes=VMEM
        ),
        cost_estimate=SMALL,
        name=name,
    )(targets, shift, *row_args, *fixed_args, *[part for parts, _, _ in matrices for part in parts])


NO_SHIFT = (0,)


def inner_product(normed, matrix, small):
    rows, depth = normed.shape
    width = matrix[0][0].shape[2]

    def body(row_refs, fixed_refs, held, out_refs, number):
        out_refs[0][...] = nn(row_refs[0][...], held[...])

        @pl.when(number == 0)
        def _():
            out_refs[1][...] = held[:, small : small + LANES]

    return gathered_call(
        body, 256, [normed], [], [matrix], jnp.array(NO_SHIFT, jnp.int32),
        [((rows, width), F32, "rows"), ((depth, LANES), BF, "one")], "inner_product",
    )


def gate_product(normed, y, matrix):
    rows, width = y.shape

    def body(row_refs, fixed_refs, held, out_refs, number):
        gate = nn(row_refs[0][...], held[...])
        out_refs[0][...] = gate
        gated = row_refs[1][...] * gate * sigmoid(gate)
        total = jnp.sum(gated * gated, axis=1, keepdims=True)
        out_refs[1][...] = jnp.broadcast_to(total, out_refs[1].shape)

    return gathered_call(
        body, 256, [normed, y], [], [matrix], jnp.array(NO_SHIFT, jnp.int32),
        [((rows, width), F32, "rows"), ((rows, LANES), F32, "rows")], "gate_product",
    )


def row_scales(squares_ref, others_ref, width):
    return lax.rsqrt((squares_ref[:, 0:1] + others_ref[:, 0:1]) / width + EPS)


def split_rows(value, number, steps, low_ref, high_ref):
    @pl.when(number < steps // 2)
    def _():
        low_ref[...] = value

    @pl.when(number >= steps // 2)
    def _():
        high_ref[...] = value


def mixed_product(y, gate, squares, others, kern, matrix, shift, inner_all):
    rows, width = y.shape
    depth = sum(part.shape[0] * part.shape[1] for part in matrix[0][:4])
    tile = 256

    def body(row_refs, fixed_refs, held, out_refs, number):
        gate_now = row_refs[1][...]
        scale = row_scales(row_refs[2], row_refs[3], inner_all)
        scaled = row_refs[0][...] * gate_now * sigmoid(gate_now) * scale
        scaled = (scaled * fixed_refs[0][6:7, :width]).astype(BF)
        out_refs[0][...] = scaled
        mixed = nt(scaled, held[...])
        split_rows(mixed, number, rows // tile, out_refs[1], out_refs[2])

    return gathered_call(
        body, tile, [y, gate, squares, others], [kern], [matrix], shift,
        [
            ((rows, width), BF, "rows"), ((rows // 2, depth), F32, "low"),
            ((rows // 2, depth), F32, "high"),
        ],
        "mixed_product",
    )


def gate_back(d_mix, y, gate, squares, others, pulls, kern, matrix, cut_at, inner_all):
    rows, width = y.shape

    def body(row_refs, fixed_refs, held, out_refs, number):
        d_scaled = nn(row_refs[0][...], held[...])
        y_now, gate_now = row_refs[1][...], row_refs[2][...]
        scale = row_scales(row_refs[3], row_refs[4], inner_all)
        pull = scale * scale * row_refs[5][:, 0:1] / inner_all
        sig = sigmoid(gate_now)
        silu = gate_now * sig
        gated = y_now * silu
        scaled_in = d_scaled * scale
        d_gated = scaled_in * fixed_refs[0][6:7, :width] - gated * pull

        @pl.when(number == 0)
        def _():
            out_refs[3][...] = jnp.zeros(out_refs[3].shape, F32)

        out_refs[3][0:1, :] += jnp.sum(scaled_in * gated, axis=0, keepdims=True)
        out_refs[0][...] = d_gated * silu
        d_gate = (d_gated * y_now * sig * (1.0 + gate_now * (1.0 - sig))).astype(BF)
        out_refs[1][...] = d_gate[:, :cut_at]
        out_refs[2][...] = d_gate[:, cut_at:]

    return gathered_call(
        body, 256, [d_mix, y, gate, squares, others, pulls], [kern], [matrix],
        jnp.array(NO_SHIFT, jnp.int32),
        [
            ((rows, width), F32, "rows"), ((rows, cut_at), BF, "rows"),
            ((rows, width - cut_at), BF, "rows"), ((8, width), F32, "one"),
        ],
        "gate_back",
    )


def normed_back(grads, matrices, shift):
    rows = grads[0].shape[0]
    widths = [grad.shape[1] for grad in grads]
    depth = sum(part.shape[0] * part.shape[1] for part in matrices[0][0][:4])
    tile = 256

    def body(row_refs, fixed_refs, held, out_refs, number):
        total = None
        start = 0
        for ref, width in zip(row_refs, widths):
            term = nt(ref[...], held[:, start : start + width])
            total = term if total is None else total + term
            start += width
        split_rows(total, number, rows // tile, out_refs[0], out_refs[1])

    return gathered_call(
        body, tile, grads, [], matrices, shift,
        [((rows // 2, depth), F32, "low"), ((rows // 2, depth), F32, "high")], "normed_back",
    )


def rows_call(body, tile, row_args, fixed_args, outs, name):
    arrays = [arg if isinstance(arg, tuple) else (arg, None) for arg in row_args]
    rows = arrays[0][0].shape[-2]

    def spec(array, number):
        if number is None:
            return pl.BlockSpec((tile, array.shape[1]), lambda i: (i, 0))
        return pl.BlockSpec((None, tile, array.shape[2]), lambda i: (number, i, 0))

    return pl.pallas_call(
        body,
        grid=(rows // tile,),
        out_shape=tuple(jax.ShapeDtypeStruct(shape, kind) for shape, kind, _ in outs),
        in_specs=[spec(*item) for item in arrays]
        + [pl.BlockSpec(arg.shape, lambda i: (0, 0)) for arg in fixed_args],
        out_specs=tuple(
            pl.BlockSpec(shape, lambda i: (0, 0))
            if one
            else pl.BlockSpec((tile, shape[1]), lambda i: (i, 0))
            for shape, _, one in outs
        ),
        compiler_params=pltpu.CompilerParams(
            dimension_semantics=("arbitrary",), vmem_limit_bytes=VMEM
        ),
        cost_estimate=SMALL,
        name=name,
    )(*[array for array, _ in arrays], *fixed_args)


def columns_call(body, row_args, outs, name):
    arrays = [arg if isinstance(arg, tuple) else (arg, None) for arg in row_args]
    width = arrays[0][0].shape[-1]
    tile = width // 2

    def spec(array, number):
        if number is None:
            return pl.BlockSpec((array.shape[0], tile), lambda i: (0, i))
        return pl.BlockSpec((None, array.shape[1], tile), lambda i: (number, 0, i))

    return pl.pallas_call(
        body,
        grid=(width // tile,),
        out_shape=tuple(jax.ShapeDtypeStruct(shape, BF) for shape in outs),
        in_specs=[spec(*item) for item in arrays],
        out_specs=tuple(pl.BlockSpec((shape[0], tile), lambda i: (0, i)) for shape in outs),
        compiler_params=pltpu.CompilerParams(
            dimension_semantics=("arbitrary",), vmem_limit_bytes=VMEM
        ),
        cost_estimate=SMALL,
        name=name,
    )(*[array for array, _ in arrays])


def normed_rows(tokens, others, gain, core):
    rows, width = tokens.shape
    tile = 128

    def body(core_ref, mine_ref, other_ref, gain_ref, out_ref):
        for ref, spot in ((mine_ref, core_ref[0]), (other_ref, 1 - core_ref[0])):
            values = ref[...].astype(F32)
            out_ref[spot] = (values * norm_rows(values) * gain_ref[...]).astype(BF)

    by_rows = pl.BlockSpec((tile, width), lambda i: (i, 0))
    return pl.pallas_call(
        body,
        grid=(rows // tile,),
        out_shape=jax.ShapeDtypeStruct((2, rows, width), BF),
        in_specs=[
            pl.BlockSpec(memory_space=pltpu.SMEM), by_rows, by_rows,
            pl.BlockSpec((1, width), lambda i: (0, 0)),
        ],
        out_specs=pl.BlockSpec((2, tile, width), lambda i: (0, i, 0)),
        compiler_params=pltpu.CompilerParams(
            dimension_semantics=("arbitrary",), vmem_limit_bytes=VMEM
        ),
        cost_estimate=SMALL,
        name="normed_rows",
    )(core, tokens, others, gain).reshape(2 * rows, width)


def marked_rows(grad_out, routes, first_lane):
    rows, width = grad_out.shape

    def body(grad_ref, routes_ref, out_ref):
        out_ref[:, :width] = grad_ref[...]
        lane = lax.broadcasted_iota(jnp.int32, (grad_ref.shape[0], LANES), 1)
        marks = jnp.zeros(lane.shape, F32)
        for number in range(routes_ref.shape[1]):
            marks = jnp.where(lane == routes_ref[:, number : number + 1] + first_lane, 1.0, marks)
        out_ref[:, width:] = marks.astype(BF)

    return rows_call(
        body, 256, [grad_out, routes], [], [((rows, width + LANES), BF, False)], "marked_rows"
    )[0]


def mid_rows_of(mixed, others, tokens, gain):
    rows, width = tokens.shape

    def body(mixed_ref, other_ref, tokens_ref, gain_ref, resid_ref, mid_ref):
        resid = tokens_ref[...].astype(F32) + mixed_ref[...] + other_ref[...]
        resid_ref[...] = resid
        mid_ref[...] = (resid * norm_rows(resid) * gain_ref[...]).astype(BF)

    return rows_call(
        body, 256, [mixed, others, tokens], [gain],
        [((rows, width), F32, False), ((rows, width), BF, False)], "mid_rows",
    )


def across_sum(mine, came, number):
    _, rows, width = mine.shape
    cut = rows // 2

    def body(mine_ref, came_ref, low_ref, high_ref):
        total = (mine_ref[...].astype(F32) + came_ref[...].astype(F32)).astype(BF)
        low_ref[...] = total[:cut]
        high_ref[...] = total[cut:]

    return columns_call(
        body, [(mine, number), (came, number)], [(cut, width)] * 2, "across_sum"
    )


def side_sums(mine, came, over_x, over_y):
    _, rows, width = mine.shape
    cut = rows // 2

    def body(mine_x, came_x, mine_y, came_y, over_x_ref, over_y_ref, x_ref, y_ref):
        to_x = mine_x[...].astype(F32) + came_x[...].astype(F32)
        x_ref[:cut] = to_x[:cut].astype(BF)
        x_ref[cut:] = (to_x[cut:] + over_y_ref[...].astype(F32)).astype(BF)
        to_y = mine_y[...].astype(F32) + came_y[...].astype(F32)
        y_ref[:cut] = (to_y[:cut] + over_x_ref[...].astype(F32)).astype(BF)
        y_ref[cut:] = to_y[cut:].astype(BF)

    return columns_call(
        body, [(mine, 0), (came, 0), (mine, 1), (came, 1), over_x, over_y],
        [(rows, width)] * 2, "side_sums",
    )


def own_sum(mine_ref, came_ref, x_ref, y_ref):
    return (
        mine_ref[...].astype(F32) + came_ref[...].astype(F32)
        + x_ref[...].astype(F32) + y_ref[...].astype(F32)
    )


def norm_back(d_rows, values, gain, grad_ref):
    scale = norm_rows(values)

    @pl.when(pl.program_id(0) == 0)
    def _():
        grad_ref[...] = jnp.zeros(grad_ref.shape, F32)

    grad_ref[0:1, :] += jnp.sum(d_rows * values * scale, axis=0, keepdims=True)
    pulled = d_rows * gain
    mean = jnp.mean(values * pulled, axis=-1, keepdims=True)
    return scale * pulled - values * (scale * scale * scale) * mean


def resid_back(mine, came, from_x, from_y, resid, tokens, grad_out, gain):
    rows, width = tokens.shape

    def body(
        mine_ref, came_ref, x_ref, y_ref, resid_ref, tokens_ref, grad_ref, gain_ref,
        d_resid_ref, d_mix_ref, pulls_ref, gain_grad_ref,
    ):
        resid_now = resid_ref[...]
        d_mid = own_sum(mine_ref, came_ref, x_ref, y_ref)
        d_extra = norm_back(d_mid, resid_now, gain_ref[...], gain_grad_ref)
        d_resid = grad_ref[...].astype(F32) + d_extra
        d_resid_ref[...] = d_resid
        d_mix = d_resid.astype(BF)
        d_mix_ref[...] = d_mix
        mixed = resid_now - tokens_ref[...].astype(F32)
        pull = jnp.sum(d_mix.astype(F32) * mixed, axis=1, keepdims=True)
        pulls_ref[...] = jnp.broadcast_to(pull, pulls_ref.shape)

    return rows_call(
        body, 256, [(mine, 0), (came, 0), from_x, from_y, resid, tokens, grad_out], [gain],
        [
            ((rows, width), F32, False), ((rows, width), BF, False),
            ((rows, LANES), F32, False), ((8, width), F32, True),
        ],
        "resid_back",
    )


def output_rows(mine, came, from_x, from_y, resid):
    def body(mine_ref, came_ref, x_ref, y_ref, resid_ref, out_ref):
        out_ref[...] = (resid_ref[...] + own_sum(mine_ref, came_ref, x_ref, y_ref)).astype(BF)

    return rows_call(
        body, 256, [(mine, 0), (came, 0), from_x, from_y, resid], [], [(resid.shape, BF, False)],
        "output_rows",
    )[0]


def tokens_back(mine, came, tokens, d_resid, gain):
    rows, width = tokens.shape

    def body(mine_ref, came_ref, tokens_ref, d_resid_ref, gain_ref, out_ref, gain_grad_ref):
        d_rows = mine_ref[...] + came_ref[...]
        d_extra = norm_back(d_rows, tokens_ref[...].astype(F32), gain_ref[...], gain_grad_ref)
        out_ref[...] = (d_resid_ref[...] + d_extra).astype(BF)

    return rows_call(
        body, 256, [mine, came, tokens, d_resid], [gain],
        [((rows, width), BF, False), ((8, width), F32, True)], "tokens_back",
    )


def pack_small(par_grads, head_grads, gain_grads, mid_gains, in_gains, spread, core, local, heads):
    width_d = in_gains.shape[1]
    both = 2 * local
    rest = par_grads.shape[1] - local - LANES

    def body(core_ref, par_ref, head_ref, gain_ref, mid_ref, in_ref, spread_ref, out_ref):
        out_ref[...] = jnp.zeros(out_ref.shape, F32)
        spot = pl.ds(pl.multiple_of(core_ref[0] * local, LANES), local)
        out_ref[0:5, spot] = par_ref[0:5, :local]
        out_ref[0:5, both:] = par_ref[0:5, local + LANES :]
        out_ref[5:6, spot] = gain_ref[0:1, :]
        out_ref[6:7, :width_d] = in_ref[0:1, :]
        out_ref[6:7, width_d : 2 * width_d] = mid_ref[0:1, :]
        lane = lax.broadcasted_iota(jnp.int32, (8, LANES), 1)
        skip = gather_heads(par_ref[:, :local], spread_ref[...], lane < heads)
        for number, row in enumerate((head_ref[0:1], head_ref[1:2], skip[5:6])):
            start = pl.multiple_of((2 * number + core_ref[0]) * LANES, LANES)
            out_ref[7:8, pl.ds(start, LANES)] = row

    return small_call(
        body, [((8, both + rest), F32)],
        [core, par_grads, head_grads, gain_grads, mid_gains, in_gains, spread], "pack_small", 1,
    )[0]


def unpack_experts(came, place, units, shared_units):
    height, width = came[0].shape
    hidden = width // 3
    own = EXPERTS // GROUP

    def body(place_ref, *refs):
        came_refs, (gu_ref, down_ref, sgu_ref, sdown_ref) = refs[:GROUP], refs[GROUP:]
        for k in range(GROUP):
            bit_0 = lax.rem(place_ref[0] + k % 2, 2)
            bit_1 = lax.rem(place_ref[0] // 2 + k // 2, 2)
            member = bit_0 + 2 * bit_1
            for e in range(own):
                expert = member * own + e
                for j in range(2):
                    start = j * hidden + e * units
                    gu_ref[expert, :, j, :] = came_refs[k][:, start : start + units].astype(F32)
                start = 2 * hidden + e * units
                down_ref[expert] = came_refs[k][:, start : start + units].astype(F32).T
            spot = pl.ds(pl.multiple_of(member * shared_units, shared_units), shared_units)
            for j in range(2):
                start = j * hidden + own * units
                sgu_ref[:, j, spot] = came_refs[k][:, start : start + shared_units].astype(F32)
            start = 2 * hidden + own * units
            sdown_ref[spot, :] = came_refs[k][:, start : start + shared_units].astype(F32).T

    return pl.pallas_call(
        body,
        out_shape=(
            jax.ShapeDtypeStruct((EXPERTS, height, 2, units), F32),
            jax.ShapeDtypeStruct((EXPERTS, units, height), F32),
            jax.ShapeDtypeStruct((height, 2, GROUP * shared_units), F32),
            jax.ShapeDtypeStruct((GROUP * shared_units, height), F32),
        ),
        in_specs=[pl.BlockSpec(memory_space=pltpu.SMEM)]
        + [pl.BlockSpec(memory_space=pltpu.VMEM)] * GROUP,
        out_specs=(pl.BlockSpec(memory_space=pltpu.VMEM),) * 4,
        compiler_params=pltpu.CompilerParams(vmem_limit_bytes=VMEM),
        cost_estimate=SMALL,
        name="unpack_experts",
    )(place, *came)


def expert_body(plan, *refs):
    own, units, shared, counts, part_count, aliased = plan
    hidden = own * units + shared
    refs = list(refs)

    def take(number):
        out = refs[:number]
        del refs[:number]
        return out

    order_ref, base_ref = take(2)
    x_pieces = [take(number) for number in counts]
    ym_pieces = [take(number) for number in counts]
    count = len(counts)
    (router_ref,) = take(1)
    part_refs = take(part_count)
    take(aliased)
    x_out, dy_out, gu_ref, down_ref = take(4)
    out_mine, out_other, dx_mine, dx_other = take(4)
    w, sems, x_held, ym_held, row_sems = refs
    step = pl.program_id(0)
    width = router_ref.shape[0]

    def fetch(number):
        slot = number % 2
        copies = []
        for which, (parts, target) in enumerate(
            ((x_pieces[number], x_held), (ym_pieces[number], ym_held))
        ):
            start = 0
            for half, ref in enumerate(parts):
                rows = ref.shape[0]
                copies.append(
                    pltpu.make_async_copy(
                        ref, target.at[slot, start : start + rows], row_sems.at[which, slot, half]
                    )
                )
                start += rows
        return copies

    @pl.when(step == 0)
    def _():
        loads = load_pieces(order_ref, part_refs, [0] * part_count, w, 0, sems)
        for copy in fetch(0) + loads:
            copy.start()
        for copy in loads:
            copy.wait()

    for number in range(count):

        @pl.when(step == number)
        def _():
            if number + 1 < count:
                for copy in fetch(number + 1):
                    copy.start()
            for copy in fetch(number):
                copy.wait()

    slot = lax.rem(step, 2)
    x_now, ym_now = x_held.at[slot], ym_held.at[slot]
    x_out[...] = x_now[...]
    dy_out[...] = ym_now[:, :width]
    tile = x_now.shape[0]
    lane = lax.broadcasted_iota(jnp.int32, (tile, LANES), 1)
    routed = ym_now[:, width:].astype(F32) > 0.5
    logits = nn(x_now[...], router_ref[...])
    top = jnp.max(jnp.where(routed, logits, -1e30), axis=1, keepdims=True)
    powers = jnp.where(routed, jnp.exp(jnp.where(routed, logits - top, 0.0)), 0.0)
    gates = powers / jnp.sum(powers, axis=1, keepdims=True)
    d_gates = jnp.zeros((tile, LANES), F32)
    parts = [(e * units, units, e) for e in range(own)] + [(own * units, shared, None)]
    for start, size, expert in parts:
        cols = [slice(k * hidden + start, k * hidden + start + size) for k in range(3)]
        pre = nn(x_now[...], w[:, cols[0]])
        up = nn(x_now[...], w[:, cols[1]])
        d_act = nn(ym_now[:, :width], w[:, cols[2]])
        sig = sigmoid(pre)
        silu = pre * sig
        act = (silu * up).astype(BF).astype(F32)
        if expert is not None:
            here = lane == base_ref[0] + expert
            gate = jnp.sum(jnp.where(here, gates, 0.0), axis=1, keepdims=True)
            d_gate = jnp.sum(act * d_act, axis=1, keepdims=True)
            d_gates = jnp.where(here, d_gate, d_gates)
            d_act = d_act * gate
            act = act * gate
        gu_ref[:, cols[0]] = (d_act * up * sig * (1.0 + pre * (1.0 - sig))).astype(BF)
        gu_ref[:, cols[1]] = (d_act * silu).astype(BF)
        down_ref[:, start : start + size] = act.astype(BF)
    mean = jnp.sum(gates * d_gates, axis=1, keepdims=True)
    d_logits = (gates * (d_gates - mean)).astype(BF)
    gu_ref[:, 2 * hidden :] = d_logits
    cut = 256

    def results(out_ref, dx_ref):
        for number in range(width // cut):
            rows = slice(number * cut, (number + 1) * cut)
            out_ref[0, :, rows] = nt(down_ref[...], w[rows, 2 * hidden :]).astype(BF)
            d_x = nt(gu_ref[:, : 2 * hidden], w[rows, : 2 * hidden])
            dx_ref[0, :, rows] = (d_x + nt(d_logits, router_ref[rows, :])).astype(BF)

    @pl.when(slot == 0)
    def _():
        results(out_mine, dx_mine)

    @pl.when(slot == 1)
    def _():
        results(out_other, dx_other)


def expert_rows(members, x_pieces, ym_pieces, held, base, router, parts, targets, units, shared):
    low, count = members[0], len(members)
    width = router.shape[0]
    x_pieces = [item if isinstance(item, tuple) else (item,) for item in x_pieces]
    ym_pieces = [item if isinstance(item, tuple) else (item,) for item in ym_pieces]
    tile = sum(part.shape[0] for part in x_pieces[0])
    counts = [len(item) for item in x_pieces]
    rows = 2 * GROUP * tile
    steps = 2 * count
    own = EXPERTS // GROUP
    hidden = own * units + shared

    def like(columns):
        spec = pl.BlockSpec((tile, columns), lambda i: (i + 2 * low, 0))
        return jax.ShapeDtypeStruct((rows, columns), BF), spec

    result = (
        jax.ShapeDtypeStruct((count, tile, width), BF),
        pl.BlockSpec((1, tile, width), lambda i: (i // 2, 0, 0)),
    )
    outs = [like(width), like(width), like(2 * hidden + LANES), like(hidden)] + [result] * 4
    any_ref = pl.BlockSpec(memory_space=pl.ANY)
    flat = [part for item in x_pieces + ym_pieces for part in item]
    args = [targets, base, *flat, router, *parts, *held]
    specs = [pl.BlockSpec(memory_space=pltpu.SMEM)] * 2 + [any_ref] * len(flat)
    specs += [pl.BlockSpec(router.shape, lambda i: (0, 0))]
    specs += [any_ref] * (len(parts) + len(held))
    aliases = {len(args) - len(held) + i: i for i in range(len(held))}
    done = pl.pallas_call(
        functools.partial(
            expert_body, (own, units, shared, counts, len(parts), len(held))
        ),
        grid=(steps,),
        out_shape=tuple(shape for shape, _ in outs),
        in_specs=specs,
        out_specs=tuple(spec for _, spec in outs),
        scratch_shapes=[
            pltpu.VMEM((width, 3 * hidden), BF), pltpu.SemaphoreType.DMA((targets.shape[0],)),
            pltpu.VMEM((2, tile, width), BF), pltpu.VMEM((2, tile, width + LANES), BF),
            pltpu.SemaphoreType.DMA((2, 2, 2)),
        ],
        input_output_aliases=aliases,
        compiler_params=pltpu.CompilerParams(
            dimension_semantics=("arbitrary",), vmem_limit_bytes=VMEM
        ),
        cost_estimate=SMALL,
        name="expert_rows",
    )(*args)
    return list(done[:4]), list(done[4:])


def shards(
    tokens, routes, gain_in, w_zx, w_dt, w_bc, conv_w, conv_b, dt_bias, a_log, d_skip, norm_gain,
    w_out, gain_mid, router, shared_gu, shared_down, expert_gu, expert_down, grad_out,
):
    core = lax.axis_index("tensor")
    me = lax.axis_index("dp")
    lines = lax.axis_size("dp") // GROUP
    line, place = me // GROUP, lax.rem(me, GROUP)
    piece, width_d = tokens.shape
    local = w_zx.shape[2]
    heads = w_dt.shape[1]
    units = expert_gu.shape[3]
    own = EXPERTS // GROUP
    inner_all = norm_gain.shape[0]
    height = w_zx.shape[0]
    cut_in, cut_gate = 2 * local // 3, local // 2
    third = (lines - 1 + 2) // 3
    place_now = place.reshape(1)
    where = jnp.stack([place, line]).astype(jnp.int32)
    base = (heads + own * place).reshape(1)
    tiles = 4
    mine_last = (tiles // 2 * (1 - core)).reshape(1).astype(jnp.int32)

    lines_back = lax.rem(line - jnp.arange(lines, dtype=jnp.int32) + lines, lines)
    members = place ^ jnp.arange(GROUP, dtype=jnp.int32)
    pieces = jnp.concatenate([members, members[3:]])
    mixer_targets = (pieces[:, None] + GROUP * lines_back[None, :]).reshape(-1)
    expert_targets = (members[None, :] + GROUP * lines_back[:, None]).reshape(-1)
    order = Order()

    core_now = core.reshape(1)
    gain_in, gain_mid = gain_in[None], gain_mid[None]
    joint = jnp.concatenate([w_bc, router], axis=1)
    joint_came = swap(joint)
    ring_a = [w_zx[:, 1, :cut_in]]
    tokens_other = swap(tokens)
    order.set(ring_a[0], joint)
    joint = in_order(joint, order(joint_came), core)
    bc_cols, router_cols = joint[:, : 2 * NS], joint[:, 2 * NS :]
    pad = jnp.zeros((height, LANES - heads - EXPERTS), BF)
    ring_b = [jnp.concatenate([w_zx[:, 1, cut_in:], w_dt, router_cols, pad, bc_cols], axis=1)]
    order.set(
        ring_b[0], gain_in, gain_mid, where, base, mine_last, place_now, core_now, mixer_targets,
        expert_targets,
    )
    shared_units = shared_gu.shape[2] // GROUP
    hidden = own * units + shared_units
    gu = order(expert_gu).reshape(GROUP, own, height, 2, units).transpose(0, 2, 3, 1, 4)
    gu = gu.reshape(GROUP, height, 2, own * units)
    order.set(gu)
    ring_on(ring_a, order, 1, 1 + third, lines)
    ring_on(ring_b, order, 1, 1 + third, lines)
    order.set(ring_a[-1], ring_b[-1])
    down = order(expert_down).reshape(GROUP, own, units, height).transpose(0, 3, 1, 2)
    down = down.reshape(GROUP, height, own * units)
    sgu = order(shared_gu).reshape(height, 2, GROUP, shared_units).transpose(2, 0, 1, 3)
    sdown = order(shared_down).reshape(GROUP, shared_units, height).transpose(0, 2, 1)
    order.set(down, sgu, sdown)
    ring_on(ring_a, order, 1 + third, 1 + 2 * third, lines)
    ring_on(ring_b, order, 1 + third, 1 + 2 * third, lines)
    order.set(ring_a[-1], ring_b[-1])
    gu, sgu, down, sdown = order((gu, sgu, down, sdown))
    packed = jnp.concatenate([gu[:, :, 0], sgu[:, :, 0], gu[:, :, 1], sgu[:, :, 1], down, sdown], axis=2)
    to_send = [pick(packed, members[k]) for k in range(GROUP)]
    order.set(*to_send)
    came = to_send[:1] + [hop(to_send[k], k) for k in range(1, GROUP)]
    lane = jnp.arange(LANES, dtype=jnp.int32)
    cut = functools.partial(lax.dynamic_slice_in_dim, start_index=core * local, slice_size=local)
    cut_heads = functools.partial(lax.dynamic_slice_in_dim, start_index=core * heads, slice_size=heads)
    conv_w, conv_b, norm_gain, routes = order((conv_w, conv_b, norm_gain, routes))
    conv_all = jnp.concatenate([conv_w, conv_b[None]])
    kern = jnp.concatenate(
        [cut(conv_all, axis=1), jnp.zeros((5, LANES), F32), conv_all[:, inner_all:]], axis=1
    )
    tail = jnp.zeros((1, kern.shape[1] - local), F32)
    skip_wide = jnp.repeat(cut_heads(d_skip, axis=0), P_SIZE)[None]
    kern = jnp.concatenate(
        [
            kern,
            jnp.concatenate([skip_wide, tail], axis=1),
            jnp.concatenate([cut(norm_gain, axis=0)[None], tail], axis=1),
            jnp.zeros((1, kern.shape[1]), F32),
        ]
    )
    head_par = jnp.pad(
        jnp.stack([cut_heads(dt_bias, axis=0), jnp.exp(cut_heads(a_log, axis=0))]),
        ((0, 6), (0, LANES - heads)),
    )
    head_of = jnp.arange(local, dtype=jnp.int32) // P_SIZE
    spread = (lax.rem(lane, LANES // 2)[:, None] == head_of[None, :]).astype(BF)
    own_routes = lax.dynamic_slice_in_dim(routes, core * piece, piece, 0)
    go_ring = [order(jnp.concatenate([w_zx[:, 0], w_out.T], axis=1))]
    order.set(kern, head_par, spread, own_routes, go_ring[0])
    ring_on(ring_a, order, 1 + 2 * third, lines, lines)
    ring_on(ring_b, order, 1 + 2 * third, lines, lines)
    order.set(ring_a[-1], ring_b[-1])

    def matrix(parts, cut_at):
        return pieces_of(parts, mixer_targets, cut_at)

    def along_both(stacked):
        return [stacked, hop(stacked, 1), hop(stacked, 2)]

    def across_halves(parts, cut_at):
        width = parts[0].shape[2]
        low, high = cut_columns(parts[1], 0, cut_at), cut_columns(parts[2], cut_at, width - cut_at)
        order.set(low, high)
        return parts + [hop(low, 2), hop(high, 1)]

    tokens_other = order.take(tokens_other)
    in_stack = stack_pairs(ring_a, ring_b)
    marked = marked_rows(order(grad_out), own_routes, heads)
    order.set(in_stack, marked)
    ring_on(go_ring, order, 1, 1 + third, lines)
    order.set(go_ring[-1])
    in_w = along_both(order(in_stack))
    came = order.take(*came)
    expert_ring = [stack_columns(came, 0, 3 * hidden)]
    normed = normed_rows(order(tokens), tokens_other, gain_in, core_now)
    order.set(normed, expert_ring[0])
    ring_on(go_ring, order, 1 + third, 1 + 2 * third, lines)
    order.set(go_ring[-1])
    marked_other = swap(order(marked))
    in_w = list(order.take(*in_w))
    marked_other = order.take(marked_other)
    in_w = across_halves(in_w, cut_in)
    ring_on(go_ring, order, 1 + 2 * third, lines, lines)
    order.set(go_ring[-1])
    gate_stack = stack_columns(go_ring, 0, local)
    expert_ring[0] = order(expert_ring[0])
    in_w = order.take(*in_w, gate_stack)
    gate_stack, in_w = in_w[-1], list(in_w[:-1])

    gate_w = along_both(gate_stack)
    in_matrix = matrix(in_w, cut_in)
    zi, router_w = inner_product(order(normed), in_matrix, local)
    y, states = front_scan(zi, kern, head_par, spread)
    order.set(y)
    gate_w = list(order.take(*gate_w))
    gate_w = across_halves(gate_w, cut_gate)
    out_stack = stack_columns(order(go_ring), local, width_d)
    order.set(out_stack)
    ring_on(expert_ring, order, 1, 1 + third, lines)
    order.set(expert_ring[-1])
    gate_w = list(order.take(*gate_w))
    out_w = along_both(order(out_stack))
    gate_matrix = matrix(gate_w, cut_gate)
    gate, squares = gate_product(order(normed), y, gate_matrix)
    order.set(gate)
    squares_other = order.take(swap(squares))
    out_w = list(order.take(*out_w))
    out_w = across_halves(out_w, cut_gate)
    out_w = list(order.take(*out_w))
    ring_on(expert_ring, order, 1 + third, 1 + 2 * third, lines)
    order.set(expert_ring[-1])
    marked_sent = order(marked)
    marked_x, marked_y = hop(marked_sent, 1), hop(marked_sent, 2)
    out_matrix = matrix(out_w, cut_gate)
    scaled, mixed_sent, mixed_mine = mixed_product(
        order(y), gate, squares, squares_other, kern, out_matrix, mine_last, inner_all
    )
    order.set(mixed_mine)
    marked_x, marked_y = order.take(marked_x, marked_y)
    half_rows = piece // 2

    def halves_of(from_x, from_y):
        return cut_rows_of(from_x, 0, half_rows), cut_rows_of(from_y, half_rows, half_rows)

    def across(halves):
        return hop(halves[0], 2), hop(halves[1], 1)

    marked_halves = halves_of(marked_x, marked_y)
    order.set(*marked_halves)
    ring_on(expert_ring, order, 1 + 2 * third, lines, lines)
    order.set(expert_ring[-1])
    mixed_came = order.take(swap(order(mixed_sent)))
    resid, mid = mid_rows_of(mixed_mine, mixed_came, tokens, gain_mid)
    order.set(mid)

    mid_x, mid_y = hop(mid, 1), hop(mid, 2)
    mid_other = order.take(swap(mid))
    marked_swap_x, marked_swap_y = swap(order(marked_x)), swap(order(marked_y))
    parts, _, expert_order = pieces_of(expert_ring, expert_targets, 0)
    common = (base, router_w, parts, expert_order, units, shared_units)
    kept, result_0 = expert_rows(
        [0], [order(mid), mid_other], [marked, marked_other], [], *common
    )
    order.set(result_0[0])
    mid_x, mid_y, marked_swap_x, marked_swap_y = order.take(
        mid_x, mid_y, marked_swap_x, marked_swap_y
    )
    mid_swap_x, mid_swap_y = order.take(swap(mid_x), swap(mid_y))
    mid_halves = halves_of(mid_x, mid_y)
    order.set(*mid_halves, mid_swap_x, mid_swap_y)
    mid_d, marked_d = across(order(mid_halves)), across(order(marked_halves))
    kept, result = expert_rows(
        [1, 2], order([mid_x, mid_swap_x, mid_y, mid_swap_y]),
        [marked_x, marked_swap_x, marked_y, marked_swap_y], kept, *common,
    )
    order.set(result[0])
    mid_d = order.take(*mid_d)
    marked_d = order.take(*marked_d)
    mid_d_other = order.take(*[swap(item) for item in mid_d])
    marked_d_other = order.take(*[swap(item) for item in marked_d])
    d_others, d_other_0 = swap(order(result[3])), swap(order(result_0[3]))
    kept, result_3 = expert_rows(
        [3], [order(mid_d), mid_d_other], [marked_d, marked_d_other], kept, *common
    )
    order.set(result_3[0])
    x_all, dy_all, gu, down = kept
    d_others, d_other_0 = order.take(d_others, d_other_0)
    d_other_3 = order.take(swap(result_3[3]))
    over_low, over_high = across_sum(result_3[2], d_other_3, 0)
    order.set(over_low)
    d_over = hop(over_low, 1), hop(over_high, 2)
    out_others = swap(order(result_3[1])), swap(order(result[1])), swap(order(result_0[1]))

    grad_down = tn(order(dy_all), down, BF)
    order.set(grad_down)
    d_over = order.take(*d_over)
    out_other_3, out_others, out_other_0 = order.take(*out_others)
    to_x, to_y = side_sums(result[2], d_others, *d_over)
    order.set(to_x)
    arrays = {}

    def whole_block(name, width):
        return lambda line_at: [(width, [(arrays[name], 0, line_at)], None)]

    sums = LineSums(
        {"gu": whole_block("gu", 2 * hidden), "down": whole_block("down", hidden)},
        order, lines, GROUP * height, where,
    )
    arrays["down"] = grad_down
    arrays["gu"] = None
    sums.start("down")
    d_came = hop(to_x, 1), hop(to_y, 2)
    out_over = across_sum(result_3[0], order(out_other_3), 0)
    order.set(out_over[0], sums.sent)
    out_over = hop(out_over[0], 1), hop(out_over[1], 2)
    grad_gu = tn(order(x_all), gu, BF)
    order.set(grad_gu)
    arrays["gu"] = grad_gu
    sums.run(third, "gu")
    order.set(sums.sent)
    d_came = order.take(*d_came)
    out_over = order.take(*out_over)
    out_sums = side_sums(result[0], out_others, *out_over)
    order.set(out_sums[0])
    out_came = hop(out_sums[0], 1), hop(out_sums[1], 2)

    d_resid, d_mix_mine, pulls, mid_gains = resid_back(
        result_0[2], d_other_0, *d_came, order(resid), tokens, grad_out, gain_mid
    )
    order.set(d_mix_mine)
    d_mix_came, pulls_came = order.take(swap(d_mix_mine), swap(pulls))
    d_mix, pulls = pair_rows([(d_mix_mine, order(d_mix_came)), (pulls, pulls_came)], core_now)
    order.set(d_mix)
    d_y, dz_a, dz_b, gain_grads = gate_back(
        order(d_mix), y, gate, squares, squares_other, pulls, kern, out_matrix, cut_gate, inner_all
    )
    order.set(d_y)
    out_came = order.take(*out_came)

    def hop_first(pair):
        sent = [item.start(order) for item in pair]
        order.set(*sent)
        for item, values in zip(pair, sent):
            item.came = hop(values, item.bits)

    def hop_second(pair):
        for item in pair:
            item.came = order(item.came)
        sent = [item.turn() for item in pair]
        order.set(*sent)
        for item, values in zip(pair, sent):
            item.came_last = hop(values, 3 - item.bits)

    def all_came(pair):
        for item in pair:
            item.came_last = order(item.came_last)
        order.set(*[item.came_last for item in pair])

    grad_out_w = tn(order(d_mix), scaled, BF)
    normed_now = order(normed)
    grad_gate_a, grad_gate_b = tn(normed_now, dz_a, BF), tn(normed_now, dz_b, BF)
    order.set(grad_gate_a, grad_gate_b, grad_out_w)
    og_pair = [
        Plane([(grad_out_w, 0, cut_gate), (grad_gate_a, 0, cut_gate)], 1, where, lines),
        Plane([(grad_out_w, 1, cut_gate), (grad_gate_b, 0, cut_gate)], 2, where, lines),
    ]
    hop_first(og_pair)
    sums.run(third)
    order.set(sums.sent)
    di_a, di_b, par_grads, head_grads = back_scan(
        order(d_y), zi, states, kern, head_par, spread, cut_in
    )
    order.set(di_a)
    hop_second(og_pair)
    grad_in_a = tn(order(normed), di_a, BF)
    start = local - cut_in
    grad_router = jnp.pad(
        order(grad_gu[:, 2 * hidden :]).astype(F32),
        ((0, 0), (start, di_b.shape[1] - start - LANES)),
    )
    grad_in_b = (tn(order(normed), di_b) + grad_router).astype(BF)
    order.set(grad_in_a, grad_in_b)
    sums.run(third)
    order.set(sums.sent)
    all_came(og_pair)
    in_pair = [
        Plane([(grad_in_a, 0, cut_in)], 1, where, lines),
        Plane([(grad_in_b, 0, grad_in_b.shape[1])], 2, where, lines),
    ]
    hop_first(in_pair)
    d_sent, d_mine = normed_back(
        order([dz_a, dz_b, di_a, di_b]), [gate_matrix, in_matrix], mine_last
    )
    order.set(d_mine)

    def pair_groups(pair):
        return lambda line_at: [group for item in pair for group in item.groups(line_at)]

    rest = LineSums(
        {"og": pair_groups(og_pair), "in": pair_groups(in_pair)}, order, lines, height, where
    )
    hop_second(in_pair)
    sums.run(third)
    order.set(sums.final["gu"])
    rest.start("og")
    order.set(rest.sent)
    to_send = member_pieces(sums.final["gu"], sums.final["down"], where, height)
    order.set(*to_send)
    all_came(in_pair)
    came = to_send[:1] + [hop(order(to_send[k]), k) for k in range(1, GROUP)]
    rest.run(third)
    order.set(rest.sent)
    d_other = order.take(swap(order(d_sent)))
    grad_tokens, in_gains = tokens_back(d_mine, d_other, tokens, d_resid, gain_in)
    order.set(grad_tokens)
    small = pack_small(
        par_grads, head_grads, gain_grads, mid_gains, in_gains, spread, core_now, local, heads
    )
    order.set(small)
    rest.run(third, "in")
    order.set(rest.sent)
    small = order.take(small + order(swap(small)))
    output = output_rows(order(result_0[0]), out_other_0, *out_came, resid)
    order.set(output)
    small = order.take(small + order(hop(small, 1)))
    rest.run(third)
    order.set(rest.sent)
    came = list(order.take(*came))
    g_egu, g_edown, g_sgu, g_sdown = unpack_experts(came, place_now, units, shared_units)
    order.set(g_edown)
    rest.run(third)
    order.set(rest.sent)
    bits = 2
    while bits < lines * GROUP:
        small = order.take(small + order(hop(small, bits)))
        bits *= 2
    rest.run(third)
    og_held, g_inner = rest.final["og"], rest.final["in"]
    quarters = [og_held[:, i * cut_gate : (i + 1) * cut_gate] for i in range(4)]
    g_out = jnp.concatenate([quarters[0], quarters[2]], axis=1).T
    g_gate = jnp.concatenate([quarters[1], quarters[3]], axis=1)
    g_zx = jnp.stack([g_gate, g_inner[:, :local]], axis=1)
    g_dt = g_inner[:, local : local + heads]
    g_joint = jnp.concatenate(
        [g_inner[:, local + heads : local + heads + EXPERTS], g_inner[:, local + LANES :]], axis=1
    )
    joint_rows = height // 2
    g_joint = lax.dynamic_slice_in_dim(g_joint, core * joint_rows, joint_rows, 0) + swap(
        lax.dynamic_slice_in_dim(g_joint, (1 - core) * joint_rows, joint_rows, 0)
    )

    def of_heads(number):
        return jnp.concatenate(
            [
                small[7, (2 * number + which) * LANES : (2 * number + which) * LANES + heads]
                for which in range(2)
            ]
        )

    return (
        output, grad_tokens, small[6, :width_d], g_zx, g_dt, g_joint[:, EXPERTS:], small[:4],
        small[4], of_heads(0), of_heads(1), of_heads(2), small[5, :inner_all], g_out,
        small[6, width_d : 2 * width_d], g_joint[:, :EXPERTS], g_sgu, g_sdown, g_egu, g_edown,
    )


def solution(mesh):
    both = P(("dp", "tensor"), None)
    rows = P("dp", None, "tensor")
    cols = P("tensor", "dp")
    return jax.shard_map(
        shards,
        mesh=mesh,
        in_specs=(
            both, P("dp", None), P(), rows, P("dp", "tensor"), both, P(), P(), P(), P(), P(), P(),
            cols, P(), both, rows, cols, P(None, "dp", None, "tensor"), P(None, "tensor", "dp"),
            both,
        ),
        out_specs=(
            both, both, P(), rows, P("dp", "tensor"), both, P(), P(), P(), P(), P(), P(),
            cols, P(), both, rows, cols, P(None, "dp", None, "tensor"), P(None, "tensor", "dp"),
        ),
        check_vma=False,
    )
```

```python
import functools

import jax
import jax.numpy as jnp
from jax import lax
from jax.experimental import pallas as pl
from jax.experimental.pallas import tpu as pltpu
from jax.sharding import PartitionSpec as P

F32 = jnp.float32
BF = jnp.bfloat16
EPS = 1e-05
H = 48
P_SIZE = 64
NS = 128
EXPERTS = 16
BL = 128
GROUP = 4
LANES = 128
VMEM = 60 * 1024 * 1024
SMALL = pl.CostEstimate(flops=1000, bytes_accessed=1000, transcendentals=0)
highest = lax.Precision.HIGHEST


def nn(left, right):
    return lax.dot_general(left, right, (((1,), (0,)), ((), ())), preferred_element_type=F32)


def nt(left, right):
    return lax.dot_general(left, right, (((1,), (1,)), ((), ())), preferred_element_type=F32)


def tn(left, right, kind=F32):
    return lax.dot_general(left, right, (((0,), (0,)), ((), ())), preferred_element_type=kind)


def hop(values, bits):
    count = lax.axis_size("dp")
    return lax.ppermute(values, "dp", [(i, i ^ bits) for i in range(count)])


def next_line(values):
    count = lax.axis_size("dp")
    return lax.ppermute(values, "dp", [(i, (i + GROUP) % count) for i in range(count)])


def swap(values):
    return lax.ppermute(values, "tensor", [(0, 1), (1, 0)])


def pick(values, index, axis=0):
    return lax.dynamic_index_in_dim(values, index, axis, keepdims=False)


def in_order(mine, theirs, core):
    return jnp.where(
        core == 0, jnp.concatenate([mine, theirs]), jnp.concatenate([theirs, mine])
    )


def tie(values, *others):
    flat, tree = jax.tree.flatten(values)
    held = lax.optimization_barrier((flat, others))
    return jax.tree.unflatten(tree, held[0])


class Order:
    def __init__(self):
        self.marks = self.last = ()

    def __call__(self, values):
        return tie(values, *self.marks)

    def set(self, *marks):
        self.marks, self.last = marks + self.last, marks

    def take(self, *values):
        values = self(values)
        self.set(*values)
        return values if len(values) > 1 else values[0]


def ring_on(blocks, order, low, high, lines):
    for _ in range(low, min(high, lines)):
        blocks.append(order(next_line(blocks[-1])))


def pieces_of(parts, targets, cut):
    inner, height, width = parts[0].shape
    starts = [0] * len(parts)
    if cut:
        starts[-1] = cut
    if height % 32 == 0:
        return parts, starts, targets
    if cut:
        parts = parts[:3] + [jnp.concatenate(parts[3:], axis=-1)]
    flat = jnp.concatenate(parts)
    total = flat.shape[0]
    source = jnp.zeros((total,), jnp.int32)
    source = source.at[targets[:total]].set(jnp.arange(total, dtype=jnp.int32))
    whole = flat[source].reshape(1, total * height, width)
    return [whole], [0], jnp.zeros((1,), jnp.int32)


def load_pieces(target_ref, part_refs, starts, held, base, sems):
    copies = []
    for ref, start in zip(part_refs, starts):
        inner, height, width = ref.shape
        for j in range(inner):
            row = pl.multiple_of(target_ref[len(copies)] * height, height)
            copies.append(
                pltpu.make_async_copy(
                    ref.at[j],
                    held.at[pl.ds(row, height), base + start : base + start + width],
                    sems.at[len(copies)],
                )
            )
    return copies


def run_copies(copies):
    for copy in copies:
        copy.start()
    for copy in copies:
        copy.wait()


def norm_rows(values):
    return lax.rsqrt(jnp.mean(values * values, axis=-1, keepdims=True) + EPS)


def sigmoid(values):
    return 1.0 / (1.0 + jnp.exp(-values))


def split_two(values):
    high = values.astype(BF)
    return high, (values - high.astype(F32)).astype(BF)


def spread_heads(values, spread):
    high, low = split_two(values)
    packed = high.astype(F32) + pltpu.roll(low.astype(F32), LANES // 2, 1)
    return nn(packed.astype(BF), spread)


def gather_heads(values, spread, heads_on):
    high, low = split_two(values)
    return jnp.where(heads_on, nt(high, spread) + nt(low, spread), 0.0)


def conv_rows(ext, kern, low, high, offset):
    summed = kern[4:5, low:high]
    for j in range(4):
        summed = summed + kern[j : j + 1, low:high] * ext[offset + j : offset + j + BL, low:high]
    return summed


def step_terms(raw, head_par, heads_on):
    shifted = raw + head_par[0:1]
    soft = jnp.maximum(shifted, 0.0) + jnp.log1p(jnp.exp(-jnp.abs(shifted)))
    step = jnp.where(heads_on, soft, 0.0)
    return shifted, step, -step * head_par[1:2]


def front_body(zi_ref, kern_ref, head_ref, spread_ref, y_ref, state_ref, ext, state):
    width = y_ref.shape[1]
    first = pl.program_id(0) == 0

    @pl.when(first)
    def _():
        ext[0:8, :] = jnp.zeros((8, ext.shape[1]), F32)
        state[...] = jnp.zeros(state.shape, F32)

    @pl.when(jnp.logical_not(first))
    def _():
        ext[0:8, :] = ext[BL : BL + 8, :]

    ext[8 : BL + 8, :] = zi_ref[...]
    rows = lax.broadcasted_iota(jnp.int32, (BL, LANES), 0)
    cols = lax.broadcasted_iota(jnp.int32, (BL, LANES), 1)
    causal = cols <= rows
    heads_on = cols < width // P_SIZE
    spread = spread_ref[...]
    state_ref[0] = state[...]
    pre = conv_rows(ext, kern_ref, 0, width, 5)
    x = pre * sigmoid(pre)
    pre = conv_rows(ext, kern_ref, width + LANES, ext.shape[1], 5)
    maps = pre * sigmoid(pre)
    b, c = maps[:, :NS], maps[:, NS:]
    shifted, step, decay = step_terms(zi_ref[:, width : width + LANES], head_ref, heads_on)
    cum = jnp.dot(causal.astype(F32), decay, precision=highest, preferred_element_type=F32)
    cum_t = cum.T
    last = cum[BL - 1 : BL]
    scores = nt(c.astype(BF), b.astype(BF))
    u = x * spread_heads(step, spread)
    from_start = spread_heads(jnp.where(heads_on, jnp.exp(cum), 0.0), spread)
    to_end = spread_heads(jnp.where(heads_on, jnp.exp(last - cum), 0.0), spread)
    u_low = u.astype(BF)
    left = cols < P_SIZE
    within = []
    for pair in range(width // LANES):
        mats = []
        for head in (2 * pair, 2 * pair + 1):
            gap = cum[:, head : head + 1] - cum_t[head : head + 1, :]
            mats.append((jnp.where(causal, jnp.exp(gap), 0.0) * scores).astype(BF))
        cut = u_low[:, pair * LANES : (pair + 1) * LANES]
        zero = jnp.zeros_like(cut)
        stacked = jnp.concatenate([jnp.where(left, cut, zero), jnp.where(left, zero, cut)], axis=0)
        within.append(nn(jnp.concatenate(mats, axis=1), stacked))
    before = state[...]
    across = nn(c.astype(BF), before.astype(BF)) * from_start
    y_ref[...] = jnp.concatenate(within, axis=1) + across + kern_ref[5:6, :width] * x
    grown = nn(b.T.astype(BF), (u * to_end).astype(BF))
    state[...] = before * from_start[BL - 1 : BL] + grown


def front_scan(zi, kern, head_par, spread):
    length, width = zi.shape[0], spread.shape[1]
    steps = length // BL
    return pl.pallas_call(
        front_body,
        grid=(steps,),
        out_shape=(
            jax.ShapeDtypeStruct((length, width), F32),
            jax.ShapeDtypeStruct((steps, NS, width), F32),
        ),
        in_specs=[
            pl.BlockSpec((BL, zi.shape[1]), lambda i: (i, 0)),
            pl.BlockSpec(kern.shape, lambda i: (0, 0)),
            pl.BlockSpec(head_par.shape, lambda i: (0, 0)),
            pl.BlockSpec(spread.shape, lambda i: (0, 0)),
        ],
        out_specs=(
            pl.BlockSpec((BL, width), lambda i: (i, 0)),
            pl.BlockSpec((1, NS, width), lambda i: (i, 0, 0)),
        ),
        scratch_shapes=[pltpu.VMEM((BL + 8, zi.shape[1]), F32), pltpu.VMEM((NS, width), F32)],
        compiler_params=pltpu.CompilerParams(
            dimension_semantics=("arbitrary",), vmem_limit_bytes=VMEM
        ),
        cost_estimate=SMALL,
        name="front_scan",
    )(zi, kern, head_par, spread)


def back_body(
    dy_ref, zi_ref, prev_ref, state_ref, kern_ref, head_ref, spread_ref,
    dia_ref, dib_ref, par_ref, hg_ref, ext, ext_d, d_state,
):
    width = dy_ref.shape[1]
    wide = zi_ref.shape[1]
    cut_at = dia_ref.shape[1]
    number = pl.program_id(0)
    steps = pl.num_programs(0)

    @pl.when(number == 0)
    def _():
        ext_d[BL : BL + 8, :] = jnp.zeros((8, wide), F32)
        d_state[...] = jnp.zeros(d_state.shape, F32)
        par_ref[...] = jnp.zeros(par_ref.shape, F32)
        hg_ref[...] = jnp.zeros(hg_ref.shape, F32)

    @pl.when(number > 0)
    def _():
        ext_d[BL : BL + 8, :] = ext_d[0:8, :]

    ext[0:8, :] = jnp.where(number == steps - 1, 0.0, prev_ref[...])
    ext[8 : BL + 8, :] = zi_ref[...]
    rows = lax.broadcasted_iota(jnp.int32, (BL, LANES), 0)
    cols = lax.broadcasted_iota(jnp.int32, (BL, LANES), 1)
    upper = rows <= cols
    strict = rows < cols
    heads_on = cols < width // P_SIZE
    left = cols < P_SIZE
    spread = spread_ref[...]
    pre_x = conv_rows(ext, kern_ref, 0, width, 5)
    sig_x = sigmoid(pre_x)
    x = pre_x * sig_x
    pre_m = conv_rows(ext, kern_ref, width + LANES, wide, 5)
    sig_m = sigmoid(pre_m)
    maps = pre_m * sig_m
    b, c = maps[:, :NS], maps[:, NS:]
    b_low, c_low = b.astype(BF), c.astype(BF)
    shifted, step, decay = step_terms(zi_ref[:, width : width + LANES], head_ref, heads_on)
    cum = jnp.dot(
        (cols <= rows).astype(F32), decay, precision=highest, preferred_element_type=F32
    )
    cum_t = cum.T
    last = cum[BL - 1 : BL]
    step_wide = spread_heads(step, spread)
    from_start = spread_heads(jnp.where(heads_on, jnp.exp(cum), 0.0), spread)
    to_end = spread_heads(jnp.where(heads_on, jnp.exp(last - cum), 0.0), spread)
    whole = from_start[BL - 1 : BL]
    d_y = dy_ref[...]
    par_ref[5:6, :width] += jnp.sum(d_y * x, axis=0, keepdims=True)
    u = x * step_wide
    u_low, dy_low = u.astype(BF), d_y.astype(BF)
    scores_t = nt(b_low, c_low)
    d_scores_t = jnp.zeros((BL, BL), F32)
    du_parts = []
    gap_rows = jnp.zeros((BL, LANES), F32)
    gap_cols = []
    for pair in range(width // LANES):
        lanes = slice(pair * LANES, (pair + 1) * LANES)
        cut_u, cut_d = u_low[:, lanes], dy_low[:, lanes]
        zero = jnp.zeros_like(cut_u)
        stack_u = jnp.concatenate([jnp.where(left, cut_u, zero), jnp.where(left, zero, cut_u)], axis=0)
        stack_d = jnp.concatenate([jnp.where(left, cut_d, zero), jnp.where(left, zero, cut_d)], axis=0)
        d_weights = nt(stack_u, cut_d)
        mats = []
        for place, head in enumerate((2 * pair, 2 * pair + 1)):
            gap = cum_t[head : head + 1, :] - cum[:, head : head + 1]
            decays = jnp.where(upper, jnp.exp(gap), 0.0)
            weight = decays * scores_t
            mats.append(weight.astype(BF))
            d_weight = d_weights[place * BL : (place + 1) * BL]
            d_scores_t = d_scores_t + decays * d_weight
            moved = jnp.where(strict, weight * d_weight, 0.0)
            gap_rows = jnp.where(cols == head, jnp.sum(moved, axis=1, keepdims=True), gap_rows)
            gap_cols.append(jnp.sum(moved, axis=0, keepdims=True))
        du_parts.append(nn(jnp.concatenate(mats, axis=1), stack_d))
    gap_cols.append(jnp.zeros((LANES - width // P_SIZE, BL), F32))
    gap_cols = jnp.concatenate(gap_cols, axis=0).T
    before, d_after = state_ref[0], d_state[...]
    before_low, d_after_low = before.astype(BF), d_after.astype(BF)
    dy_start = d_y * from_start
    dy_start_low = dy_start.astype(BF)
    reach = gather_heads(dy_start * nn(c_low, before_low), spread, heads_on)
    u_end = u * to_end
    d_from_state = nn(b_low, d_after_low)
    kept = gather_heads(u_end * d_from_state, spread, heads_on)
    carried = jnp.sum(before * d_after, axis=0, keepdims=True) * whole
    carried = gather_heads(jnp.broadcast_to(carried, (8, width)), spread, heads_on[:8])[0:1]
    d_c = nt(dy_start_low, before_low) + nn(d_scores_t.T.astype(BF), b_low)
    d_b = nt(u_end.astype(BF), d_after_low) + nn(d_scores_t.astype(BF), c_low)
    d_state[...] = d_after * whole + nn(c.T.astype(BF), dy_start_low)
    d_u = jnp.concatenate(du_parts, axis=1) + to_end * d_from_state
    d_decay = (
        jnp.dot(
            upper.astype(F32), reach + gap_cols - gap_rows, precision=highest,
            preferred_element_type=F32,
        )
        + jnp.dot(
            (cols < rows).astype(F32), kept, precision=highest, preferred_element_type=F32
        )
        + carried
    )
    d_step = gather_heads(x * d_u, spread, heads_on)
    rate = head_ref[1:2]
    d_raw = jnp.where(heads_on, (d_step - rate * d_decay) * sigmoid(shifted), 0.0)
    hg_ref[0:1, :] += jnp.sum(d_raw, axis=0, keepdims=True)
    hg_ref[1:2, :] += jnp.sum(jnp.where(heads_on, d_decay * decay, 0.0), axis=0, keepdims=True)
    d_x = step_wide * d_u + kern_ref[5:6, :width] * d_y
    ext_d[0:BL, :width] = d_x * sig_x * (1.0 + pre_x * (1.0 - sig_x))
    ext_d[0:BL, width : width + LANES] = jnp.zeros((BL, LANES), F32)
    ext_d[0:BL, width + LANES :] = (
        jnp.concatenate([d_b, d_c], axis=1) * sig_m * (1.0 + pre_m * (1.0 - sig_m))
    )
    for low, high in ((0, cut_at), (cut_at, width), (width + LANES, wide)):
        d_act = ext_d[0:BL, low:high]
        d_in = jnp.zeros((BL, high - low), F32)
        for j in range(4):
            d_in = d_in + kern_ref[j : j + 1, low:high] * ext_d[3 - j : 3 - j + BL, low:high]
            par_ref[j : j + 1, low:high] += jnp.sum(
                d_act * ext[5 + j : 5 + j + BL, low:high], axis=0, keepdims=True
            )
        par_ref[4:5, low:high] += jnp.sum(d_act, axis=0, keepdims=True)
        if low < cut_at:
            dia_ref[...] = d_in.astype(BF)
        else:
            dib_ref[:, low - cut_at : high - cut_at] = d_in.astype(BF)
    dib_ref[:, width - cut_at : width - cut_at + LANES] = d_raw.astype(BF)


def back_scan(d_y, zi, states, kern, head_par, spread, cut_at):
    length, width = d_y.shape
    wide = zi.shape[1]
    steps = length // BL
    per = BL // 8

    def back(i):
        return (steps - 1 - i, 0)

    def fixed(i):
        return (0, 0)

    return pl.pallas_call(
        back_body,
        grid=(steps,),
        out_shape=(
            jax.ShapeDtypeStruct((length, cut_at), BF),
            jax.ShapeDtypeStruct((length, wide - cut_at), BF),
            jax.ShapeDtypeStruct((8, wide), F32),
            jax.ShapeDtypeStruct((8, LANES), F32),
        ),
        in_specs=[
            pl.BlockSpec((BL, width), back),
            pl.BlockSpec((BL, wide), back),
            pl.BlockSpec((8, wide), lambda i: (jnp.maximum((steps - 1 - i) * per - 1, 0), 0)),
            pl.BlockSpec((1, NS, width), lambda i: (steps - 1 - i, 0, 0)),
            pl.BlockSpec(kern.shape, fixed),
            pl.BlockSpec(head_par.shape, fixed),
            pl.BlockSpec(spread.shape, fixed),
        ],
        out_specs=(
            pl.BlockSpec((BL, cut_at), back),
            pl.BlockSpec((BL, wide - cut_at), back),
            pl.BlockSpec((8, wide), fixed),
            pl.BlockSpec((8, LANES), fixed),
        ),
        scratch_shapes=[
            pltpu.VMEM((BL + 8, wide), F32),
            pltpu.VMEM((BL + 8, wide), F32),
            pltpu.VMEM((NS, width), F32),
        ],
        compiler_params=pltpu.CompilerParams(
            dimension_semantics=("arbitrary",), vmem_limit_bytes=VMEM
        ),
        cost_estimate=SMALL,
        name="back_scan",
    )(d_y, zi, zi, states, kern, head_par, spread)


def small_call(body, outs, args, name, scalars=0):
    vmem, smem = pl.BlockSpec(memory_space=pltpu.VMEM), pl.BlockSpec(memory_space=pltpu.SMEM)
    return pl.pallas_call(
        body,
        out_shape=tuple(jax.ShapeDtypeStruct(shape, kind) for shape, kind in outs),
        in_specs=[smem] * scalars + [vmem] * (len(args) - scalars),
        out_specs=tuple(vmem for _ in outs),
        compiler_params=pltpu.CompilerParams(vmem_limit_bytes=VMEM),
        cost_estimate=SMALL,
        name=name,
    )(*args)


def stack_columns(blocks, start, width):
    height = blocks[0].shape[0]

    def body(*refs):
        for number, ref in enumerate(refs[:-1]):
            refs[-1][number] = ref[:, start : start + width]

    shape = (len(blocks), height, width)
    return small_call(body, [(shape, blocks[0].dtype)], blocks, "stack_columns")[0]


def stack_pairs(first, second):
    height, low = first[0].shape
    high = second[0].shape[1]

    def body(*refs):
        for number in range(len(first)):
            refs[-1][number, :, :low] = refs[number][...]
            refs[-1][number, :, low:] = refs[len(first) + number][...]

    shape = (len(first), height, low + high)
    return small_call(body, [(shape, first[0].dtype)], [*first, *second], "stack_pairs")[0]


def cut_columns(values, start, width):
    def body(values_ref, out_ref):
        out_ref[...] = values_ref[:, :, start : start + width]

    return small_call(
        body, [(values.shape[:2] + (width,), values.dtype)], [values], "cut_columns"
    )[0]


def cut_rows_of(values, start, rows):
    def body(values_ref, out_ref):
        out_ref[...] = values_ref[start : start + rows]

    return small_call(body, [((rows, values.shape[1]), values.dtype)], [values], "cut_rows")[0]


def pair_rows(pairs, core):
    def body(core_ref, *refs):
        for number in range(len(pairs)):
            mine_ref, other_ref = refs[2 * number : 2 * number + 2]
            out_ref = refs[2 * len(pairs) + number]
            out_ref[core_ref[0]] = mine_ref[...]
            out_ref[1 - core_ref[0]] = other_ref[...]

    outs = [((2,) + mine.shape, mine.dtype) for mine, _ in pairs]
    args = [core] + [item for pair in pairs for item in pair]
    done = small_call(body, outs, args, "pair_rows", 1)
    return [item.reshape(-1, item.shape[2]) for item in done]


def add_blocks(groups, height, count, kind, where, name):
    total = sum(width for width, _, _ in groups)
    flat = [(width, item) for width, items, _ in groups for item in items]
    overs = []
    for _, _, over in groups:
        if over is not None and not any(over[0] is array for array in overs):
            overs.append(over[0])

    if height % 32:
        columns = []
        for width, items, over in groups:
            term = 0.0
            for array, number, spot in items:
                part = array[:, number * width : (number + 1) * width].reshape(-1, height, width)
                picked = [pick(part, spot(i, where)) for i in range(count)]
                term = term + jnp.concatenate(picked).astype(F32)
            if over is not None:
                term = term + over[0][:, over[1] : over[1] + width].astype(F32)
            columns.append(term)
        return jnp.concatenate(columns, axis=1).astype(kind)

    def body(where_ref, *refs):
        item_refs = refs[: len(flat)]
        over_refs = refs[len(flat) : len(flat) + len(overs)]
        out_ref, sems = refs[len(flat) + len(overs)], refs[-1]
        helds = refs[len(flat) + len(overs) + 1 : -1]
        copies = []
        for row, (ref, held, (width, (_, number, spot))) in enumerate(zip(item_refs, helds, flat)):
            for i in range(count):
                start = pl.multiple_of(spot(i, where_ref) * height, height)
                copies.append(
                    pltpu.make_async_copy(
                        ref.at[pl.ds(start, height), number * width : (number + 1) * width],
                        held.at[i * height : (i + 1) * height],
                        sems.at[row, i],
                    )
                )
        run_copies(copies)
        at = start = 0
        for width, items, over in groups:
            term = helds[at][...]
            if len(items) > 1 or over is not None:
                term = term.astype(F32)
            for held in helds[at + 1 : at + len(items)]:
                term = term + held[...].astype(F32)
            if over is not None:
                (number,) = [i for i, array in enumerate(overs) if array is over[0]]
                term = term + over_refs[number][:, over[1] : over[1] + width].astype(F32)
            out_ref[:, start : start + width] = term.astype(kind)
            at += len(items)
            start += width

    vmem, any_ref = pl.BlockSpec(memory_space=pltpu.VMEM), pl.BlockSpec(memory_space=pl.ANY)
    return pl.pallas_call(
        body,
        out_shape=jax.ShapeDtypeStruct((count * height, total), kind),
        in_specs=[pl.BlockSpec(memory_space=pltpu.SMEM)]
        + [any_ref] * len(flat)
        + [vmem] * len(overs),
        out_specs=vmem,
        scratch_shapes=[
            pltpu.VMEM((count * height, width), item[0].dtype) for width, item in flat
        ]
        + [pltpu.SemaphoreType.DMA((len(flat), count))],
        compiler_params=pltpu.CompilerParams(vmem_limit_bytes=VMEM),
        cost_estimate=SMALL,
        name=name,
    )(where, *[item[0] for _, item in flat], *overs)


class Plane:
    def __init__(self, values, bits, where, lines):
        self.values, self.bits, self.where, self.lines = values, bits, where, lines
        self.height = values[0][0].shape[0] // (lines * GROUP)
        self.came = self.came_last = None

    def _spot(self, i, first, second):
        x, y = (first, second) if self.bits == 1 else (second, first)
        return i * GROUP + y * 2 + x

    def _own(self, where, axis):
        return lax.rem(where[0], 2) if axis == 1 else where[0] // 2

    def start(self, order):
        def spot(i, where):
            return self._spot(i // 2, 1 - self._own(where, self.bits), i % 2)

        groups = [
            (width, [(order(array), number, spot)], None) for array, number, width in self.values
        ]
        return add_blocks(groups, self.height, 2 * self.lines, BF, self.where, "plane_start")

    def _groups(self, keep, line_at, last):
        def which(where):
            own = self._own(where, 3 - self.bits)
            return own if keep else 1 - own

        def in_came(i, where):
            return 2 * line_at(i, where) + which(where)

        def in_values(i, where):
            return self._spot(line_at(i, where), self._own(where, self.bits), which(where))

        width = sum(item[2] for item in self.values)
        groups = []
        start = 0
        for array, number, wide in self.values:
            items = [(array, number, in_values), (self.came, start, in_came)]
            if last:
                items.append((self.came_last, start, line_at))
            groups.append((wide, items, None))
            start += 1
        return groups

    def turn(self):
        return add_blocks(
            self._groups(False, lambda i, where: i, False), self.height, self.lines, BF,
            self.where, "plane_turn",
        )

    def groups(self, line_at):
        return self._groups(True, line_at, True)


class LineSums:
    def __init__(self, parts, order, lines, height, where, apart=()):
        self.parts, self.order, self.lines, self.apart = parts, order, lines, apart
        self.height, self.where = height, where
        self.steps, self.final, self.names = {}, {}, []
        self.sent = None

    def _step(self, names, overs, kind):
        groups = []
        for name in names:
            back = self.steps[name] + 1

            def line_at(i, spots, back=back):
                return lax.rem(spots[1] - back + 2 * self.lines, self.lines)

            over = overs.get(name)
            start = 0
            for width, items, _ in self.parts[name](line_at):
                groups.append((width, items, None if over is None else (over[0], over[1] + start)))
                start += width
        return add_blocks(groups, self.height, 1, kind, self.where, "line_step")

    def _send(self, names, overs):
        self.names = names
        self.sent = self._step(names, overs, BF) if names else None

    def start(self, *names):
        for name in names:
            self.steps[name] = 0
        self._send(list(names), {})

    def run(self, count, *new):
        for number in range(count):
            joining = list(new) if number + 1 == count else []
            overs = {}
            if self.names:
                came = self.order(next_line(self.sent))
                start = 0
                for name in self.names:
                    overs[name] = (came, start)
                    start += sum(width for width, _, _ in self.parts[name](None))
                    self.steps[name] += 1
                    if self.steps[name] + 1 == self.lines:
                        if name in self.apart:
                            self.final[name] = overs[name]
                        else:
                            self.final[name] = self._step([name], overs, F32)
            staying = [name for name in self.names if name not in self.final]
            for name in joining:
                self.steps[name] = 0
            if staying or joining or self.names:
                self._send(staying + joining, overs)


def member_pieces(parts, where, lines, height):
    def member(k, spots):
        bit_0 = lax.rem(spots[0] + k % 2, 2)
        return bit_0 + 2 * lax.rem(spots[0] // 2 + k // 2, 2)

    total = sum(item[3] for item in parts)
    if height % 32:
        done = []
        for k in range(GROUP):
            columns = []
            for array, came, number, width in parts:
                block = pick(array[:, :width].reshape(lines, GROUP, height, width), where[1])
                other = came[:, number * width : (number + 1) * width]
                block = block.astype(F32) + other.reshape(GROUP, height, width).astype(F32)
                columns.append(pick(block, member(k, where)))
            done.append(jnp.concatenate(columns, axis=1).astype(BF))
        return done

    def body(where_ref, *refs):
        count = len(parts)
        array_refs, came_refs = refs[:count], refs[count : 2 * count]
        out_refs = refs[2 * count : 2 * count + GROUP]
        helds, sems = refs[2 * count + GROUP : -1], refs[-1]
        rows = GROUP * height
        start = pl.multiple_of(where_ref[1] * rows, rows)
        copies = []
        for i, (_, _, number, width) in enumerate(parts):
            copies += [
                pltpu.make_async_copy(
                    array_refs[i].at[pl.ds(start, rows), :width], helds[2 * i], sems.at[2 * i]
                ),
                pltpu.make_async_copy(
                    came_refs[i].at[:, number * width : (number + 1) * width],
                    helds[2 * i + 1], sems.at[2 * i + 1],
                ),
            ]
        run_copies(copies)
        for k, out_ref in enumerate(out_refs):
            spot = pl.ds(pl.multiple_of(member(k, where_ref) * height, height), height)
            at = 0
            for i, (_, _, _, width) in enumerate(parts):
                term = helds[2 * i][spot, :].astype(F32) + helds[2 * i + 1][spot, :].astype(F32)
                out_ref[:, at : at + width] = term.astype(BF)
                at += width

    vmem, any_ref = pl.BlockSpec(memory_space=pltpu.VMEM), pl.BlockSpec(memory_space=pl.ANY)
    held = [pltpu.VMEM((GROUP * height, width), BF) for *_, width in parts for _ in range(2)]
    return list(
        pl.pallas_call(
            body,
            out_shape=(jax.ShapeDtypeStruct((height, total), BF),) * GROUP,
            in_specs=[pl.BlockSpec(memory_space=pltpu.SMEM)] + [any_ref] * (2 * len(parts)),
            out_specs=(vmem,) * GROUP,
            scratch_shapes=held + [pltpu.SemaphoreType.DMA((2 * len(parts),))],
            compiler_params=pltpu.CompilerParams(vmem_limit_bytes=VMEM),
            cost_estimate=SMALL,
            name="member_pieces",
        )(where, *[item[0] for item in parts], *[item[1] for item in parts])
    )


def sum_in_order(pieces, place, count):
    rows, width = pieces[0].shape

    def body(place_ref, *refs):
        out_ref, held = refs[-2:]
        for k in range(count):
            spot = 0
            bit = 1
            while bit < count:
                own = lax.rem(place_ref[0] // bit, 2)
                spot = spot + bit * (1 - own if k & bit else own)
                bit *= 2
            held[spot] = refs[k][...]
        total = held[0]
        for number in range(1, count):
            total = total + held[number]
        out_ref[...] = total

    vmem = pl.BlockSpec(memory_space=pltpu.VMEM)
    return pl.pallas_call(
        body,
        out_shape=jax.ShapeDtypeStruct((rows, width), F32),
        in_specs=[pl.BlockSpec(memory_space=pltpu.SMEM)] + [vmem] * count,
        out_specs=vmem,
        scratch_shapes=[pltpu.VMEM((count, rows, width), F32)],
        compiler_params=pltpu.CompilerParams(vmem_limit_bytes=VMEM),
        cost_estimate=SMALL,
        name="sum_in_order",
    )(place, *pieces)


def gathered_call(body, tile, row_args, fixed_args, matrices, shift, outs, name):
    depth = sum(part.shape[0] * part.shape[1] for part in matrices[0][0][:4])
    widths = [parts[0].shape[2] for parts, _, _ in matrices]
    counts = [len(parts) for parts, _, _ in matrices]
    targets = matrices[0][2]
    rows = row_args[0].shape[0]
    steps = rows // tile
    row_count, fixed_count = len(row_args), len(fixed_args)

    def whole(*refs):
        order_ref = refs[0]
        at = 2
        row_refs = refs[at : at + row_count]
        at += row_count
        fixed_refs = refs[at : at + fixed_count]
        at += fixed_count
        part_refs = refs[at : at + sum(counts)]
        at += sum(counts)
        out_refs = refs[at : at + len(outs)]
        held, sems = refs[-2], refs[-1]

        @pl.when(pl.program_id(0) == 0)
        def _():
            copies = []
            used = base = 0
            for number, (count, width) in enumerate(zip(counts, widths)):
                copies += load_pieces(
                    order_ref, part_refs[used : used + count], matrices[number][1], held, base,
                    sems.at[number],
                )
                used += count
                base += width
            run_copies(copies)

        body(row_refs, fixed_refs, held, out_refs, pl.program_id(0))

    def rows_map(i, order_ref, shift_ref):
        return (lax.rem(i + shift_ref[0], steps), 0)

    def fixed_map(i, order_ref, shift_ref):
        return (0, 0)

    def low_map(i, order_ref, shift_ref):
        return (jnp.minimum(i, steps // 2 - 1), 0)

    def high_map(i, order_ref, shift_ref):
        return (jnp.maximum(i - steps // 2, 0), 0)

    maps = {"rows": rows_map, "low": low_map, "high": high_map}

    def out_spec(shape, kind):
        if kind == "one":
            return pl.BlockSpec(shape, fixed_map)
        return pl.BlockSpec((tile, shape[1]), maps[kind])

    return pl.pallas_call(
        whole,
        grid_spec=pltpu.PrefetchScalarGridSpec(
            num_scalar_prefetch=2,
            grid=(steps,),
            in_specs=[pl.BlockSpec((tile, arg.shape[1]), rows_map) for arg in row_args]
            + [pl.BlockSpec(arg.shape, fixed_map) for arg in fixed_args]
            + [pl.BlockSpec(memory_space=pl.ANY)] * sum(counts),
            out_specs=tuple(out_spec(shape, kind) for shape, _, kind in outs),
            scratch_shapes=[
                pltpu.VMEM((depth, sum(widths)), BF),
                pltpu.SemaphoreType.DMA((len(matrices), targets.shape[0])),
            ],
        ),
        out_shape=tuple(jax.ShapeDtypeStruct(shape, kind) for shape, kind, _ in outs),
        compiler_params=pltpu.CompilerParams(
            dimension_semantics=("arbitrary",), vmem_limit_bytes=VMEM
        ),
        cost_estimate=SMALL,
        name=name,
    )(targets, shift, *row_args, *fixed_args, *[part for parts, _, _ in matrices for part in parts])


NO_SHIFT = (0,)


def inner_product(normed, matrix, small):
    rows, depth = normed.shape
    width = matrix[0][0].shape[2]

    def body(row_refs, fixed_refs, held, out_refs, number):
        out_refs[0][...] = nn(row_refs[0][...], held[...])

        @pl.when(number == 0)
        def _():
            out_refs[1][...] = held[:, small : small + LANES]

    return gathered_call(
        body, 256, [normed], [], [matrix], jnp.array(NO_SHIFT, jnp.int32),
        [((rows, width), F32, "rows"), ((depth, LANES), BF, "one")], "inner_product",
    )


def gate_product(normed, y, matrix):
    rows, width = y.shape

    def body(row_refs, fixed_refs, held, out_refs, number):
        gate = nn(row_refs[0][...], held[...])
        out_refs[0][...] = gate
        gated = row_refs[1][...] * gate * sigmoid(gate)
        total = jnp.sum(gated * gated, axis=1, keepdims=True)
        out_refs[1][...] = jnp.broadcast_to(total, out_refs[1].shape)

    return gathered_call(
        body, 256, [normed, y], [], [matrix], jnp.array(NO_SHIFT, jnp.int32),
        [((rows, width), F32, "rows"), ((rows, LANES), F32, "rows")], "gate_product",
    )


def row_scales(squares_ref, others_ref, width):
    return lax.rsqrt((squares_ref[:, 0:1] + others_ref[:, 0:1]) / width + EPS)


def split_rows(value, number, steps, low_ref, high_ref):
    @pl.when(number < steps // 2)
    def _():
        low_ref[...] = value.astype(BF)

    @pl.when(number >= steps // 2)
    def _():
        high_ref[...] = value


def mixed_product(y, gate, squares, others, kern, matrix, shift, inner_all):
    rows, width = y.shape
    depth = sum(part.shape[0] * part.shape[1] for part in matrix[0][:4])
    tile = 256

    def body(row_refs, fixed_refs, held, out_refs, number):
        gate_now = row_refs[1][...]
        scale = row_scales(row_refs[2], row_refs[3], inner_all)
        scaled = row_refs[0][...] * gate_now * sigmoid(gate_now) * scale
        scaled = (scaled * fixed_refs[0][6:7, :width]).astype(BF)
        out_refs[0][...] = scaled
        mixed = nt(scaled, held[...])
        split_rows(mixed, number, rows // tile, out_refs[1], out_refs[2])

    return gathered_call(
        body, tile, [y, gate, squares, others], [kern], [matrix], shift,
        [
            ((rows, width), BF, "rows"), ((rows // 2, depth), BF, "low"),
            ((rows // 2, depth), F32, "high"),
        ],
        "mixed_product",
    )


def gate_back(d_mix, y, gate, squares, others, pulls, kern, matrix, cut_at, inner_all):
    rows, width = y.shape

    def body(row_refs, fixed_refs, held, out_refs, number):
        d_scaled = nn(row_refs[0][...], held[...])
        y_now, gate_now = row_refs[1][...], row_refs[2][...]
        scale = row_scales(row_refs[3], row_refs[4], inner_all)
        pull = scale * scale * row_refs[5][:, 0:1] / inner_all
        sig = sigmoid(gate_now)
        silu = gate_now * sig
        gated = y_now * silu
        scaled_in = d_scaled * scale
        d_gated = scaled_in * fixed_refs[0][6:7, :width] - gated * pull

        @pl.when(number == 0)
        def _():
            out_refs[3][...] = jnp.zeros(out_refs[3].shape, F32)

        out_refs[3][0:1, :] += jnp.sum(scaled_in * gated, axis=0, keepdims=True)
        out_refs[0][...] = d_gated * silu
        d_gate = (d_gated * y_now * sig * (1.0 + gate_now * (1.0 - sig))).astype(BF)
        out_refs[1][...] = d_gate[:, :cut_at]
        out_refs[2][...] = d_gate[:, cut_at:]

    return gathered_call(
        body, 256, [d_mix, y, gate, squares, others, pulls], [kern], [matrix],
        jnp.array(NO_SHIFT, jnp.int32),
        [
            ((rows, width), F32, "rows"), ((rows, cut_at), BF, "rows"),
            ((rows, width - cut_at), BF, "rows"), ((8, width), F32, "one"),
        ],
        "gate_back",
    )


def normed_back(grads, matrices, shift):
    rows = grads[0].shape[0]
    widths = [grad.shape[1] for grad in grads]
    depth = sum(part.shape[0] * part.shape[1] for part in matrices[0][0][:4])
    tile = 256

    def body(row_refs, fixed_refs, held, out_refs, number):
        total = None
        start = 0
        for ref, width in zip(row_refs, widths):
            term = nt(ref[...], held[:, start : start + width])
            total = term if total is None else total + term
            start += width
        split_rows(total, number, rows // tile, out_refs[0], out_refs[1])

    return gathered_call(
        body, tile, grads, [], matrices, shift,
        [((rows // 2, depth), BF, "low"), ((rows // 2, depth), F32, "high")], "normed_back",
    )


def rows_call(body, tile, row_args, fixed_args, outs, name):
    arrays = [arg if isinstance(arg, tuple) else (arg, None) for arg in row_args]
    rows = arrays[0][0].shape[-2]

    def spec(array, number):
        if number is None:
            return pl.BlockSpec((tile, array.shape[1]), lambda i: (i, 0))
        return pl.BlockSpec((None, tile, array.shape[2]), lambda i: (number, i, 0))

    return pl.pallas_call(
        body,
        grid=(rows // tile,),
        out_shape=tuple(jax.ShapeDtypeStruct(shape, kind) for shape, kind, _ in outs),
        in_specs=[spec(*item) for item in arrays]
        + [pl.BlockSpec(arg.shape, lambda i: (0, 0)) for arg in fixed_args],
        out_specs=tuple(
            pl.BlockSpec(shape, lambda i: (0, 0))
            if one
            else pl.BlockSpec((tile, shape[1]), lambda i: (i, 0))
            for shape, _, one in outs
        ),
        compiler_params=pltpu.CompilerParams(
            dimension_semantics=("arbitrary",), vmem_limit_bytes=VMEM
        ),
        cost_estimate=SMALL,
        name=name,
    )(*[array for array, _ in arrays], *fixed_args)


def columns_call(body, row_args, outs, name):
    arrays = [arg if isinstance(arg, tuple) else (arg, None) for arg in row_args]
    width = arrays[0][0].shape[-1]
    tile = width // 2

    def spec(array, number):
        if number is None:
            return pl.BlockSpec((array.shape[0], tile), lambda i: (0, i))
        return pl.BlockSpec((None, array.shape[1], tile), lambda i: (number, 0, i))

    return pl.pallas_call(
        body,
        grid=(width // tile,),
        out_shape=tuple(jax.ShapeDtypeStruct(shape, BF) for shape in outs),
        in_specs=[spec(*item) for item in arrays],
        out_specs=tuple(pl.BlockSpec((shape[0], tile), lambda i: (0, i)) for shape in outs),
        compiler_params=pltpu.CompilerParams(
            dimension_semantics=("arbitrary",), vmem_limit_bytes=VMEM
        ),
        cost_estimate=SMALL,
        name=name,
    )(*[array for array, _ in arrays])


def normed_rows(tokens, others, gain, core):
    rows, width = tokens.shape
    tile = 128

    def body(core_ref, mine_ref, other_ref, gain_ref, out_ref):
        for ref, spot in ((mine_ref, core_ref[0]), (other_ref, 1 - core_ref[0])):
            values = ref[...].astype(F32)
            out_ref[spot] = (values * norm_rows(values) * gain_ref[...]).astype(BF)

    by_rows = pl.BlockSpec((tile, width), lambda i: (i, 0))
    return pl.pallas_call(
        body,
        grid=(rows // tile,),
        out_shape=jax.ShapeDtypeStruct((2, rows, width), BF),
        in_specs=[
            pl.BlockSpec(memory_space=pltpu.SMEM), by_rows, by_rows,
            pl.BlockSpec((1, width), lambda i: (0, 0)),
        ],
        out_specs=pl.BlockSpec((2, tile, width), lambda i: (0, i, 0)),
        compiler_params=pltpu.CompilerParams(
            dimension_semantics=("arbitrary",), vmem_limit_bytes=VMEM
        ),
        cost_estimate=SMALL,
        name="normed_rows",
    )(core, tokens, others, gain).reshape(2 * rows, width)


def marked_rows(grad_out, routes, core, first_lane):
    rows, width = grad_out.shape
    tile = 256

    def body(core_ref, grad_ref, routes_ref, out_ref):
        out_ref[:, :width] = grad_ref[...]
        lane = lax.broadcasted_iota(jnp.int32, (tile, LANES), 1)
        start = pl.multiple_of(core_ref[0] * rows + pl.program_id(0) * tile, tile)
        named = routes_ref[pl.ds(start, tile), :]
        marks = jnp.zeros(lane.shape, F32)
        for number in range(routes_ref.shape[1]):
            marks = jnp.where(lane == named[:, number : number + 1] + first_lane, 1.0, marks)
        out_ref[:, width:] = marks.astype(BF)

    return pl.pallas_call(
        body,
        grid=(rows // tile,),
        out_shape=jax.ShapeDtypeStruct((rows, width + LANES), BF),
        in_specs=[
            pl.BlockSpec(memory_space=pltpu.SMEM),
            pl.BlockSpec((tile, width), lambda i: (i, 0)),
            pl.BlockSpec(routes.shape, lambda i: (0, 0)),
        ],
        out_specs=pl.BlockSpec((tile, width + LANES), lambda i: (i, 0)),
        compiler_params=pltpu.CompilerParams(
            dimension_semantics=("arbitrary",), vmem_limit_bytes=VMEM
        ),
        cost_estimate=SMALL,
        name="marked_rows",
    )(core, grad_out, routes)


def prepare_params(conv_w, conv_b, norm_gain, d_skip, dt_bias, a_log, core, local, heads):
    wide = conv_w.shape[1]
    both = norm_gain.shape[1]

    def body(core_ref, w_ref, b_ref, gain_ref, skip_ref, bias_ref, log_ref, kern_ref, head_ref, spread_ref):
        row = lax.broadcasted_iota(jnp.int32, (LANES, local), 0)
        column = lax.broadcasted_iota(jnp.int32, (LANES, local), 1)
        head = jnp.where(row >= LANES // 2, row - LANES // 2, row)
        low = head * P_SIZE
        spread = jnp.where((column >= low) & (column < low + P_SIZE), 1.0, 0.0).astype(BF)
        spread_ref[...] = spread
        first = core_ref[0] == 0

        def mine(ref):
            return jnp.where(first, ref[:, :heads], ref[:, heads : 2 * heads])

        kern_ref[...] = jnp.zeros(kern_ref.shape, F32)
        spot = pl.ds(pl.multiple_of(core_ref[0] * local, LANES), local)
        kern_ref[0:4, :local] = w_ref[:, spot]
        kern_ref[0:4, local + LANES :] = w_ref[:, both:]
        kern_ref[4:5, :local] = b_ref[:, spot]
        kern_ref[4:5, local + LANES :] = b_ref[:, both:]
        head_ref[...] = jnp.zeros(head_ref.shape, F32)
        head_ref[2:3, :heads] = mine(skip_ref)
        kern_ref[5:6, :local] = spread_heads(head_ref[...], spread)[2:3]
        kern_ref[6:7, :local] = gain_ref[:, spot]
        head_ref[0:1, :heads] = mine(bias_ref)
        head_ref[1:2, :heads] = jnp.exp(mine(log_ref))

    return small_call(
        body,
        [((8, local + LANES + wide - both), F32), ((8, LANES), F32), ((LANES, local), BF)],
        [core, conv_w, conv_b, norm_gain, d_skip, dt_bias, a_log], "prepare_params", 1,
    )


def mid_rows_of(mixed, others, tokens, gain):
    rows, width = tokens.shape

    def body(mixed_ref, other_ref, tokens_ref, gain_ref, resid_ref, mid_ref):
        resid = tokens_ref[...].astype(F32) + mixed_ref[...] + other_ref[...].astype(F32)
        resid_ref[...] = resid
        mid_ref[...] = (resid * norm_rows(resid) * gain_ref[...]).astype(BF)

    return rows_call(
        body, 256, [mixed, others, tokens], [gain],
        [((rows, width), F32, False), ((rows, width), BF, False)], "mid_rows",
    )


def across_sum(mine, came, number):
    _, rows, width = mine.shape
    cut = rows // 2

    def body(mine_ref, came_ref, low_ref, high_ref):
        total = (mine_ref[...].astype(F32) + came_ref[...].astype(F32)).astype(BF)
        low_ref[...] = total[:cut]
        high_ref[...] = total[cut:]

    return columns_call(
        body, [(mine, number), (came, number)], [(cut, width)] * 2, "across_sum"
    )


def side_sums(mine, came, over_x, over_y):
    _, rows, width = mine.shape
    cut = rows // 2

    def body(mine_x, came_x, mine_y, came_y, over_x_ref, over_y_ref, x_ref, y_ref):
        to_x = mine_x[...].astype(F32) + came_x[...].astype(F32)
        x_ref[:cut] = to_x[:cut].astype(BF)
        x_ref[cut:] = (to_x[cut:] + over_y_ref[...].astype(F32)).astype(BF)
        to_y = mine_y[...].astype(F32) + came_y[...].astype(F32)
        y_ref[:cut] = (to_y[:cut] + over_x_ref[...].astype(F32)).astype(BF)
        y_ref[cut:] = to_y[cut:].astype(BF)

    return columns_call(
        body, [(mine, 0), (came, 0), (mine, 1), (came, 1), over_x, over_y],
        [(rows, width)] * 2, "side_sums",
    )


def own_sum(mine_ref, came_ref, x_ref, y_ref):
    return (
        mine_ref[...].astype(F32) + came_ref[...].astype(F32)
        + x_ref[...].astype(F32) + y_ref[...].astype(F32)
    )


def norm_back(d_rows, values, gain, grad_ref):
    scale = norm_rows(values)

    @pl.when(pl.program_id(0) == 0)
    def _():
        grad_ref[...] = jnp.zeros(grad_ref.shape, F32)

    grad_ref[0:1, :] += jnp.sum(d_rows * values * scale, axis=0, keepdims=True)
    pulled = d_rows * gain
    mean = jnp.mean(values * pulled, axis=-1, keepdims=True)
    return scale * pulled - values * (scale * scale * scale) * mean


def resid_back(mine, came, from_x, from_y, resid, tokens, grad_out, gain):
    rows, width = tokens.shape

    def body(
        mine_ref, came_ref, x_ref, y_ref, resid_ref, tokens_ref, grad_ref, gain_ref,
        d_resid_ref, d_mix_ref, pulls_ref, gain_grad_ref,
    ):
        resid_now = resid_ref[...]
        d_mid = own_sum(mine_ref, came_ref, x_ref, y_ref)
        d_extra = norm_back(d_mid, resid_now, gain_ref[...], gain_grad_ref)
        d_resid = grad_ref[...].astype(F32) + d_extra
        d_resid_ref[...] = d_resid
        d_mix = d_resid.astype(BF)
        d_mix_ref[...] = d_mix
        mixed = resid_now - tokens_ref[...].astype(F32)
        pull = jnp.sum(d_mix.astype(F32) * mixed, axis=1, keepdims=True)
        pulls_ref[...] = jnp.broadcast_to(pull, pulls_ref.shape)

    return rows_call(
        body, 256, [(mine, 0), (came, 0), from_x, from_y, resid, tokens, grad_out], [gain],
        [
            ((rows, width), F32, False), ((rows, width), BF, False),
            ((rows, LANES), F32, False), ((8, width), F32, True),
        ],
        "resid_back",
    )


def output_rows(mine, came, from_x, from_y, resid):
    def body(mine_ref, came_ref, x_ref, y_ref, resid_ref, out_ref):
        out_ref[...] = (resid_ref[...] + own_sum(mine_ref, came_ref, x_ref, y_ref)).astype(BF)

    return rows_call(
        body, 256, [(mine, 0), (came, 0), from_x, from_y, resid], [], [(resid.shape, BF, False)],
        "output_rows",
    )[0]


def tokens_back(mine, came, tokens, d_resid, gain):
    rows, width = tokens.shape

    def body(mine_ref, came_ref, tokens_ref, d_resid_ref, gain_ref, out_ref, gain_grad_ref):
        d_rows = mine_ref[...] + came_ref[...].astype(F32)
        d_extra = norm_back(d_rows, tokens_ref[...].astype(F32), gain_ref[...], gain_grad_ref)
        out_ref[...] = (d_resid_ref[...] + d_extra).astype(BF)

    return rows_call(
        body, 256, [mine, came, tokens, d_resid], [gain],
        [((rows, width), BF, False), ((8, width), F32, True)], "tokens_back",
    )


def pack_small(par_grads, head_grads, gain_grads, mid_gains, in_gains, spread, core, local, heads):
    width_d = in_gains.shape[1]
    both = 2 * local
    rest = par_grads.shape[1] - local - LANES

    def body(core_ref, par_ref, head_ref, gain_ref, mid_ref, in_ref, spread_ref, out_ref):
        out_ref[...] = jnp.zeros(out_ref.shape, F32)
        spot = pl.ds(pl.multiple_of(core_ref[0] * local, LANES), local)
        out_ref[0:5, spot] = par_ref[0:5, :local]
        out_ref[0:5, both:] = par_ref[0:5, local + LANES :]
        out_ref[5:6, spot] = gain_ref[0:1, :]
        out_ref[6:7, :width_d] = in_ref[0:1, :]
        out_ref[6:7, width_d : 2 * width_d] = mid_ref[0:1, :]
        lane = lax.broadcasted_iota(jnp.int32, (8, LANES), 1)
        skip = gather_heads(par_ref[:, :local], spread_ref[...], lane < heads)
        for number, row in enumerate((head_ref[0:1], head_ref[1:2], skip[5:6])):
            start = pl.multiple_of((2 * number + core_ref[0]) * LANES, LANES)
            out_ref[7:8, pl.ds(start, LANES)] = row

    return small_call(
        body, [((8, both + rest), F32)],
        [core, par_grads, head_grads, gain_grads, mid_gains, in_gains, spread], "pack_small", 1,
    )[0]


def out_outputs(og_sums, cut):
    height = og_sums.shape[0]

    def body(sums_ref, out_ref):
        out_ref[:cut, :] = sums_ref[:, :cut].T
        out_ref[cut:, :] = sums_ref[:, 2 * cut : 3 * cut].T

    return small_call(body, [((2 * cut, height), F32)], [og_sums], "out_outputs")[0]


def inner_outputs(og_sums, in_sums, core, local, heads, cut):
    height = in_sums.shape[0]
    half = height // 2
    if height % 32:
        gate = jnp.concatenate([og_sums[:, cut : 2 * cut], og_sums[:, 3 * cut :]], axis=1)
        joint = in_sums[:, local:].reshape(2, half, -1)
        return (
            jnp.stack([gate, in_sums[:, :local]], axis=1), in_sums[:, local : local + heads],
            pick(joint, core[0]), pick(joint, 1 - core[0]),
        )

    def body(core_ref, og_ref, in_ref, zx_ref, dt_ref, mine_ref, sent_ref):
        zx_ref[:, 0, :cut] = og_ref[:, cut : 2 * cut]
        zx_ref[:, 0, cut:] = og_ref[:, 3 * cut :]
        zx_ref[:, 1, :] = in_ref[:, :local]
        dt_ref[...] = in_ref[:, local : local + heads]
        for ref, spot in ((mine_ref, core_ref[0]), (sent_ref, 1 - core_ref[0])):
            ref[...] = in_ref[pl.ds(pl.multiple_of(spot * half, half), half), local:]

    rest = in_sums.shape[1] - local
    return small_call(
        body,
        [
            ((height, 2, local), F32), ((height, heads), F32), ((half, rest), F32),
            ((half, rest), F32),
        ],
        [core, og_sums, in_sums], "inner_outputs", 1,
    )


def unpack_experts(came, place, units, shared_units):
    height, width = came[0].shape
    hidden = width // 3
    own = EXPERTS // GROUP

    def body(place_ref, *refs):
        came_refs, (gu_ref, down_ref, sgu_ref, sdown_ref) = refs[:GROUP], refs[GROUP:]
        for k in range(GROUP):
            bit_0 = lax.rem(place_ref[0] + k % 2, 2)
            bit_1 = lax.rem(place_ref[0] // 2 + k // 2, 2)
            member = bit_0 + 2 * bit_1
            for e in range(own):
                expert = member * own + e
                for j in range(2):
                    start = j * hidden + e * units
                    gu_ref[expert, :, j, :] = came_refs[k][:, start : start + units].astype(F32)
                start = 2 * hidden + e * units
                down_ref[expert] = came_refs[k][:, start : start + units].astype(F32).T
            spot = pl.ds(pl.multiple_of(member * shared_units, shared_units), shared_units)
            for j in range(2):
                start = j * hidden + own * units
                sgu_ref[:, j, spot] = came_refs[k][:, start : start + shared_units].astype(F32)
            start = 2 * hidden + own * units
            sdown_ref[spot, :] = came_refs[k][:, start : start + shared_units].astype(F32).T

    return pl.pallas_call(
        body,
        out_shape=(
            jax.ShapeDtypeStruct((EXPERTS, height, 2, units), F32),
            jax.ShapeDtypeStruct((EXPERTS, units, height), F32),
            jax.ShapeDtypeStruct((height, 2, GROUP * shared_units), F32),
            jax.ShapeDtypeStruct((GROUP * shared_units, height), F32),
        ),
        in_specs=[pl.BlockSpec(memory_space=pltpu.SMEM)]
        + [pl.BlockSpec(memory_space=pltpu.VMEM)] * GROUP,
        out_specs=(pl.BlockSpec(memory_space=pltpu.VMEM),) * 4,
        compiler_params=pltpu.CompilerParams(vmem_limit_bytes=VMEM),
        cost_estimate=SMALL,
        name="unpack_experts",
    )(place, *came)


def expert_body(plan, *refs):
    own, units, shared, counts, part_count, aliased = plan
    hidden = own * units + shared
    refs = list(refs)

    def take(number):
        out = refs[:number]
        del refs[:number]
        return out

    order_ref, base_ref = take(2)
    x_pieces = [take(number) for number in counts]
    ym_pieces = [take(number) for number in counts]
    count = len(counts)
    (router_ref,) = take(1)
    part_refs = take(part_count)
    take(aliased)
    x_out, dy_out, gate_ref, up_ref, down_ref = take(5)
    out_mine, out_other, dx_mine, dx_other = take(4)
    w, sems, x_held, ym_held, row_sems = refs
    step = pl.program_id(0)
    width = router_ref.shape[0]

    def fetch(number):
        slot = number % 2
        copies = []
        for which, (parts, target) in enumerate(
            ((x_pieces[number], x_held), (ym_pieces[number], ym_held))
        ):
            start = 0
            for half, ref in enumerate(parts):
                rows = ref.shape[0]
                copies.append(
                    pltpu.make_async_copy(
                        ref, target.at[slot, start : start + rows], row_sems.at[which, slot, half]
                    )
                )
                start += rows
        return copies

    @pl.when(step == 0)
    def _():
        loads = load_pieces(order_ref, part_refs, [0] * part_count, w, 0, sems)
        for copy in fetch(0) + loads:
            copy.start()
        for copy in loads:
            copy.wait()

    for number in range(count):

        @pl.when(step == number)
        def _():
            if number + 1 < count:
                for copy in fetch(number + 1):
                    copy.start()
            for copy in fetch(number):
                copy.wait()

    slot = lax.rem(step, 2)
    x_now, ym_now = x_held.at[slot], ym_held.at[slot]
    x_out[...] = x_now[...]
    dy_out[...] = ym_now[:, :width]
    tile = x_now.shape[0]
    lane = lax.broadcasted_iota(jnp.int32, (tile, LANES), 1)
    routed = ym_now[:, width:].astype(F32) > 0.5
    logits = nn(x_now[...], router_ref[...])
    top = jnp.max(jnp.where(routed, logits, -1e30), axis=1, keepdims=True)
    powers = jnp.where(routed, jnp.exp(jnp.where(routed, logits - top, 0.0)), 0.0)
    gates = powers / jnp.sum(powers, axis=1, keepdims=True)
    d_gates = jnp.zeros((tile, LANES), F32)
    parts = [(e * units, units, e) for e in range(own)] + [(own * units, shared, None)]
    for start, size, expert in parts:
        cols = [slice(k * hidden + start, k * hidden + start + size) for k in range(3)]
        pre = nn(x_now[...], w[:, cols[0]])
        up = nn(x_now[...], w[:, cols[1]])
        d_act = nn(ym_now[:, :width], w[:, cols[2]])
        sig = sigmoid(pre)
        silu = pre * sig
        act = (silu * up).astype(BF).astype(F32)
        if expert is not None:
            here = lane == base_ref[0] + expert
            gate = jnp.sum(jnp.where(here, gates, 0.0), axis=1, keepdims=True)
            d_gate = jnp.sum(act * d_act, axis=1, keepdims=True)
            d_gates = jnp.where(here, d_gate, d_gates)
            d_act = d_act * gate
            act = act * gate
        gate_ref[:, cols[0]] = (d_act * up * sig * (1.0 + pre * (1.0 - sig))).astype(BF)
        up_ref[:, cols[0]] = (d_act * silu).astype(BF)
        down_ref[:, start : start + size] = act.astype(BF)
    mean = jnp.sum(gates * d_gates, axis=1, keepdims=True)
    d_logits = (gates * (d_gates - mean)).astype(BF)
    up_ref[:, hidden:] = d_logits
    cut = 256

    def results(out_ref, dx_ref):
        for number in range(width // cut):
            rows = slice(number * cut, (number + 1) * cut)
            out_ref[0, :, rows] = nt(down_ref[...], w[rows, 2 * hidden :]).astype(BF)
            d_x = nt(gate_ref[...], w[rows, :hidden])
            d_x = d_x + nt(up_ref[:, :hidden], w[rows, hidden : 2 * hidden])
            dx_ref[0, :, rows] = (d_x + nt(d_logits, router_ref[rows, :])).astype(BF)

    @pl.when(slot == 0)
    def _():
        results(out_mine, dx_mine)

    @pl.when(slot == 1)
    def _():
        results(out_other, dx_other)


def expert_rows(members, x_pieces, ym_pieces, held, base, router, parts, targets, units, shared):
    low, count = members[0], len(members)
    width = router.shape[0]
    x_pieces = [item if isinstance(item, tuple) else (item,) for item in x_pieces]
    ym_pieces = [item if isinstance(item, tuple) else (item,) for item in ym_pieces]
    tile = sum(part.shape[0] for part in x_pieces[0])
    counts = [len(item) for item in x_pieces]
    rows = 2 * GROUP * tile
    steps = 2 * count
    own = EXPERTS // GROUP
    hidden = own * units + shared

    def like(columns):
        spec = pl.BlockSpec((tile, columns), lambda i: (i + 2 * low, 0))
        return jax.ShapeDtypeStruct((rows, columns), BF), spec

    result = (
        jax.ShapeDtypeStruct((count, tile, width), BF),
        pl.BlockSpec((1, tile, width), lambda i: (i // 2, 0, 0)),
    )
    outs = [like(columns) for columns in (width, width, hidden, hidden + LANES, hidden)]
    outs += [result] * 4
    any_ref = pl.BlockSpec(memory_space=pl.ANY)
    flat = [part for item in x_pieces + ym_pieces for part in item]
    args = [targets, base, *flat, router, *parts, *held]
    specs = [pl.BlockSpec(memory_space=pltpu.SMEM)] * 2 + [any_ref] * len(flat)
    specs += [pl.BlockSpec(router.shape, lambda i: (0, 0))]
    specs += [any_ref] * (len(parts) + len(held))
    aliases = {len(args) - len(held) + i: i for i in range(len(held))}
    done = pl.pallas_call(
        functools.partial(
            expert_body, (own, units, shared, counts, len(parts), len(held))
        ),
        grid=(steps,),
        out_shape=tuple(shape for shape, _ in outs),
        in_specs=specs,
        out_specs=tuple(spec for _, spec in outs),
        scratch_shapes=[
            pltpu.VMEM((width, 3 * hidden), BF), pltpu.SemaphoreType.DMA((targets.shape[0],)),
            pltpu.VMEM((2, tile, width), BF), pltpu.VMEM((2, tile, width + LANES), BF),
            pltpu.SemaphoreType.DMA((2, 2, 2)),
        ],
        input_output_aliases=aliases,
        compiler_params=pltpu.CompilerParams(
            dimension_semantics=("arbitrary",), vmem_limit_bytes=VMEM
        ),
        cost_estimate=SMALL,
        name="expert_rows",
    )(*args)
    return list(done[:5]), list(done[5:])


def shards(
    tokens, routes, gain_in, w_zx, w_dt, w_bc, conv_w, conv_b, dt_bias, a_log, d_skip, norm_gain,
    w_out, gain_mid, router, shared_gu, shared_down, expert_gu, expert_down, grad_out,
):
    core = lax.axis_index("tensor")
    me = lax.axis_index("dp")
    lines = lax.axis_size("dp") // GROUP
    line, place = me // GROUP, lax.rem(me, GROUP)
    piece, width_d = tokens.shape
    local = w_zx.shape[2]
    heads = w_dt.shape[1]
    units = expert_gu.shape[3]
    own = EXPERTS // GROUP
    inner_all = norm_gain.shape[0]
    height = w_zx.shape[0]
    cut_in, cut_gate = 2 * local // 3, local // 2
    third = (lines - 1 + 2) // 3
    place_now = place.reshape(1)
    where = jnp.stack([place, line]).astype(jnp.int32)
    base = (heads + own * place).reshape(1)
    tiles = 4
    mine_last = (tiles // 2 * (1 - core)).reshape(1).astype(jnp.int32)

    lines_back = lax.rem(line - jnp.arange(lines, dtype=jnp.int32) + lines, lines)
    members = place ^ jnp.arange(GROUP, dtype=jnp.int32)
    pieces = jnp.concatenate([members, members[3:]])
    mixer_targets = (pieces[:, None] + GROUP * lines_back[None, :]).reshape(-1)
    expert_targets = (members[None, :] + GROUP * lines_back[:, None]).reshape(-1)
    order = Order()

    core_now = core.reshape(1)
    gain_in, gain_mid, conv_b, norm_gain = gain_in[None], gain_mid[None], conv_b[None], norm_gain[None]
    d_skip, dt_bias, a_log = d_skip[None], dt_bias[None], a_log[None]
    joint = jnp.concatenate([w_bc, router], axis=1)
    joint_came = swap(joint)
    ring_a = [w_zx[:, 1, :cut_in]]
    tokens_other = swap(tokens)
    order.set(ring_a[0], joint)
    joint = in_order(joint, order(joint_came), core)
    bc_cols, router_cols = joint[:, : 2 * NS], joint[:, 2 * NS :]
    pad = jnp.zeros((height, LANES - heads - EXPERTS), BF)
    ring_b = [jnp.concatenate([w_zx[:, 1, cut_in:], w_dt, router_cols, pad, bc_cols], axis=1)]
    order.set(ring_b[0])
    shared_units = shared_gu.shape[2] // GROUP
    hidden = own * units + shared_units
    gu = order(expert_gu).reshape(GROUP, own, height, 2, units).transpose(0, 2, 3, 1, 4)
    gu = gu.reshape(GROUP, height, 2, own * units)
    order.set(
        gu, gain_in, gain_mid, where, base, mine_last, place_now, core_now, mixer_targets,
        expert_targets,
    )
    ring_on(ring_a, order, 1, 1 + third, lines)
    ring_on(ring_b, order, 1, 1 + third, lines)
    order.set(ring_a[-1], ring_b[-1])
    down = order(expert_down).reshape(GROUP, own, units, height).transpose(0, 3, 1, 2)
    down = down.reshape(GROUP, height, own * units)
    sgu = order(shared_gu).reshape(height, 2, GROUP, shared_units).transpose(2, 0, 1, 3)
    sdown = order(shared_down).reshape(GROUP, shared_units, height).transpose(0, 2, 1)
    order.set(down, sgu, sdown)
    ring_on(ring_a, order, 1 + third, 1 + 2 * third, lines)
    ring_on(ring_b, order, 1 + third, 1 + 2 * third, lines)
    order.set(ring_a[-1], ring_b[-1])
    gu, sgu, down, sdown = order((gu, sgu, down, sdown))
    packed = jnp.concatenate([gu[:, :, 0], sgu[:, :, 0], gu[:, :, 1], sgu[:, :, 1], down, sdown], axis=2)
    to_send = [pick(packed, members[k]) for k in range(GROUP)]
    order.set(*to_send)
    came = to_send[:1] + [hop(to_send[k], k) for k in range(1, GROUP)]
    go_block = order(jnp.concatenate([w_zx[:, 0], w_out.T], axis=1))
    order.set(go_block)
    ring_on(ring_a, order, 1 + 2 * third, lines, lines)
    ring_on(ring_b, order, 1 + 2 * third, lines, lines)
    order.set(ring_a[-1], ring_b[-1])

    def matrix(parts, cut_at):
        return pieces_of(parts, mixer_targets, cut_at)

    def along_both(stacked):
        return [stacked, hop(stacked, 1), hop(stacked, 2)]

    def across_halves(parts, cut_at):
        width = parts[0].shape[2]
        low, high = cut_columns(parts[1], 0, cut_at), cut_columns(parts[2], cut_at, width - cut_at)
        order.set(low, high)
        return parts + [hop(low, 2), hop(high, 1)]

    go_ring = [order(go_block)]
    tokens_other = order.take(tokens_other)
    in_stack = stack_pairs(ring_a, ring_b)
    order.set(in_stack)
    ring_on(go_ring, order, 1, 1 + third, lines)
    order.set(go_ring[-1])
    came = order.take(*came)
    ring_on(go_ring, order, 1 + third, 1 + 2 * third, lines)
    order.set(go_ring[-1])
    in_w = along_both(order(in_stack))
    expert_ring = [stack_columns(order(came), 0, 3 * hidden)]
    marked = marked_rows(order(grad_out), routes, core_now, heads)
    normed = normed_rows(order(tokens), tokens_other, gain_in, core_now)
    kern, head_par, spread = prepare_params(
        order(conv_w), conv_b, norm_gain, d_skip, dt_bias, a_log, core_now, local, heads
    )
    order.set(normed, marked, expert_ring[0], kern)
    ring_on(go_ring, order, 1 + 2 * third, lines, lines)
    order.set(go_ring[-1])
    expert_ring[0] = order(expert_ring[0])
    in_w = list(order.take(*in_w))
    in_w = across_halves(in_w, cut_in)
    marked_other = order.take(swap(order(marked)))
    gate_stack = stack_columns(order(go_ring), 0, local)
    in_w = order.take(*in_w, gate_stack)
    gate_stack, in_w = in_w[-1], list(in_w[:-1])

    gate_w = along_both(gate_stack)
    in_matrix = matrix(in_w, cut_in)
    zi, router_w = inner_product(order(normed), in_matrix, local)
    order.set(zi)
    ring_on(expert_ring, order, 1, 1 + third, lines)
    order.set(expert_ring[-1])
    y, states = front_scan(order(zi), kern, head_par, spread)
    order.set(y)
    gate_w = list(order.take(*gate_w))
    gate_w = across_halves(gate_w, cut_gate)
    out_stack = stack_columns(order(go_ring), local, width_d)
    order.set(out_stack)
    gate_w = list(order.take(*gate_w))
    out_w = along_both(order(out_stack))
    gate_matrix = matrix(gate_w, cut_gate)
    gate, squares = gate_product(order(normed), y, gate_matrix)
    order.set(gate)
    squares_other = order.take(swap(squares))
    out_w = list(order.take(*out_w))
    ring_on(expert_ring, order, 1 + third, 1 + 2 * third, lines)
    order.set(expert_ring[-1])
    out_w = across_halves(out_w, cut_gate)
    out_w = list(order.take(*out_w))
    marked_sent = order(marked)
    marked_x, marked_y = hop(marked_sent, 1), hop(marked_sent, 2)
    out_matrix = matrix(out_w, cut_gate)
    scaled, mixed_sent, mixed_mine = mixed_product(
        order(y), gate, squares, squares_other, kern, out_matrix, mine_last, inner_all
    )
    order.set(mixed_mine)
    marked_x, marked_y = order.take(marked_x, marked_y)
    half_rows = piece // 2

    def halves_of(from_x, from_y):
        return cut_rows_of(from_x, 0, half_rows), cut_rows_of(from_y, half_rows, half_rows)

    def across(halves):
        return hop(halves[0], 2), hop(halves[1], 1)

    marked_halves = halves_of(marked_x, marked_y)
    order.set(*marked_halves)
    ring_on(expert_ring, order, 1 + 2 * third, lines, lines)
    order.set(expert_ring[-1])
    mixed_came = order.take(swap(order(mixed_sent)))
    resid, mid = mid_rows_of(mixed_mine, mixed_came, tokens, gain_mid)
    order.set(mid)

    mid_x, mid_y = hop(mid, 1), hop(mid, 2)
    mid_other = order.take(swap(mid))
    marked_swap_x, marked_swap_y = swap(order(marked_x)), swap(order(marked_y))
    parts, _, expert_order = pieces_of(expert_ring, expert_targets, 0)
    common = (base, router_w, parts, expert_order, units, shared_units)
    kept, result_0 = expert_rows(
        [0], [order(mid), mid_other], [marked, marked_other], [], *common
    )
    order.set(result_0[0])
    mid_x, mid_y, marked_swap_x, marked_swap_y = order.take(
        mid_x, mid_y, marked_swap_x, marked_swap_y
    )
    mid_halves = halves_of(mid_x, mid_y)
    order.set(*mid_halves)
    mid_swap_x, mid_swap_y = order.take(swap(mid_x), swap(mid_y))
    mid_d, marked_d = across(order(mid_halves)), across(order(marked_halves))
    kept, result = expert_rows(
        [1, 2], order([mid_x, mid_swap_x, mid_y, mid_swap_y]),
        [marked_x, marked_swap_x, marked_y, marked_swap_y], kept, *common,
    )
    order.set(result[0])
    mid_d = order.take(*mid_d)
    marked_d = order.take(*marked_d)
    mid_d_other = order.take(*[swap(item) for item in mid_d])
    marked_d_other = order.take(*[swap(item) for item in marked_d])
    d_others, d_other_0 = swap(order(result[3])), swap(order(result_0[3]))
    kept, result_3 = expert_rows(
        [3], [order(mid_d), mid_d_other], [marked_d, marked_d_other], kept, *common
    )
    order.set(result_3[0])
    x_all, dy_all, gate_acts, up_acts, down = kept
    d_others, d_other_0 = order.take(d_others, d_other_0)
    d_other_3 = order.take(swap(result_3[3]))
    over_low, over_high = across_sum(result_3[2], d_other_3, 0)
    order.set(over_low)
    d_over = hop(over_low, 1), hop(over_high, 2)
    out_others = swap(order(result_3[1])), swap(order(result[1])), swap(order(result_0[1]))

    grad_down = tn(order(dy_all), down, BF)
    order.set(grad_down)
    d_over = order.take(*d_over)
    out_other_3, out_others, out_other_0 = order.take(*out_others)
    to_x, to_y = side_sums(result[2], d_others, *d_over)
    order.set(to_x)
    arrays = {}

    def whole_block(name, width):
        return lambda line_at: [(width, [(arrays[name], 0, line_at)], None)]

    sums = LineSums(
        {name: whole_block(name, hidden) for name in ("gate", "up", "down")},
        order, lines, GROUP * height, where, ("gate", "up", "down"),
    )
    arrays["down"] = grad_down
    sums.start("down")
    d_came = hop(to_x, 1), hop(to_y, 2)
    out_over = across_sum(result_3[0], order(out_other_3), 0)
    order.set(out_over[0], sums.sent)
    out_over = hop(out_over[0], 1), hop(out_over[1], 2)
    arrays["gate"] = tn(order(x_all), gate_acts, BF)
    order.set(arrays["gate"])
    sums.run(third, "gate")
    order.set(sums.sent)
    arrays["up"] = tn(order(x_all), up_acts, BF)
    order.set(arrays["up"])
    d_came = order.take(*d_came)
    out_over = order.take(*out_over)
    out_sums = side_sums(result[0], out_others, *out_over)
    order.set(out_sums[0])
    out_came = hop(out_sums[0], 1), hop(out_sums[1], 2)

    d_resid, d_mix_mine, pulls, mid_gains = resid_back(
        result_0[2], d_other_0, *d_came, order(resid), tokens, grad_out, gain_mid
    )
    order.set(d_mix_mine)
    sums.run(third, "up")
    order.set(sums.sent)
    d_mix_came, pulls_came = order.take(swap(d_mix_mine), swap(pulls))
    d_mix, pulls = pair_rows([(d_mix_mine, order(d_mix_came)), (pulls, pulls_came)], core_now)
    order.set(d_mix)
    d_y, dz_a, dz_b, gain_grads = gate_back(
        order(d_mix), y, gate, squares, squares_other, pulls, kern, out_matrix, cut_gate, inner_all
    )
    order.set(d_y)

    def hop_first(pair, *before):
        sent = [item.start(order) for item in pair]
        order.set(*sent)
        for other in before:
            all_came(other)
        for item, values in zip(pair, sent):
            item.came = hop(order(values), item.bits)

    def hop_second(pair):
        for item in pair:
            item.came = order(item.came)
        sent = [item.turn() for item in pair]
        order.set(*sent)
        for item, values in zip(pair, sent):
            item.came_last = hop(values, 3 - item.bits)

    def all_came(pair):
        for item in pair:
            item.came_last = order(item.came_last)
        order.set(*[item.came_last for item in pair])

    grad_out_w = tn(order(d_mix), scaled, BF)
    normed_now = order(normed)
    grad_gate_a, grad_gate_b = tn(normed_now, dz_a, BF), tn(normed_now, dz_b, BF)
    order.set(grad_gate_a, grad_gate_b, grad_out_w)
    out_came = order.take(*out_came)
    og_pair = [
        Plane([(grad_out_w, 0, cut_gate), (grad_gate_a, 0, cut_gate)], 1, where, lines),
        Plane([(grad_out_w, 1, cut_gate), (grad_gate_b, 0, cut_gate)], 2, where, lines),
    ]
    hop_first(og_pair)
    output = output_rows(order(result_0[0]), out_other_0, *out_came, resid)
    order.set(output)
    sums.run(third)
    order.set(sums.sent)
    di_a, di_b, par_grads, head_grads = back_scan(
        order(d_y), zi, states, kern, head_par, spread, cut_in
    )
    order.set(di_a)
    hop_second(og_pair)
    grad_in_a = tn(order(normed), di_a, BF)
    start = local - cut_in
    grad_router = jnp.pad(
        order(arrays["up"][:, hidden:]).astype(F32),
        ((0, 0), (start, di_b.shape[1] - start - LANES)),
    )
    grad_in_b = (tn(order(normed), di_b) + grad_router).astype(BF)
    order.set(grad_in_a, grad_in_b)
    sums.run(third)
    order.set(sums.sent)
    in_pair = [
        Plane([(grad_in_a, 0, cut_in)], 1, where, lines),
        Plane([(grad_in_b, 0, grad_in_b.shape[1])], 2, where, lines),
    ]
    hop_first(in_pair, og_pair)

    def pair_groups(pair):
        return lambda line_at: [group for item in pair for group in item.groups(line_at)]

    rest = LineSums(
        {"og": pair_groups(og_pair), "in": pair_groups(in_pair)}, order, lines, height, where
    )
    rest.start("og")
    order.set(rest.sent)
    d_sent, d_mine = normed_back(
        order([dz_a, dz_b, di_a, di_b]), [gate_matrix, in_matrix], mine_last
    )
    order.set(d_mine)

    hop_second(in_pair)
    sums.run(third)
    order.set(sums.final["up"][0])
    rest.run(third)
    order.set(rest.sent)
    d_other = order.take(swap(order(d_sent)))
    grad_tokens, in_gains = tokens_back(d_mine, d_other, tokens, d_resid, gain_in)
    order.set(grad_tokens)
    small = pack_small(
        par_grads, head_grads, gain_grads, mid_gains, in_gains, spread, core_now, local, heads
    )
    order.set(small)
    all_came(in_pair)
    rest.run(third, "in")
    order.set(rest.sent)
    to_send = member_pieces(
        [
            (arrays[name], order(sums.final[name][0]), sums.final[name][1] // hidden, hidden)
            for name in ("gate", "up", "down")
        ],
        where, lines, height,
    )
    order.set(*to_send)
    came = to_send[:1] + [hop(order(to_send[k]), k) for k in range(1, GROUP)]
    small = sum_in_order([small, order(swap(small))], core_now, 2)
    order.set(small)
    small = sum_in_order([small] + order([hop(small, k) for k in range(1, GROUP)]), place_now, GROUP)
    order.set(small)
    bits = GROUP
    while bits < lines * GROUP:
        if 2 * bits < lines * GROUP:
            others = order([hop(small, k * bits) for k in range(1, 4)])
            small = sum_in_order([small] + others, (me // bits).reshape(1), 4)
            bits *= 4
        else:
            small = sum_in_order([small, order(hop(small, bits))], (me // bits).reshape(1), 2)
            bits *= 2
        order.set(small)
    rest.run(third)
    order.set(rest.sent)
    came = list(order.take(*came))
    g_egu, g_edown, g_sgu, g_sdown = unpack_experts(came, place_now, units, shared_units)
    order.set(g_edown)
    rest.run(third)
    order.set(rest.sent)
    g_out = out_outputs(order(rest.final["og"]), cut_gate)
    order.set(g_out)
    rest.run(third)
    order.set(rest.final["in"])
    g_zx, g_dt, joint_mine, joint_sent = inner_outputs(
        rest.final["og"], rest.final["in"], core_now, local, heads, cut_gate
    )
    joint = joint_mine + swap(joint_sent)
    g_router, g_bc = joint[:, heads : heads + EXPERTS], joint[:, LANES:]

    def of_heads(number):
        return jnp.concatenate(
            [
                small[7, (2 * number + which) * LANES : (2 * number + which) * LANES + heads]
                for which in range(2)
            ]
        )

    return (
        output, grad_tokens, small[6, :width_d], g_zx, g_dt, g_bc, small[:4],
        small[4], of_heads(0), of_heads(1), of_heads(2), small[5, :inner_all], g_out,
        small[6, width_d : 2 * width_d], g_router, g_sgu, g_sdown, g_egu, g_edown,
    )


def solution(mesh):
    both = P(("dp", "tensor"), None)
    rows = P("dp", None, "tensor")
    cols = P("tensor", "dp")
    return jax.shard_map(
        shards,
        mesh=mesh,
        in_specs=(
            both, P("dp", None), P(), rows, P("dp", "tensor"), both, P(), P(), P(), P(), P(), P(),
            cols, P(), both, rows, cols, P(None, "dp", None, "tensor"), P(None, "tensor", "dp"),
            both,
        ),
        out_specs=(
            both, both, P(), rows, P("dp", "tensor"), both, P(), P(), P(), P(), P(), P(),
            cols, P(), both, rows, cols, P(None, "dp", None, "tensor"), P(None, "tensor", "dp"),
        ),
        check_vma=False,
    )
```

```python
import functools

import jax
import jax.numpy as jnp
from jax import lax
from jax.experimental import pallas as pl
from jax.experimental.pallas import tpu as pltpu
from jax.sharding import PartitionSpec as P

F32 = jnp.float32
BF = jnp.bfloat16
EPS = 1e-05
H = 48
P_SIZE = 64
NS = 128
EXPERTS = 16
BL = 128
GROUP = 4
LANES = 128
VMEM = 60 * 1024 * 1024
SMALL = pl.CostEstimate(flops=1000, bytes_accessed=1000, transcendentals=0)
highest = lax.Precision.HIGHEST


def nn(left, right):
    return lax.dot_general(left, right, (((1,), (0,)), ((), ())), preferred_element_type=F32)


def nt(left, right):
    return lax.dot_general(left, right, (((1,), (1,)), ((), ())), preferred_element_type=F32)


def tn(left, right, kind=F32):
    return lax.dot_general(left, right, (((0,), (0,)), ((), ())), preferred_element_type=kind)


def hop(values, bits):
    count = lax.axis_size("dp")
    return lax.ppermute(values, "dp", [(i, i ^ bits) for i in range(count)])


def next_line(values):
    count = lax.axis_size("dp")
    return lax.ppermute(values, "dp", [(i, (i + GROUP) % count) for i in range(count)])


def swap(values):
    return lax.ppermute(values, "tensor", [(0, 1), (1, 0)])


def pick(values, index, axis=0):
    return lax.dynamic_index_in_dim(values, index, axis, keepdims=False)


def in_order(mine, theirs, core):
    return jnp.where(
        core == 0, jnp.concatenate([mine, theirs]), jnp.concatenate([theirs, mine])
    )


def tie(values, *others):
    flat, tree = jax.tree.flatten(values)
    held = lax.optimization_barrier((flat, others))
    return jax.tree.unflatten(tree, held[0])


class Order:
    def __init__(self):
        self.marks = self.last = ()

    def __call__(self, values):
        return tie(values, *self.marks)

    def set(self, *marks):
        self.marks, self.last = marks + self.last, marks

    def take(self, *values):
        values = self(values)
        self.set(*values)
        return values if len(values) > 1 else values[0]


def ring_on(blocks, order, low, high, lines):
    for _ in range(low, min(high, lines)):
        blocks.append(order(next_line(blocks[-1])))


def pieces_of(parts, targets, cut):
    inner, height, width = parts[0].shape
    starts = [0] * len(parts)
    if cut:
        starts[-1] = cut
    if height % 32 == 0:
        return parts, starts, targets
    if cut:
        parts = parts[:3] + [jnp.concatenate(parts[3:], axis=-1)]
    flat = jnp.concatenate(parts)
    total = flat.shape[0]
    source = jnp.zeros((total,), jnp.int32)
    source = source.at[targets[:total]].set(jnp.arange(total, dtype=jnp.int32))
    whole = flat[source].reshape(1, total * height, width)
    return [whole], [0], jnp.zeros((1,), jnp.int32)


def load_pieces(target_ref, part_refs, starts, held, base, sems):
    copies = []
    for ref, start in zip(part_refs, starts):
        inner, height, width = ref.shape
        for j in range(inner):
            row = pl.multiple_of(target_ref[len(copies)] * height, height)
            copies.append(
                pltpu.make_async_copy(
                    ref.at[j],
                    held.at[pl.ds(row, height), base + start : base + start + width],
                    sems.at[len(copies)],
                )
            )
    return copies


def run_copies(copies):
    for copy in copies:
        copy.start()
    for copy in copies:
        copy.wait()


def norm_rows(values):
    return lax.rsqrt(jnp.mean(values * values, axis=-1, keepdims=True) + EPS)


def sigmoid(values):
    return 1.0 / (1.0 + jnp.exp(-values))


def split_two(values):
    high = values.astype(BF)
    return high, (values - high.astype(F32)).astype(BF)


def spread_heads(values, spread):
    high, low = split_two(values)
    packed = high.astype(F32) + pltpu.roll(low.astype(F32), LANES // 2, 1)
    return nn(packed.astype(BF), spread)


def gather_heads(values, spread, heads_on):
    high, low = split_two(values)
    return jnp.where(heads_on, nt(high, spread) + nt(low, spread), 0.0)


def conv_rows(ext, kern, low, high, offset):
    summed = kern[4:5, low:high]
    for j in range(4):
        summed = summed + kern[j : j + 1, low:high] * ext[offset + j : offset + j + BL, low:high]
    return summed


def step_terms(raw, head_par, heads_on):
    shifted = raw + head_par[0:1]
    soft = jnp.maximum(shifted, 0.0) + jnp.log1p(jnp.exp(-jnp.abs(shifted)))
    step = jnp.where(heads_on, soft, 0.0)
    return shifted, step, -step * head_par[1:2]


def front_body(zi_ref, kern_ref, head_ref, spread_ref, y_ref, state_ref, ext, state):
    width = y_ref.shape[1]
    first = pl.program_id(0) == 0

    @pl.when(first)
    def _():
        ext[0:8, :] = jnp.zeros((8, ext.shape[1]), F32)
        state[...] = jnp.zeros(state.shape, F32)

    @pl.when(jnp.logical_not(first))
    def _():
        ext[0:8, :] = ext[BL : BL + 8, :]

    ext[8 : BL + 8, :] = zi_ref[...]
    rows = lax.broadcasted_iota(jnp.int32, (BL, LANES), 0)
    cols = lax.broadcasted_iota(jnp.int32, (BL, LANES), 1)
    causal = cols <= rows
    heads_on = cols < width // P_SIZE
    spread = spread_ref[...]
    state_ref[0] = state[...]
    pre = conv_rows(ext, kern_ref, 0, width, 5)
    x = pre * sigmoid(pre)
    pre = conv_rows(ext, kern_ref, width + LANES, ext.shape[1], 5)
    maps = pre * sigmoid(pre)
    b, c = maps[:, :NS], maps[:, NS:]
    shifted, step, decay = step_terms(zi_ref[:, width : width + LANES], head_ref, heads_on)
    cum = jnp.dot(causal.astype(F32), decay, precision=highest, preferred_element_type=F32)
    cum_t = cum.T
    last = cum[BL - 1 : BL]
    scores = nt(c.astype(BF), b.astype(BF))
    u = x * spread_heads(step, spread)
    from_start = spread_heads(jnp.where(heads_on, jnp.exp(cum), 0.0), spread)
    to_end = spread_heads(jnp.where(heads_on, jnp.exp(last - cum), 0.0), spread)
    u_low = u.astype(BF)
    left = cols < P_SIZE
    within = []
    for pair in range(width // LANES):
        mats = []
        for head in (2 * pair, 2 * pair + 1):
            gap = cum[:, head : head + 1] - cum_t[head : head + 1, :]
            mats.append((jnp.where(causal, jnp.exp(gap), 0.0) * scores).astype(BF))
        cut = u_low[:, pair * LANES : (pair + 1) * LANES]
        zero = jnp.zeros_like(cut)
        stacked = jnp.concatenate([jnp.where(left, cut, zero), jnp.where(left, zero, cut)], axis=0)
        within.append(nn(jnp.concatenate(mats, axis=1), stacked))
    before = state[...]
    across = nn(c.astype(BF), before.astype(BF)) * from_start
    y_ref[...] = jnp.concatenate(within, axis=1) + across + kern_ref[5:6, :width] * x
    grown = nn(b.T.astype(BF), (u * to_end).astype(BF))
    state[...] = before * from_start[BL - 1 : BL] + grown


def front_scan(zi, kern, head_par, spread):
    length, width = zi.shape[0], spread.shape[1]
    steps = length // BL
    return pl.pallas_call(
        front_body,
        grid=(steps,),
        out_shape=(
            jax.ShapeDtypeStruct((length, width), F32),
            jax.ShapeDtypeStruct((steps, NS, width), F32),
        ),
        in_specs=[
            pl.BlockSpec((BL, zi.shape[1]), lambda i: (i, 0)),
            pl.BlockSpec(kern.shape, lambda i: (0, 0)),
            pl.BlockSpec(head_par.shape, lambda i: (0, 0)),
            pl.BlockSpec(spread.shape, lambda i: (0, 0)),
        ],
        out_specs=(
            pl.BlockSpec((BL, width), lambda i: (i, 0)),
            pl.BlockSpec((1, NS, width), lambda i: (i, 0, 0)),
        ),
        scratch_shapes=[pltpu.VMEM((BL + 8, zi.shape[1]), F32), pltpu.VMEM((NS, width), F32)],
        compiler_params=pltpu.CompilerParams(
            dimension_semantics=("arbitrary",), vmem_limit_bytes=VMEM
        ),
        cost_estimate=SMALL,
        name="front_scan",
    )(zi, kern, head_par, spread)


def back_body(
    dy_ref, zi_ref, prev_ref, state_ref, kern_ref, head_ref, spread_ref,
    dia_ref, dib_ref, par_ref, hg_ref, ext, ext_d, d_state,
):
    width = dy_ref.shape[1]
    wide = zi_ref.shape[1]
    cut_at = dia_ref.shape[1]
    number = pl.program_id(0)
    steps = pl.num_programs(0)

    @pl.when(number == 0)
    def _():
        ext_d[BL : BL + 8, :] = jnp.zeros((8, wide), F32)
        d_state[...] = jnp.zeros(d_state.shape, F32)
        par_ref[...] = jnp.zeros(par_ref.shape, F32)
        hg_ref[...] = jnp.zeros(hg_ref.shape, F32)

    @pl.when(number > 0)
    def _():
        ext_d[BL : BL + 8, :] = ext_d[0:8, :]

    ext[0:8, :] = jnp.where(number == steps - 1, 0.0, prev_ref[...])
    ext[8 : BL + 8, :] = zi_ref[...]
    rows = lax.broadcasted_iota(jnp.int32, (BL, LANES), 0)
    cols = lax.broadcasted_iota(jnp.int32, (BL, LANES), 1)
    upper = rows <= cols
    strict = rows < cols
    heads_on = cols < width // P_SIZE
    left = cols < P_SIZE
    spread = spread_ref[...]
    pre_x = conv_rows(ext, kern_ref, 0, width, 5)
    sig_x = sigmoid(pre_x)
    x = pre_x * sig_x
    pre_m = conv_rows(ext, kern_ref, width + LANES, wide, 5)
    sig_m = sigmoid(pre_m)
    maps = pre_m * sig_m
    b, c = maps[:, :NS], maps[:, NS:]
    b_low, c_low = b.astype(BF), c.astype(BF)
    shifted, step, decay = step_terms(zi_ref[:, width : width + LANES], head_ref, heads_on)
    cum = jnp.dot(
        (cols <= rows).astype(F32), decay, precision=highest, preferred_element_type=F32
    )
    cum_t = cum.T
    last = cum[BL - 1 : BL]
    step_wide = spread_heads(step, spread)
    from_start = spread_heads(jnp.where(heads_on, jnp.exp(cum), 0.0), spread)
    to_end = spread_heads(jnp.where(heads_on, jnp.exp(last - cum), 0.0), spread)
    whole = from_start[BL - 1 : BL]
    d_y = dy_ref[...]
    par_ref[5:6, :width] += jnp.sum(d_y * x, axis=0, keepdims=True)
    u = x * step_wide
    u_low, dy_low = u.astype(BF), d_y.astype(BF)
    scores_t = nt(b_low, c_low)
    d_scores_t = jnp.zeros((BL, BL), F32)
    du_parts = []
    gap_rows = jnp.zeros((BL, LANES), F32)
    gap_cols = []
    for pair in range(width // LANES):
        lanes = slice(pair * LANES, (pair + 1) * LANES)
        cut_u, cut_d = u_low[:, lanes], dy_low[:, lanes]
        zero = jnp.zeros_like(cut_u)
        stack_u = jnp.concatenate([jnp.where(left, cut_u, zero), jnp.where(left, zero, cut_u)], axis=0)
        stack_d = jnp.concatenate([jnp.where(left, cut_d, zero), jnp.where(left, zero, cut_d)], axis=0)
        d_weights = nt(stack_u, cut_d)
        mats = []
        for place, head in enumerate((2 * pair, 2 * pair + 1)):
            gap = cum_t[head : head + 1, :] - cum[:, head : head + 1]
            decays = jnp.where(upper, jnp.exp(gap), 0.0)
            weight = decays * scores_t
            mats.append(weight.astype(BF))
            d_weight = d_weights[place * BL : (place + 1) * BL]
            d_scores_t = d_scores_t + decays * d_weight
            moved = jnp.where(strict, weight * d_weight, 0.0)
            gap_rows = jnp.where(cols == head, jnp.sum(moved, axis=1, keepdims=True), gap_rows)
            gap_cols.append(jnp.sum(moved, axis=0, keepdims=True))
        du_parts.append(nn(jnp.concatenate(mats, axis=1), stack_d))
    gap_cols.append(jnp.zeros((LANES - width // P_SIZE, BL), F32))
    gap_cols = jnp.concatenate(gap_cols, axis=0).T
    before, d_after = state_ref[0], d_state[...]
    before_low, d_after_low = before.astype(BF), d_after.astype(BF)
    dy_start = d_y * from_start
    dy_start_low = dy_start.astype(BF)
    reach = gather_heads(dy_start * nn(c_low, before_low), spread, heads_on)
    u_end = u * to_end
    d_from_state = nn(b_low, d_after_low)
    kept = gather_heads(u_end * d_from_state, spread, heads_on)
    carried = jnp.sum(before * d_after, axis=0, keepdims=True) * whole
    carried = gather_heads(jnp.broadcast_to(carried, (8, width)), spread, heads_on[:8])[0:1]
    d_c = nt(dy_start_low, before_low) + nn(d_scores_t.T.astype(BF), b_low)
    d_b = nt(u_end.astype(BF), d_after_low) + nn(d_scores_t.astype(BF), c_low)
    d_state[...] = d_after * whole + nn(c.T.astype(BF), dy_start_low)
    d_u = jnp.concatenate(du_parts, axis=1) + to_end * d_from_state
    d_decay = (
        jnp.dot(
            upper.astype(F32), reach + gap_cols - gap_rows, precision=highest,
            preferred_element_type=F32,
        )
        + jnp.dot(
            (cols < rows).astype(F32), kept, precision=highest, preferred_element_type=F32
        )
        + carried
    )
    d_step = gather_heads(x * d_u, spread, heads_on)
    rate = head_ref[1:2]
    d_raw = jnp.where(heads_on, (d_step - rate * d_decay) * sigmoid(shifted), 0.0)
    hg_ref[0:1, :] += jnp.sum(d_raw, axis=0, keepdims=True)
    hg_ref[1:2, :] += jnp.sum(jnp.where(heads_on, d_decay * decay, 0.0), axis=0, keepdims=True)
    d_x = step_wide * d_u + kern_ref[5:6, :width] * d_y
    ext_d[0:BL, :width] = d_x * sig_x * (1.0 + pre_x * (1.0 - sig_x))
    ext_d[0:BL, width : width + LANES] = jnp.zeros((BL, LANES), F32)
    ext_d[0:BL, width + LANES :] = (
        jnp.concatenate([d_b, d_c], axis=1) * sig_m * (1.0 + pre_m * (1.0 - sig_m))
    )
    for low, high in ((0, cut_at), (cut_at, width), (width + LANES, wide)):
        d_act = ext_d[0:BL, low:high]
        d_in = jnp.zeros((BL, high - low), F32)
        for j in range(4):
            d_in = d_in + kern_ref[j : j + 1, low:high] * ext_d[3 - j : 3 - j + BL, low:high]
            par_ref[j : j + 1, low:high] += jnp.sum(
                d_act * ext[5 + j : 5 + j + BL, low:high], axis=0, keepdims=True
            )
        par_ref[4:5, low:high] += jnp.sum(d_act, axis=0, keepdims=True)
        if low < cut_at:
            dia_ref[...] = d_in.astype(BF)
        else:
            dib_ref[:, low - cut_at : high - cut_at] = d_in.astype(BF)
    dib_ref[:, width - cut_at : width - cut_at + LANES] = d_raw.astype(BF)


def back_scan(d_y, zi, states, kern, head_par, spread, cut_at):
    length, width = d_y.shape
    wide = zi.shape[1]
    steps = length // BL
    per = BL // 8

    def back(i):
        return (steps - 1 - i, 0)

    def fixed(i):
        return (0, 0)

    return pl.pallas_call(
        back_body,
        grid=(steps,),
        out_shape=(
            jax.ShapeDtypeStruct((length, cut_at), BF),
            jax.ShapeDtypeStruct((length, wide - cut_at), BF),
            jax.ShapeDtypeStruct((8, wide), F32),
            jax.ShapeDtypeStruct((8, LANES), F32),
        ),
        in_specs=[
            pl.BlockSpec((BL, width), back),
            pl.BlockSpec((BL, wide), back),
            pl.BlockSpec((8, wide), lambda i: (jnp.maximum((steps - 1 - i) * per - 1, 0), 0)),
            pl.BlockSpec((1, NS, width), lambda i: (steps - 1 - i, 0, 0)),
            pl.BlockSpec(kern.shape, fixed),
            pl.BlockSpec(head_par.shape, fixed),
            pl.BlockSpec(spread.shape, fixed),
        ],
        out_specs=(
            pl.BlockSpec((BL, cut_at), back),
            pl.BlockSpec((BL, wide - cut_at), back),
            pl.BlockSpec((8, wide), fixed),
            pl.BlockSpec((8, LANES), fixed),
        ),
        scratch_shapes=[
            pltpu.VMEM((BL + 8, wide), F32),
            pltpu.VMEM((BL + 8, wide), F32),
            pltpu.VMEM((NS, width), F32),
        ],
        compiler_params=pltpu.CompilerParams(
            dimension_semantics=("arbitrary",), vmem_limit_bytes=VMEM
        ),
        cost_estimate=SMALL,
        name="back_scan",
    )(d_y, zi, zi, states, kern, head_par, spread)


def small_call(body, outs, args, name, scalars=0):
    vmem, smem = pl.BlockSpec(memory_space=pltpu.VMEM), pl.BlockSpec(memory_space=pltpu.SMEM)
    return pl.pallas_call(
        body,
        out_shape=tuple(jax.ShapeDtypeStruct(shape, kind) for shape, kind in outs),
        in_specs=[smem] * scalars + [vmem] * (len(args) - scalars),
        out_specs=tuple(vmem for _ in outs),
        compiler_params=pltpu.CompilerParams(vmem_limit_bytes=VMEM),
        cost_estimate=SMALL,
        name=name,
    )(*args)


def stack_columns(blocks, start, width):
    height = blocks[0].shape[0]

    def body(*refs):
        for number, ref in enumerate(refs[:-1]):
            refs[-1][number] = ref[:, start : start + width]

    shape = (len(blocks), height, width)
    return small_call(body, [(shape, blocks[0].dtype)], blocks, "stack_columns")[0]


def stack_pairs(first, second):
    height, low = first[0].shape
    high = second[0].shape[1]

    def body(*refs):
        for number in range(len(first)):
            refs[-1][number, :, :low] = refs[number][...]
            refs[-1][number, :, low:] = refs[len(first) + number][...]

    shape = (len(first), height, low + high)
    return small_call(body, [(shape, first[0].dtype)], [*first, *second], "stack_pairs")[0]


def cut_columns(values, start, width):
    def body(values_ref, out_ref):
        out_ref[...] = values_ref[:, :, start : start + width]

    return small_call(
        body, [(values.shape[:2] + (width,), values.dtype)], [values], "cut_columns"
    )[0]


def cut_rows_of(values, start, rows):
    def body(values_ref, out_ref):
        out_ref[...] = values_ref[start : start + rows]

    return small_call(body, [((rows, values.shape[1]), values.dtype)], [values], "cut_rows")[0]


def pair_rows(pairs, core):
    def body(core_ref, *refs):
        for number in range(len(pairs)):
            mine_ref, other_ref = refs[2 * number : 2 * number + 2]
            out_ref = refs[2 * len(pairs) + number]
            out_ref[core_ref[0]] = mine_ref[...]
            out_ref[1 - core_ref[0]] = other_ref[...]

    outs = [((2,) + mine.shape, mine.dtype) for mine, _ in pairs]
    args = [core] + [item for pair in pairs for item in pair]
    done = small_call(body, outs, args, "pair_rows", 1)
    return [item.reshape(-1, item.shape[2]) for item in done]


def add_blocks(groups, height, count, kind, where, name):
    total = sum(width for width, _, _ in groups)
    flat = [(width, item) for width, items, _ in groups for item in items]
    overs = []
    for _, _, over in groups:
        if over is not None and not any(over[0] is array for array in overs):
            overs.append(over[0])

    if height % 32:
        columns = []
        for width, items, over in groups:
            term = 0.0
            for array, number, spot in items:
                part = array[:, number * width : (number + 1) * width].reshape(-1, height, width)
                picked = [pick(part, spot(i, where)) for i in range(count)]
                term = term + jnp.concatenate(picked).astype(F32)
            if over is not None:
                term = term + over[0][:, over[1] : over[1] + width].astype(F32)
            columns.append(term)
        return jnp.concatenate(columns, axis=1).astype(kind)

    def body(where_ref, *refs):
        item_refs = refs[: len(flat)]
        over_refs = refs[len(flat) : len(flat) + len(overs)]
        out_ref, sems = refs[len(flat) + len(overs)], refs[-1]
        helds = refs[len(flat) + len(overs) + 1 : -1]
        copies = []
        for row, (ref, held, (width, (_, number, spot))) in enumerate(zip(item_refs, helds, flat)):
            for i in range(count):
                start = pl.multiple_of(spot(i, where_ref) * height, height)
                copies.append(
                    pltpu.make_async_copy(
                        ref.at[pl.ds(start, height), number * width : (number + 1) * width],
                        held.at[i * height : (i + 1) * height],
                        sems.at[row, i],
                    )
                )
        run_copies(copies)
        at = start = 0
        for width, items, over in groups:
            term = helds[at][...]
            if len(items) > 1 or over is not None:
                term = term.astype(F32)
            for held in helds[at + 1 : at + len(items)]:
                term = term + held[...].astype(F32)
            if over is not None:
                (number,) = [i for i, array in enumerate(overs) if array is over[0]]
                term = term + over_refs[number][:, over[1] : over[1] + width].astype(F32)
            out_ref[:, start : start + width] = term.astype(kind)
            at += len(items)
            start += width

    vmem, any_ref = pl.BlockSpec(memory_space=pltpu.VMEM), pl.BlockSpec(memory_space=pl.ANY)
    return pl.pallas_call(
        body,
        out_shape=jax.ShapeDtypeStruct((count * height, total), kind),
        in_specs=[pl.BlockSpec(memory_space=pltpu.SMEM)]
        + [any_ref] * len(flat)
        + [vmem] * len(overs),
        out_specs=vmem,
        scratch_shapes=[
            pltpu.VMEM((count * height, width), item[0].dtype) for width, item in flat
        ]
        + [pltpu.SemaphoreType.DMA((len(flat), count))],
        compiler_params=pltpu.CompilerParams(vmem_limit_bytes=VMEM),
        cost_estimate=SMALL,
        name=name,
    )(where, *[item[0] for _, item in flat], *overs)


class Plane:
    def __init__(self, values, bits, where, lines):
        self.values, self.bits, self.where, self.lines = values, bits, where, lines
        self.height = values[0][0].shape[0] // (lines * GROUP)
        self.came = self.came_last = None

    def _spot(self, i, first, second):
        x, y = (first, second) if self.bits == 1 else (second, first)
        return i * GROUP + y * 2 + x

    def _own(self, where, axis):
        return lax.rem(where[0], 2) if axis == 1 else where[0] // 2

    def start(self, order):
        def spot(i, where):
            return self._spot(i // 2, 1 - self._own(where, self.bits), i % 2)

        groups = [
            (width, [(order(array), number, spot)], None) for array, number, width in self.values
        ]
        return add_blocks(groups, self.height, 2 * self.lines, BF, self.where, "plane_start")

    def _groups(self, keep, line_at, last):
        def which(where):
            own = self._own(where, 3 - self.bits)
            return own if keep else 1 - own

        def in_came(i, where):
            return 2 * line_at(i, where) + which(where)

        def in_values(i, where):
            return self._spot(line_at(i, where), self._own(where, self.bits), which(where))

        width = sum(item[2] for item in self.values)
        groups = []
        start = 0
        for array, number, wide in self.values:
            items = [(array, number, in_values), (self.came, start, in_came)]
            if last:
                items.append((self.came_last, start, line_at))
            groups.append((wide, items, None))
            start += 1
        return groups

    def turn(self):
        return add_blocks(
            self._groups(False, lambda i, where: i, False), self.height, self.lines, BF,
            self.where, "plane_turn",
        )

    def groups(self, line_at):
        return self._groups(True, line_at, True)


class LineSums:
    def __init__(self, parts, order, lines, height, where, apart=()):
        self.parts, self.order, self.lines, self.apart = parts, order, lines, apart
        self.height, self.where = height, where
        self.steps, self.final, self.names = {}, {}, []
        self.sent = None

    def _step(self, names, overs, kind):
        groups = []
        for name in names:
            back = self.steps[name] + 1

            def line_at(i, spots, back=back):
                return lax.rem(spots[1] - back + 2 * self.lines, self.lines)

            over = overs.get(name)
            start = 0
            for width, items, _ in self.parts[name](line_at):
                groups.append((width, items, None if over is None else (over[0], over[1] + start)))
                start += width
        return add_blocks(groups, self.height, 1, kind, self.where, "line_step")

    def _send(self, names, overs):
        self.names = names
        self.sent = self._step(names, overs, BF) if names else None

    def start(self, *names):
        for name in names:
            self.steps[name] = 0
        self._send(list(names), {})

    def run(self, count, *new):
        for number in range(count):
            joining = list(new) if number + 1 == count else []
            overs = {}
            if self.names:
                came = self.order(next_line(self.sent))
                start = 0
                for name in self.names:
                    overs[name] = (came, start)
                    start += sum(width for width, _, _ in self.parts[name](None))
                    self.steps[name] += 1
                    if self.steps[name] + 1 == self.lines:
                        if name in self.apart:
                            self.final[name] = overs[name]
                        else:
                            self.final[name] = self._step([name], overs, F32)
            staying = [name for name in self.names if name not in self.final]
            for name in joining:
                self.steps[name] = 0
            if staying or joining or self.names:
                self._send(staying + joining, overs)


def member_pieces(parts, where, lines, height):
    def member(k, spots):
        bit_0 = lax.rem(spots[0] + k % 2, 2)
        return bit_0 + 2 * lax.rem(spots[0] // 2 + k // 2, 2)

    total = sum(item[3] for item in parts)
    if height % 32:
        done = []
        for k in range(GROUP):
            columns = []
            for array, came, number, width in parts:
                block = pick(array[:, :width].reshape(lines, GROUP, height, width), where[1])
                other = came[:, number * width : (number + 1) * width]
                block = block.astype(F32) + other.reshape(GROUP, height, width).astype(F32)
                columns.append(pick(block, member(k, where)))
            done.append(jnp.concatenate(columns, axis=1).astype(BF))
        return done

    def body(where_ref, *refs):
        count = len(parts)
        array_refs, came_refs = refs[:count], refs[count : 2 * count]
        out_refs = refs[2 * count : 2 * count + GROUP]
        helds, sems = refs[2 * count + GROUP : -1], refs[-1]
        rows = GROUP * height
        start = pl.multiple_of(where_ref[1] * rows, rows)
        copies = []
        for i, (_, _, number, width) in enumerate(parts):
            copies += [
                pltpu.make_async_copy(
                    array_refs[i].at[pl.ds(start, rows), :width], helds[2 * i], sems.at[2 * i]
                ),
                pltpu.make_async_copy(
                    came_refs[i].at[:, number * width : (number + 1) * width],
                    helds[2 * i + 1], sems.at[2 * i + 1],
                ),
            ]
        run_copies(copies)
        for k, out_ref in enumerate(out_refs):
            spot = pl.ds(pl.multiple_of(member(k, where_ref) * height, height), height)
            at = 0
            for i, (_, _, _, width) in enumerate(parts):
                term = helds[2 * i][spot, :].astype(F32) + helds[2 * i + 1][spot, :].astype(F32)
                out_ref[:, at : at + width] = term.astype(BF)
                at += width

    vmem, any_ref = pl.BlockSpec(memory_space=pltpu.VMEM), pl.BlockSpec(memory_space=pl.ANY)
    held = [pltpu.VMEM((GROUP * height, width), BF) for *_, width in parts for _ in range(2)]
    return list(
        pl.pallas_call(
            body,
            out_shape=(jax.ShapeDtypeStruct((height, total), BF),) * GROUP,
            in_specs=[pl.BlockSpec(memory_space=pltpu.SMEM)] + [any_ref] * (2 * len(parts)),
            out_specs=(vmem,) * GROUP,
            scratch_shapes=held + [pltpu.SemaphoreType.DMA((2 * len(parts),))],
            compiler_params=pltpu.CompilerParams(vmem_limit_bytes=VMEM),
            cost_estimate=SMALL,
            name="member_pieces",
        )(where, *[item[0] for item in parts], *[item[1] for item in parts])
    )


def sum_in_order(pieces, place, count):
    rows, width = pieces[0].shape

    def body(place_ref, *refs):
        out_ref, held = refs[-2:]
        for k in range(count):
            spot = 0
            bit = 1
            while bit < count:
                own = lax.rem(place_ref[0] // bit, 2)
                spot = spot + bit * (1 - own if k & bit else own)
                bit *= 2
            held[spot] = refs[k][...]
        total = held[0]
        for number in range(1, count):
            total = total + held[number]
        out_ref[...] = total

    vmem = pl.BlockSpec(memory_space=pltpu.VMEM)
    return pl.pallas_call(
        body,
        out_shape=jax.ShapeDtypeStruct((rows, width), F32),
        in_specs=[pl.BlockSpec(memory_space=pltpu.SMEM)] + [vmem] * count,
        out_specs=vmem,
        scratch_shapes=[pltpu.VMEM((count, rows, width), F32)],
        compiler_params=pltpu.CompilerParams(vmem_limit_bytes=VMEM),
        cost_estimate=SMALL,
        name="sum_in_order",
    )(place, *pieces)


def gathered_call(body, tile, row_args, fixed_args, matrices, shift, outs, name):
    depth = sum(part.shape[0] * part.shape[1] for part in matrices[0][0][:4])
    widths = [parts[0].shape[2] for parts, _, _ in matrices]
    counts = [len(parts) for parts, _, _ in matrices]
    targets = matrices[0][2]
    rows = row_args[0].shape[0]
    steps = rows // tile
    row_count, fixed_count = len(row_args), len(fixed_args)

    def whole(*refs):
        order_ref = refs[0]
        at = 2
        row_refs = refs[at : at + row_count]
        at += row_count
        fixed_refs = refs[at : at + fixed_count]
        at += fixed_count
        part_refs = refs[at : at + sum(counts)]
        at += sum(counts)
        out_refs = refs[at : at + len(outs)]
        held, sems = refs[-2], refs[-1]

        @pl.when(pl.program_id(0) == 0)
        def _():
            copies = []
            used = base = 0
            for number, (count, width) in enumerate(zip(counts, widths)):
                copies += load_pieces(
                    order_ref, part_refs[used : used + count], matrices[number][1], held, base,
                    sems.at[number],
                )
                used += count
                base += width
            run_copies(copies)

        body(row_refs, fixed_refs, held, out_refs, pl.program_id(0))

    def rows_map(i, order_ref, shift_ref):
        return (lax.rem(i + shift_ref[0], steps), 0)

    def fixed_map(i, order_ref, shift_ref):
        return (0, 0)

    def low_map(i, order_ref, shift_ref):
        return (jnp.minimum(i, steps // 2 - 1), 0)

    def high_map(i, order_ref, shift_ref):
        return (jnp.maximum(i - steps // 2, 0), 0)

    maps = {"rows": rows_map, "low": low_map, "high": high_map}

    def out_spec(shape, kind):
        if kind == "one":
            return pl.BlockSpec(shape, fixed_map)
        return pl.BlockSpec((tile, shape[1]), maps[kind])

    return pl.pallas_call(
        whole,
        grid_spec=pltpu.PrefetchScalarGridSpec(
            num_scalar_prefetch=2,
            grid=(steps,),
            in_specs=[pl.BlockSpec((tile, arg.shape[1]), rows_map) for arg in row_args]
            + [pl.BlockSpec(arg.shape, fixed_map) for arg in fixed_args]
            + [pl.BlockSpec(memory_space=pl.ANY)] * sum(counts),
            out_specs=tuple(out_spec(shape, kind) for shape, _, kind in outs),
            scratch_shapes=[
                pltpu.VMEM((depth, sum(widths)), BF),
                pltpu.SemaphoreType.DMA((len(matrices), targets.shape[0])),
            ],
        ),
        out_shape=tuple(jax.ShapeDtypeStruct(shape, kind) for shape, kind, _ in outs),
        compiler_params=pltpu.CompilerParams(
            dimension_semantics=("arbitrary",), vmem_limit_bytes=VMEM
        ),
        cost_estimate=SMALL,
        name=name,
    )(targets, shift, *row_args, *fixed_args, *[part for parts, _, _ in matrices for part in parts])


NO_SHIFT = (0,)


def inner_product(normed, matrix, small):
    rows, depth = normed.shape
    width = matrix[0][0].shape[2]

    def body(row_refs, fixed_refs, held, out_refs, number):
        out_refs[0][...] = nn(row_refs[0][...], held[...])

        @pl.when(number == 0)
        def _():
            out_refs[1][...] = held[:, small : small + LANES]

    return gathered_call(
        body, 256, [normed], [], [matrix], jnp.array(NO_SHIFT, jnp.int32),
        [((rows, width), F32, "rows"), ((depth, LANES), BF, "one")], "inner_product",
    )


def gate_product(normed, y, matrix):
    rows, width = y.shape

    def body(row_refs, fixed_refs, held, out_refs, number):
        gate = nn(row_refs[0][...], held[...])
        out_refs[0][...] = gate
        gated = row_refs[1][...] * gate * sigmoid(gate)
        total = jnp.sum(gated * gated, axis=1, keepdims=True)
        out_refs[1][...] = jnp.broadcast_to(total, out_refs[1].shape)

    return gathered_call(
        body, 256, [normed, y], [], [matrix], jnp.array(NO_SHIFT, jnp.int32),
        [((rows, width), F32, "rows"), ((rows, LANES), F32, "rows")], "gate_product",
    )


def row_scales(squares_ref, others_ref, width):
    return lax.rsqrt((squares_ref[:, 0:1] + others_ref[:, 0:1]) / width + EPS)


def split_rows(value, number, steps, low_ref, high_ref):
    @pl.when(number < steps // 2)
    def _():
        low_ref[...] = value.astype(BF)

    @pl.when(number >= steps // 2)
    def _():
        high_ref[...] = value


def mixed_product(y, gate, squares, others, kern, matrix, shift, inner_all):
    rows, width = y.shape
    depth = sum(part.shape[0] * part.shape[1] for part in matrix[0][:4])
    tile = 256

    def body(row_refs, fixed_refs, held, out_refs, number):
        gate_now = row_refs[1][...]
        scale = row_scales(row_refs[2], row_refs[3], inner_all)
        scaled = row_refs[0][...] * gate_now * sigmoid(gate_now) * scale
        scaled = (scaled * fixed_refs[0][6:7, :width]).astype(BF)
        out_refs[0][...] = scaled
        mixed = nt(scaled, held[...])
        split_rows(mixed, number, rows // tile, out_refs[1], out_refs[2])

    return gathered_call(
        body, tile, [y, gate, squares, others], [kern], [matrix], shift,
        [
            ((rows, width), BF, "rows"), ((rows // 2, depth), BF, "low"),
            ((rows // 2, depth), F32, "high"),
        ],
        "mixed_product",
    )


def gate_back(d_mix, y, gate, squares, others, pulls, kern, matrix, cut_at, inner_all):
    rows, width = y.shape

    def body(row_refs, fixed_refs, held, out_refs, number):
        d_scaled = nn(row_refs[0][...], held[...])
        y_now, gate_now = row_refs[1][...], row_refs[2][...]
        scale = row_scales(row_refs[3], row_refs[4], inner_all)
        pull = scale * scale * row_refs[5][:, 0:1] / inner_all
        sig = sigmoid(gate_now)
        silu = gate_now * sig
        gated = y_now * silu
        scaled_in = d_scaled * scale
        d_gated = scaled_in * fixed_refs[0][6:7, :width] - gated * pull

        @pl.when(number == 0)
        def _():
            out_refs[3][...] = jnp.zeros(out_refs[3].shape, F32)

        out_refs[3][0:1, :] += jnp.sum(scaled_in * gated, axis=0, keepdims=True)
        out_refs[0][...] = d_gated * silu
        d_gate = (d_gated * y_now * sig * (1.0 + gate_now * (1.0 - sig))).astype(BF)
        out_refs[1][...] = d_gate[:, :cut_at]
        out_refs[2][...] = d_gate[:, cut_at:]

    return gathered_call(
        body, 256, [d_mix, y, gate, squares, others, pulls], [kern], [matrix],
        jnp.array(NO_SHIFT, jnp.int32),
        [
            ((rows, width), F32, "rows"), ((rows, cut_at), BF, "rows"),
            ((rows, width - cut_at), BF, "rows"), ((8, width), F32, "one"),
        ],
        "gate_back",
    )


def normed_back(grads, matrices, shift):
    rows = grads[0].shape[0]
    widths = [grad.shape[1] for grad in grads]
    depth = sum(part.shape[0] * part.shape[1] for part in matrices[0][0][:4])
    tile = 256

    def body(row_refs, fixed_refs, held, out_refs, number):
        total = None
        start = 0
        for ref, width in zip(row_refs, widths):
            term = nt(ref[...], held[:, start : start + width])
            total = term if total is None else total + term
            start += width
        split_rows(total, number, rows // tile, out_refs[0], out_refs[1])

    return gathered_call(
        body, tile, grads, [], matrices, shift,
        [((rows // 2, depth), BF, "low"), ((rows // 2, depth), F32, "high")], "normed_back",
    )


def rows_call(body, tile, row_args, fixed_args, outs, name):
    arrays = [arg if isinstance(arg, tuple) else (arg, None) for arg in row_args]
    rows = arrays[0][0].shape[-2]

    def spec(array, number):
        if number is None:
            return pl.BlockSpec((tile, array.shape[1]), lambda i: (i, 0))
        return pl.BlockSpec((None, tile, array.shape[2]), lambda i: (number, i, 0))

    return pl.pallas_call(
        body,
        grid=(rows // tile,),
        out_shape=tuple(jax.ShapeDtypeStruct(shape, kind) for shape, kind, _ in outs),
        in_specs=[spec(*item) for item in arrays]
        + [pl.BlockSpec(arg.shape, lambda i: (0, 0)) for arg in fixed_args],
        out_specs=tuple(
            pl.BlockSpec(shape, lambda i: (0, 0))
            if one
            else pl.BlockSpec((tile, shape[1]), lambda i: (i, 0))
            for shape, _, one in outs
        ),
        compiler_params=pltpu.CompilerParams(
            dimension_semantics=("arbitrary",), vmem_limit_bytes=VMEM
        ),
        cost_estimate=SMALL,
        name=name,
    )(*[array for array, _ in arrays], *fixed_args)


def columns_call(body, row_args, outs, name):
    arrays = [arg if isinstance(arg, tuple) else (arg, None) for arg in row_args]
    width = arrays[0][0].shape[-1]
    tile = width // 2

    def spec(array, number):
        if number is None:
            return pl.BlockSpec((array.shape[0], tile), lambda i: (0, i))
        return pl.BlockSpec((None, array.shape[1], tile), lambda i: (number, 0, i))

    return pl.pallas_call(
        body,
        grid=(width // tile,),
        out_shape=tuple(jax.ShapeDtypeStruct(shape, BF) for shape in outs),
        in_specs=[spec(*item) for item in arrays],
        out_specs=tuple(pl.BlockSpec((shape[0], tile), lambda i: (0, i)) for shape in outs),
        compiler_params=pltpu.CompilerParams(
            dimension_semantics=("arbitrary",), vmem_limit_bytes=VMEM
        ),
        cost_estimate=SMALL,
        name=name,
    )(*[array for array, _ in arrays])


def normed_rows(tokens, others, gain, core):
    rows, width = tokens.shape
    tile = 128

    def body(core_ref, mine_ref, other_ref, gain_ref, out_ref):
        for ref, spot in ((mine_ref, core_ref[0]), (other_ref, 1 - core_ref[0])):
            values = ref[...].astype(F32)
            out_ref[spot] = (values * norm_rows(values) * gain_ref[...]).astype(BF)

    by_rows = pl.BlockSpec((tile, width), lambda i: (i, 0))
    return pl.pallas_call(
        body,
        grid=(rows // tile,),
        out_shape=jax.ShapeDtypeStruct((2, rows, width), BF),
        in_specs=[
            pl.BlockSpec(memory_space=pltpu.SMEM), by_rows, by_rows,
            pl.BlockSpec((1, width), lambda i: (0, 0)),
        ],
        out_specs=pl.BlockSpec((2, tile, width), lambda i: (0, i, 0)),
        compiler_params=pltpu.CompilerParams(
            dimension_semantics=("arbitrary",), vmem_limit_bytes=VMEM
        ),
        cost_estimate=SMALL,
        name="normed_rows",
    )(core, tokens, others, gain).reshape(2 * rows, width)


def marked_rows(grad_out, routes, core, first_lane):
    rows, width = grad_out.shape
    tile = 256

    def body(core_ref, grad_ref, routes_ref, out_ref):
        out_ref[:, :width] = grad_ref[...]
        lane = lax.broadcasted_iota(jnp.int32, (tile, LANES), 1)
        start = pl.multiple_of(core_ref[0] * rows + pl.program_id(0) * tile, tile)
        named = routes_ref[pl.ds(start, tile), :]
        marks = jnp.zeros(lane.shape, F32)
        for number in range(routes_ref.shape[1]):
            marks = jnp.where(lane == named[:, number : number + 1] + first_lane, 1.0, marks)
        out_ref[:, width:] = marks.astype(BF)

    return pl.pallas_call(
        body,
        grid=(rows // tile,),
        out_shape=jax.ShapeDtypeStruct((rows, width + LANES), BF),
        in_specs=[
            pl.BlockSpec(memory_space=pltpu.SMEM),
            pl.BlockSpec((tile, width), lambda i: (i, 0)),
            pl.BlockSpec(routes.shape, lambda i: (0, 0)),
        ],
        out_specs=pl.BlockSpec((tile, width + LANES), lambda i: (i, 0)),
        compiler_params=pltpu.CompilerParams(
            dimension_semantics=("arbitrary",), vmem_limit_bytes=VMEM
        ),
        cost_estimate=SMALL,
        name="marked_rows",
    )(core, grad_out, routes)


def prepare_params(conv_w, conv_b, norm_gain, d_skip, dt_bias, a_log, core, local, heads):
    wide = conv_w.shape[1]
    both = norm_gain.shape[1]

    def body(core_ref, w_ref, b_ref, gain_ref, skip_ref, bias_ref, log_ref, kern_ref, head_ref, spread_ref):
        row = lax.broadcasted_iota(jnp.int32, (LANES, local), 0)
        column = lax.broadcasted_iota(jnp.int32, (LANES, local), 1)
        head = jnp.where(row >= LANES // 2, row - LANES // 2, row)
        low = head * P_SIZE
        spread = jnp.where((column >= low) & (column < low + P_SIZE), 1.0, 0.0).astype(BF)
        spread_ref[...] = spread
        first = core_ref[0] == 0

        def mine(ref):
            return jnp.where(first, ref[:, :heads], ref[:, heads : 2 * heads])

        kern_ref[...] = jnp.zeros(kern_ref.shape, F32)
        spot = pl.ds(pl.multiple_of(core_ref[0] * local, LANES), local)
        kern_ref[0:4, :local] = w_ref[:, spot]
        kern_ref[0:4, local + LANES :] = w_ref[:, both:]
        kern_ref[4:5, :local] = b_ref[:, spot]
        kern_ref[4:5, local + LANES :] = b_ref[:, both:]
        head_ref[...] = jnp.zeros(head_ref.shape, F32)
        head_ref[2:3, :heads] = mine(skip_ref)
        kern_ref[5:6, :local] = spread_heads(head_ref[...], spread)[2:3]
        kern_ref[6:7, :local] = gain_ref[:, spot]
        head_ref[0:1, :heads] = mine(bias_ref)
        head_ref[1:2, :heads] = jnp.exp(mine(log_ref))

    return small_call(
        body,
        [((8, local + LANES + wide - both), F32), ((8, LANES), F32), ((LANES, local), BF)],
        [core, conv_w, conv_b, norm_gain, d_skip, dt_bias, a_log], "prepare_params", 1,
    )


def mid_rows_of(mixed, others, tokens, gain):
    rows, width = tokens.shape

    def body(mixed_ref, other_ref, tokens_ref, gain_ref, resid_ref, mid_ref):
        resid = tokens_ref[...].astype(F32) + mixed_ref[...] + other_ref[...].astype(F32)
        resid_ref[...] = resid
        mid_ref[...] = (resid * norm_rows(resid) * gain_ref[...]).astype(BF)

    return rows_call(
        body, 256, [mixed, others, tokens], [gain],
        [((rows, width), F32, False), ((rows, width), BF, False)], "mid_rows",
    )


def across_sum(mine, came, number):
    _, rows, width = mine.shape
    cut = rows // 2

    def body(mine_ref, came_ref, low_ref, high_ref):
        total = (mine_ref[...].astype(F32) + came_ref[...].astype(F32)).astype(BF)
        low_ref[...] = total[:cut]
        high_ref[...] = total[cut:]

    return columns_call(
        body, [(mine, number), (came, number)], [(cut, width)] * 2, "across_sum"
    )


def side_sums(mine, came, over_x, over_y):
    _, rows, width = mine.shape
    cut = rows // 2

    def body(mine_x, came_x, mine_y, came_y, over_x_ref, over_y_ref, x_ref, y_ref):
        to_x = mine_x[...].astype(F32) + came_x[...].astype(F32)
        x_ref[:cut] = to_x[:cut].astype(BF)
        x_ref[cut:] = (to_x[cut:] + over_y_ref[...].astype(F32)).astype(BF)
        to_y = mine_y[...].astype(F32) + came_y[...].astype(F32)
        y_ref[:cut] = (to_y[:cut] + over_x_ref[...].astype(F32)).astype(BF)
        y_ref[cut:] = to_y[cut:].astype(BF)

    return columns_call(
        body, [(mine, 0), (came, 0), (mine, 1), (came, 1), over_x, over_y],
        [(rows, width)] * 2, "side_sums",
    )


def own_sum(mine_ref, came_ref, x_ref, y_ref):
    return (
        mine_ref[...].astype(F32) + came_ref[...].astype(F32)
        + x_ref[...].astype(F32) + y_ref[...].astype(F32)
    )


def norm_back(d_rows, values, gain, grad_ref):
    scale = norm_rows(values)

    @pl.when(pl.program_id(0) == 0)
    def _():
        grad_ref[...] = jnp.zeros(grad_ref.shape, F32)

    grad_ref[0:1, :] += jnp.sum(d_rows * values * scale, axis=0, keepdims=True)
    pulled = d_rows * gain
    mean = jnp.mean(values * pulled, axis=-1, keepdims=True)
    return scale * pulled - values * (scale * scale * scale) * mean


def resid_back(mine, came, from_x, from_y, resid, tokens, grad_out, gain):
    rows, width = tokens.shape

    def body(
        mine_ref, came_ref, x_ref, y_ref, resid_ref, tokens_ref, grad_ref, gain_ref,
        d_resid_ref, d_mix_ref, pulls_ref, gain_grad_ref,
    ):
        resid_now = resid_ref[...]
        d_mid = own_sum(mine_ref, came_ref, x_ref, y_ref)
        d_extra = norm_back(d_mid, resid_now, gain_ref[...], gain_grad_ref)
        d_resid = grad_ref[...].astype(F32) + d_extra
        d_resid_ref[...] = d_resid
        d_mix = d_resid.astype(BF)
        d_mix_ref[...] = d_mix
        mixed = resid_now - tokens_ref[...].astype(F32)
        pull = jnp.sum(d_mix.astype(F32) * mixed, axis=1, keepdims=True)
        pulls_ref[...] = jnp.broadcast_to(pull, pulls_ref.shape)

    return rows_call(
        body, 256, [(mine, 0), (came, 0), from_x, from_y, resid, tokens, grad_out], [gain],
        [
            ((rows, width), F32, False), ((rows, width), BF, False),
            ((rows, LANES), F32, False), ((8, width), F32, True),
        ],
        "resid_back",
    )


def output_rows(mine, came, from_x, from_y, resid):
    def body(mine_ref, came_ref, x_ref, y_ref, resid_ref, out_ref):
        out_ref[...] = (resid_ref[...] + own_sum(mine_ref, came_ref, x_ref, y_ref)).astype(BF)

    return rows_call(
        body, 256, [(mine, 0), (came, 0), from_x, from_y, resid], [], [(resid.shape, BF, False)],
        "output_rows",
    )[0]


def tokens_back(mine, came, tokens, d_resid, gain):
    rows, width = tokens.shape

    def body(mine_ref, came_ref, tokens_ref, d_resid_ref, gain_ref, out_ref, gain_grad_ref):
        d_rows = mine_ref[...] + came_ref[...].astype(F32)
        d_extra = norm_back(d_rows, tokens_ref[...].astype(F32), gain_ref[...], gain_grad_ref)
        out_ref[...] = (d_resid_ref[...] + d_extra).astype(BF)

    return rows_call(
        body, 256, [mine, came, tokens, d_resid], [gain],
        [((rows, width), BF, False), ((8, width), F32, True)], "tokens_back",
    )


def pack_small(par_grads, head_grads, gain_grads, mid_gains, in_gains, spread, core, local, heads):
    width_d = in_gains.shape[1]
    both = 2 * local
    rest = par_grads.shape[1] - local - LANES

    def body(core_ref, par_ref, head_ref, gain_ref, mid_ref, in_ref, spread_ref, out_ref):
        out_ref[...] = jnp.zeros(out_ref.shape, F32)
        spot = pl.ds(pl.multiple_of(core_ref[0] * local, LANES), local)
        out_ref[0:5, spot] = par_ref[0:5, :local]
        out_ref[0:5, both:] = par_ref[0:5, local + LANES :]
        out_ref[5:6, spot] = gain_ref[0:1, :]
        out_ref[6:7, :width_d] = in_ref[0:1, :]
        out_ref[6:7, width_d : 2 * width_d] = mid_ref[0:1, :]
        lane = lax.broadcasted_iota(jnp.int32, (8, LANES), 1)
        skip = gather_heads(par_ref[:, :local], spread_ref[...], lane < heads)
        for number, row in enumerate((head_ref[0:1], head_ref[1:2], skip[5:6])):
            start = pl.multiple_of((2 * number + core_ref[0]) * LANES, LANES)
            out_ref[7:8, pl.ds(start, LANES)] = row

    return small_call(
        body, [((8, both + rest), F32)],
        [core, par_grads, head_grads, gain_grads, mid_gains, in_gains, spread], "pack_small", 1,
    )[0]


def out_outputs(og_sums, cut):
    height = og_sums.shape[0]

    def body(sums_ref, out_ref):
        out_ref[:cut, :] = sums_ref[:, :cut].T
        out_ref[cut:, :] = sums_ref[:, 2 * cut : 3 * cut].T

    return small_call(body, [((2 * cut, height), F32)], [og_sums], "out_outputs")[0]


def inner_outputs(og_sums, in_sums, core, local, heads, cut):
    height = in_sums.shape[0]
    half = height // 2
    if height % 32:
        gate = jnp.concatenate([og_sums[:, cut : 2 * cut], og_sums[:, 3 * cut :]], axis=1)
        joint = in_sums[:, local:].reshape(2, half, -1)
        return (
            jnp.stack([gate, in_sums[:, :local]], axis=1), in_sums[:, local : local + heads],
            pick(joint, core[0]), pick(joint, 1 - core[0]),
        )

    def body(core_ref, og_ref, in_ref, zx_ref, dt_ref, mine_ref, sent_ref):
        zx_ref[:, 0, :cut] = og_ref[:, cut : 2 * cut]
        zx_ref[:, 0, cut:] = og_ref[:, 3 * cut :]
        zx_ref[:, 1, :] = in_ref[:, :local]
        dt_ref[...] = in_ref[:, local : local + heads]
        for ref, spot in ((mine_ref, core_ref[0]), (sent_ref, 1 - core_ref[0])):
            ref[...] = in_ref[pl.ds(pl.multiple_of(spot * half, half), half), local:]

    rest = in_sums.shape[1] - local
    return small_call(
        body,
        [
            ((height, 2, local), F32), ((height, heads), F32), ((half, rest), F32),
            ((half, rest), F32),
        ],
        [core, og_sums, in_sums], "inner_outputs", 1,
    )


def unpack_experts(came, place, units, shared_units):
    height, width = came[0].shape
    hidden = width // 3
    own = EXPERTS // GROUP

    def body(place_ref, *refs):
        came_refs, (gu_ref, down_ref, sgu_ref, sdown_ref) = refs[:GROUP], refs[GROUP:]
        for k in range(GROUP):
            bit_0 = lax.rem(place_ref[0] + k % 2, 2)
            bit_1 = lax.rem(place_ref[0] // 2 + k // 2, 2)
            member = bit_0 + 2 * bit_1
            for e in range(own):
                expert = member * own + e
                for j in range(2):
                    start = j * hidden + e * units
                    gu_ref[expert, :, j, :] = came_refs[k][:, start : start + units].astype(F32)
                start = 2 * hidden + e * units
                down_ref[expert] = came_refs[k][:, start : start + units].astype(F32).T
            spot = pl.ds(pl.multiple_of(member * shared_units, shared_units), shared_units)
            for j in range(2):
                start = j * hidden + own * units
                sgu_ref[:, j, spot] = came_refs[k][:, start : start + shared_units].astype(F32)
            start = 2 * hidden + own * units
            sdown_ref[spot, :] = came_refs[k][:, start : start + shared_units].astype(F32).T

    return pl.pallas_call(
        body,
        out_shape=(
            jax.ShapeDtypeStruct((EXPERTS, height, 2, units), F32),
            jax.ShapeDtypeStruct((EXPERTS, units, height), F32),
            jax.ShapeDtypeStruct((height, 2, GROUP * shared_units), F32),
            jax.ShapeDtypeStruct((GROUP * shared_units, height), F32),
        ),
        in_specs=[pl.BlockSpec(memory_space=pltpu.SMEM)]
        + [pl.BlockSpec(memory_space=pltpu.VMEM)] * GROUP,
        out_specs=(pl.BlockSpec(memory_space=pltpu.VMEM),) * 4,
        compiler_params=pltpu.CompilerParams(vmem_limit_bytes=VMEM),
        cost_estimate=SMALL,
        name="unpack_experts",
    )(place, *came)


def expert_body(plan, *refs):
    own, units, shared, counts, part_count, aliased = plan
    hidden = own * units + shared
    refs = list(refs)

    def take(number):
        out = refs[:number]
        del refs[:number]
        return out

    order_ref, base_ref = take(2)
    x_pieces = [take(number) for number in counts]
    ym_pieces = [take(number) for number in counts]
    count = len(counts)
    (router_ref,) = take(1)
    part_refs = take(part_count)
    take(aliased)
    x_out, dy_out, gate_ref, up_ref, down_ref = take(5)
    out_mine, out_other, dx_mine, dx_other = take(4)
    w, sems, x_held, ym_held, row_sems = refs
    step = pl.program_id(0)
    width = router_ref.shape[0]

    def fetch(number):
        slot = number % 2
        copies = []
        for which, (parts, target) in enumerate(
            ((x_pieces[number], x_held), (ym_pieces[number], ym_held))
        ):
            start = 0
            for half, ref in enumerate(parts):
                rows = ref.shape[0]
                copies.append(
                    pltpu.make_async_copy(
                        ref, target.at[slot, start : start + rows], row_sems.at[which, slot, half]
                    )
                )
                start += rows
        return copies

    @pl.when(step == 0)
    def _():
        loads = load_pieces(order_ref, part_refs, [0] * part_count, w, 0, sems)
        for copy in fetch(0) + loads:
            copy.start()
        for copy in loads:
            copy.wait()

    for number in range(count):

        @pl.when(step == number)
        def _():
            if number + 1 < count:
                for copy in fetch(number + 1):
                    copy.start()
            for copy in fetch(number):
                copy.wait()

    slot = lax.rem(step, 2)
    x_now, ym_now = x_held.at[slot], ym_held.at[slot]
    x_out[...] = x_now[...]
    dy_out[...] = ym_now[:, :width]
    tile = x_now.shape[0]
    lane = lax.broadcasted_iota(jnp.int32, (tile, LANES), 1)
    routed = ym_now[:, width:].astype(F32) > 0.5
    logits = nn(x_now[...], router_ref[...])
    top = jnp.max(jnp.where(routed, logits, -1e30), axis=1, keepdims=True)
    powers = jnp.where(routed, jnp.exp(jnp.where(routed, logits - top, 0.0)), 0.0)
    gates = powers / jnp.sum(powers, axis=1, keepdims=True)
    d_gates = jnp.zeros((tile, LANES), F32)
    parts = [(e * units, units, e) for e in range(own)] + [(own * units, shared, None)]
    for start, size, expert in parts:
        cols = [slice(k * hidden + start, k * hidden + start + size) for k in range(3)]
        pre = nn(x_now[...], w[:, cols[0]])
        up = nn(x_now[...], w[:, cols[1]])
        d_act = nn(ym_now[:, :width], w[:, cols[2]])
        sig = sigmoid(pre)
        silu = pre * sig
        act = (silu * up).astype(BF).astype(F32)
        if expert is not None:
            here = lane == base_ref[0] + expert
            gate = jnp.sum(jnp.where(here, gates, 0.0), axis=1, keepdims=True)
            d_gate = jnp.sum(act * d_act, axis=1, keepdims=True)
            d_gates = jnp.where(here, d_gate, d_gates)
            d_act = d_act * gate
            act = act * gate
        gate_ref[:, cols[0]] = (d_act * up * sig * (1.0 + pre * (1.0 - sig))).astype(BF)
        up_ref[:, cols[0]] = (d_act * silu).astype(BF)
        down_ref[:, start : start + size] = act.astype(BF)
    mean = jnp.sum(gates * d_gates, axis=1, keepdims=True)
    d_logits = (gates * (d_gates - mean)).astype(BF)
    up_ref[:, hidden:] = d_logits
    cut = 256

    def results(out_ref, dx_ref):
        for number in range(width // cut):
            rows = slice(number * cut, (number + 1) * cut)
            out_ref[0, :, rows] = nt(down_ref[...], w[rows, 2 * hidden :]).astype(BF)
            d_x = nt(gate_ref[...], w[rows, :hidden])
            d_x = d_x + nt(up_ref[:, :hidden], w[rows, hidden : 2 * hidden])
            dx_ref[0, :, rows] = (d_x + nt(d_logits, router_ref[rows, :])).astype(BF)

    @pl.when(slot == 0)
    def _():
        results(out_mine, dx_mine)

    @pl.when(slot == 1)
    def _():
        results(out_other, dx_other)


def expert_rows(members, x_pieces, ym_pieces, held, base, router, parts, targets, units, shared):
    low, count = members[0], len(members)
    width = router.shape[0]
    x_pieces = [item if isinstance(item, tuple) else (item,) for item in x_pieces]
    ym_pieces = [item if isinstance(item, tuple) else (item,) for item in ym_pieces]
    tile = sum(part.shape[0] for part in x_pieces[0])
    counts = [len(item) for item in x_pieces]
    rows = 2 * GROUP * tile
    steps = 2 * count
    own = EXPERTS // GROUP
    hidden = own * units + shared

    def like(columns):
        spec = pl.BlockSpec((tile, columns), lambda i: (i + 2 * low, 0))
        return jax.ShapeDtypeStruct((rows, columns), BF), spec

    result = (
        jax.ShapeDtypeStruct((count, tile, width), BF),
        pl.BlockSpec((1, tile, width), lambda i: (i // 2, 0, 0)),
    )
    outs = [like(columns) for columns in (width, width, hidden, hidden + LANES, hidden)]
    outs += [result] * 4
    any_ref = pl.BlockSpec(memory_space=pl.ANY)
    flat = [part for item in x_pieces + ym_pieces for part in item]
    args = [targets, base, *flat, router, *parts, *held]
    specs = [pl.BlockSpec(memory_space=pltpu.SMEM)] * 2 + [any_ref] * len(flat)
    specs += [pl.BlockSpec(router.shape, lambda i: (0, 0))]
    specs += [any_ref] * (len(parts) + len(held))
    aliases = {len(args) - len(held) + i: i for i in range(len(held))}
    done = pl.pallas_call(
        functools.partial(
            expert_body, (own, units, shared, counts, len(parts), len(held))
        ),
        grid=(steps,),
        out_shape=tuple(shape for shape, _ in outs),
        in_specs=specs,
        out_specs=tuple(spec for _, spec in outs),
        scratch_shapes=[
            pltpu.VMEM((width, 3 * hidden), BF), pltpu.SemaphoreType.DMA((targets.shape[0],)),
            pltpu.VMEM((2, tile, width), BF), pltpu.VMEM((2, tile, width + LANES), BF),
            pltpu.SemaphoreType.DMA((2, 2, 2)),
        ],
        input_output_aliases=aliases,
        compiler_params=pltpu.CompilerParams(
            dimension_semantics=("arbitrary",), vmem_limit_bytes=VMEM
        ),
        cost_estimate=SMALL,
        name="expert_rows",
    )(*args)
    return list(done[:5]), list(done[5:])


def shards(
    tokens, routes, gain_in, w_zx, w_dt, w_bc, conv_w, conv_b, dt_bias, a_log, d_skip, norm_gain,
    w_out, gain_mid, router, shared_gu, shared_down, expert_gu, expert_down, grad_out,
):
    core = lax.axis_index("tensor")
    me = lax.axis_index("dp")
    lines = lax.axis_size("dp") // GROUP
    line, place = me // GROUP, lax.rem(me, GROUP)
    piece, width_d = tokens.shape
    local = w_zx.shape[2]
    heads = w_dt.shape[1]
    units = expert_gu.shape[3]
    own = EXPERTS // GROUP
    inner_all = norm_gain.shape[0]
    height = w_zx.shape[0]
    cut_in, cut_gate = 2 * local // 3, local // 2
    third = (lines - 1 + 2) // 3
    place_now = place.reshape(1)
    where = jnp.stack([place, line]).astype(jnp.int32)
    base = (heads + own * place).reshape(1)
    tiles = 4
    mine_last = (tiles // 2 * (1 - core)).reshape(1).astype(jnp.int32)

    lines_back = lax.rem(line - jnp.arange(lines, dtype=jnp.int32) + lines, lines)
    members = place ^ jnp.arange(GROUP, dtype=jnp.int32)
    pieces = jnp.concatenate([members, members[3:]])
    mixer_targets = (pieces[:, None] + GROUP * lines_back[None, :]).reshape(-1)
    expert_targets = (members[None, :] + GROUP * lines_back[:, None]).reshape(-1)
    order = Order()

    core_now = core.reshape(1)
    gain_in, gain_mid, conv_b, norm_gain = gain_in[None], gain_mid[None], conv_b[None], norm_gain[None]
    d_skip, dt_bias, a_log = d_skip[None], dt_bias[None], a_log[None]
    joint = jnp.concatenate([w_bc, router], axis=1)
    joint_came = swap(joint)
    ring_a = [w_zx[:, 1, :cut_in]]
    tokens_other = swap(tokens)
    order.set(ring_a[0], joint)
    joint = in_order(joint, order(joint_came), core)
    bc_cols, router_cols = joint[:, : 2 * NS], joint[:, 2 * NS :]
    pad = jnp.zeros((height, LANES - heads - EXPERTS), BF)
    ring_b = [jnp.concatenate([w_zx[:, 1, cut_in:], w_dt, router_cols, pad, bc_cols], axis=1)]
    order.set(ring_b[0])
    ring_on(ring_a, order, 1, 1 + third, lines)
    order.set(ring_a[-1])
    shared_units = shared_gu.shape[2] // GROUP
    hidden = own * units + shared_units
    gu = order(expert_gu).reshape(GROUP, own, height, 2, units).transpose(0, 2, 3, 1, 4)
    gu = gu.reshape(GROUP, height, 2, own * units)
    order.set(gu)
    ring_on(ring_b, order, 1, 1 + third, lines)
    ring_on(ring_a, order, 1 + third, 1 + 2 * third, lines)
    order.set(ring_a[-1], ring_b[-1])
    down = order(expert_down).reshape(GROUP, own, units, height).transpose(0, 3, 1, 2)
    down = down.reshape(GROUP, height, own * units)
    sgu = order(shared_gu).reshape(height, 2, GROUP, shared_units).transpose(2, 0, 1, 3)
    sdown = order(shared_down).reshape(GROUP, shared_units, height).transpose(0, 2, 1)
    order.set(
        down, sgu, sdown, gain_in, gain_mid, where, base, mine_last, place_now, core_now,
        mixer_targets, expert_targets,
    )
    ring_on(ring_b, order, 1 + third, 1 + 2 * third, lines)
    ring_on(ring_a, order, 1 + 2 * third, lines, lines)
    order.set(ring_a[-1], ring_b[-1])
    gu, sgu, down, sdown = order((gu, sgu, down, sdown))
    packed = jnp.concatenate([gu[:, :, 0], sgu[:, :, 0], gu[:, :, 1], sgu[:, :, 1], down, sdown], axis=2)
    to_send = [pick(packed, members[k]) for k in range(GROUP)]
    order.set(*to_send)
    came = to_send[:1] + [hop(to_send[k], k) for k in range(1, GROUP)]
    go_block = order(jnp.concatenate([w_zx[:, 0], w_out.T], axis=1))
    order.set(go_block)
    ring_on(ring_b, order, 1 + 2 * third, lines, lines)
    order.set(ring_a[-1], ring_b[-1])

    def matrix(parts, cut_at):
        return pieces_of(parts, mixer_targets, cut_at)

    def along_both(stacked):
        return [stacked, hop(stacked, 1), hop(stacked, 2)]

    def across_halves(parts, cut_at):
        width = parts[0].shape[2]
        low, high = cut_columns(parts[1], 0, cut_at), cut_columns(parts[2], cut_at, width - cut_at)
        order.set(low, high)
        return parts + [hop(low, 2), hop(high, 1)]

    go_ring = [order(go_block)]
    tokens_other = order.take(tokens_other)
    in_stack = stack_pairs(ring_a, ring_b)
    order.set(in_stack)
    ring_on(go_ring, order, 1, 1 + third, lines)
    order.set(go_ring[-1])
    came = order.take(*came)
    ring_on(go_ring, order, 1 + third, 1 + 2 * third, lines)
    order.set(go_ring[-1])
    in_w = along_both(order(in_stack))
    expert_ring = [stack_columns(order(came), 0, 3 * hidden)]
    marked = marked_rows(order(grad_out), routes, core_now, heads)
    normed = normed_rows(order(tokens), tokens_other, gain_in, core_now)
    kern, head_par, spread = prepare_params(
        order(conv_w), conv_b, norm_gain, d_skip, dt_bias, a_log, core_now, local, heads
    )
    order.set(normed, marked, expert_ring[0], kern)
    ring_on(go_ring, order, 1 + 2 * third, lines, lines)
    order.set(go_ring[-1])
    expert_ring[0] = order(expert_ring[0])
    in_w = list(order.take(*in_w))
    in_w = across_halves(in_w, cut_in)
    marked_other = order.take(swap(order(marked)))
    gate_stack = stack_columns(order(go_ring), 0, local)
    in_w = order.take(*in_w, gate_stack)
    gate_stack, in_w = in_w[-1], list(in_w[:-1])

    gate_w = along_both(gate_stack)
    in_matrix = matrix(in_w, cut_in)
    zi, router_w = inner_product(order(normed), in_matrix, local)
    order.set(zi)
    ring_on(expert_ring, order, 1, 1 + third, lines)
    order.set(expert_ring[-1])
    y, states = front_scan(order(zi), kern, head_par, spread)
    order.set(y)
    gate_w = list(order.take(*gate_w))
    gate_w = across_halves(gate_w, cut_gate)
    out_stack = stack_columns(order(go_ring), local, width_d)
    order.set(out_stack)
    gate_w = list(order.take(*gate_w))
    out_w = along_both(order(out_stack))
    gate_matrix = matrix(gate_w, cut_gate)
    gate, squares = gate_product(order(normed), y, gate_matrix)
    order.set(gate)
    squares_other = order.take(swap(squares))
    out_w = list(order.take(*out_w))
    ring_on(expert_ring, order, 1 + third, 1 + 2 * third, lines)
    order.set(expert_ring[-1])
    out_w = across_halves(out_w, cut_gate)
    out_w = list(order.take(*out_w))
    marked_sent = order(marked)
    marked_x, marked_y = hop(marked_sent, 1), hop(marked_sent, 2)
    out_matrix = matrix(out_w, cut_gate)
    scaled, mixed_sent, mixed_mine = mixed_product(
        order(y), gate, squares, squares_other, kern, out_matrix, mine_last, inner_all
    )
    order.set(mixed_mine)
    marked_x, marked_y = order.take(marked_x, marked_y)
    half_rows = piece // 2

    def halves_of(from_x, from_y):
        return cut_rows_of(from_x, 0, half_rows), cut_rows_of(from_y, half_rows, half_rows)

    def across(halves):
        return hop(halves[0], 2), hop(halves[1], 1)

    marked_halves = halves_of(marked_x, marked_y)
    order.set(*marked_halves)
    ring_on(expert_ring, order, 1 + 2 * third, lines, lines)
    order.set(expert_ring[-1])
    mixed_came = order.take(swap(order(mixed_sent)))
    resid, mid = mid_rows_of(mixed_mine, mixed_came, tokens, gain_mid)
    order.set(mid)

    mid_x, mid_y = hop(mid, 1), hop(mid, 2)
    mid_other = order.take(swap(mid))
    marked_swap_x, marked_swap_y = swap(order(marked_x)), swap(order(marked_y))
    parts, _, expert_order = pieces_of(expert_ring, expert_targets, 0)
    common = (base, router_w, parts, expert_order, units, shared_units)
    kept, result_0 = expert_rows(
        [0], [order(mid), mid_other], [marked, marked_other], [], *common
    )
    order.set(result_0[0])
    mid_x, mid_y, marked_swap_x, marked_swap_y = order.take(
        mid_x, mid_y, marked_swap_x, marked_swap_y
    )
    mid_halves = halves_of(mid_x, mid_y)
    order.set(*mid_halves)
    mid_swap_x, mid_swap_y = order.take(swap(mid_x), swap(mid_y))
    mid_d, marked_d = across(order(mid_halves)), across(order(marked_halves))
    kept, result = expert_rows(
        [1, 2], order([mid_x, mid_swap_x, mid_y, mid_swap_y]),
        [marked_x, marked_swap_x, marked_y, marked_swap_y], kept, *common,
    )
    order.set(result[0])
    mid_d = order.take(*mid_d)
    marked_d = order.take(*marked_d)
    mid_d_other = order.take(*[swap(item) for item in mid_d])
    marked_d_other = order.take(*[swap(item) for item in marked_d])
    d_others, d_other_0 = swap(order(result[3])), swap(order(result_0[3]))
    kept, result_3 = expert_rows(
        [3], [order(mid_d), mid_d_other], [marked_d, marked_d_other], kept, *common
    )
    order.set(result_3[0])
    x_all, dy_all, gate_acts, up_acts, down = kept
    d_others, d_other_0 = order.take(d_others, d_other_0)
    d_other_3 = order.take(swap(result_3[3]))
    over_low, over_high = across_sum(result_3[2], d_other_3, 0)
    order.set(over_low)
    d_over = hop(over_low, 1), hop(over_high, 2)
    out_others = swap(order(result_3[1])), swap(order(result[1])), swap(order(result_0[1]))

    grad_down = tn(order(dy_all), down, BF)
    order.set(grad_down)
    d_over = order.take(*d_over)
    out_other_3, out_others, out_other_0 = order.take(*out_others)
    to_x, to_y = side_sums(result[2], d_others, *d_over)
    order.set(to_x)
    arrays = {}

    def whole_block(name, width):
        return lambda line_at: [(width, [(arrays[name], 0, line_at)], None)]

    sums = LineSums(
        {name: whole_block(name, hidden) for name in ("gate", "up", "down")},
        order, lines, GROUP * height, where, ("gate", "up", "down"),
    )
    arrays["down"] = grad_down
    sums.start("down")
    d_came = hop(to_x, 1), hop(to_y, 2)
    out_over = across_sum(result_3[0], order(out_other_3), 0)
    order.set(out_over[0], sums.sent)
    out_over = hop(out_over[0], 1), hop(out_over[1], 2)
    arrays["gate"] = tn(order(x_all), gate_acts, BF)
    order.set(arrays["gate"])
    sums.run(third, "gate")
    order.set(sums.sent)
    arrays["up"] = tn(order(x_all), up_acts, BF)
    order.set(arrays["up"])
    d_came = order.take(*d_came)
    out_over = order.take(*out_over)
    out_sums = side_sums(result[0], out_others, *out_over)
    order.set(out_sums[0])
    out_came = hop(out_sums[0], 1), hop(out_sums[1], 2)

    d_resid, d_mix_mine, pulls, mid_gains = resid_back(
        result_0[2], d_other_0, *d_came, order(resid), tokens, grad_out, gain_mid
    )
    order.set(d_mix_mine)
    sums.run(third, "up")
    order.set(sums.sent)
    d_mix_came, pulls_came = order.take(swap(d_mix_mine), swap(pulls))
    d_mix, pulls = pair_rows([(d_mix_mine, order(d_mix_came)), (pulls, pulls_came)], core_now)
    order.set(d_mix)
    d_y, dz_a, dz_b, gain_grads = gate_back(
        order(d_mix), y, gate, squares, squares_other, pulls, kern, out_matrix, cut_gate, inner_all
    )
    order.set(d_y)

    def hop_first(pair, *before):
        sent = [item.start(order) for item in pair]
        order.set(*sent)
        for other in before:
            all_came(other)
        for item, values in zip(pair, sent):
            item.came = hop(order(values), item.bits)

    def hop_second(pair):
        for item in pair:
            item.came = order(item.came)
        sent = [item.turn() for item in pair]
        order.set(*sent)
        for item, values in zip(pair, sent):
            item.came_last = hop(values, 3 - item.bits)

    def all_came(pair):
        for item in pair:
            item.came_last = order(item.came_last)
        order.set(*[item.came_last for item in pair])

    grad_out_w = tn(order(d_mix), scaled, BF)
    normed_now = order(normed)
    grad_gate_a, grad_gate_b = tn(normed_now, dz_a, BF), tn(normed_now, dz_b, BF)
    order.set(grad_gate_a, grad_gate_b, grad_out_w)
    out_came = order.take(*out_came)
    og_pair = [
        Plane([(grad_out_w, 0, cut_gate), (grad_gate_a, 0, cut_gate)], 1, where, lines),
        Plane([(grad_out_w, 1, cut_gate), (grad_gate_b, 0, cut_gate)], 2, where, lines),
    ]
    hop_first(og_pair)
    output = output_rows(order(result_0[0]), out_other_0, *out_came, resid)
    order.set(output)
    sums.run(third)
    order.set(sums.sent)
    di_a, di_b, par_grads, head_grads = back_scan(
        order(d_y), zi, states, kern, head_par, spread, cut_in
    )
    order.set(di_a)
    hop_second(og_pair)
    grad_in_a = tn(order(normed), di_a, BF)
    start = local - cut_in
    grad_router = jnp.pad(
        order(arrays["up"][:, hidden:]).astype(F32),
        ((0, 0), (start, di_b.shape[1] - start - LANES)),
    )
    grad_in_b = (tn(order(normed), di_b) + grad_router).astype(BF)
    order.set(grad_in_a, grad_in_b)
    sums.run(third)
    order.set(sums.sent)
    in_pair = [
        Plane([(grad_in_a, 0, cut_in)], 1, where, lines),
        Plane([(grad_in_b, 0, grad_in_b.shape[1])], 2, where, lines),
    ]
    hop_first(in_pair, og_pair)

    def pair_groups(pair):
        return lambda line_at: [group for item in pair for group in item.groups(line_at)]

    rest = LineSums(
        {"og": pair_groups(og_pair), "in": pair_groups(in_pair)}, order, lines, height, where
    )
    rest.start("og")
    order.set(rest.sent)
    d_sent, d_mine = normed_back(
        order([dz_a, dz_b, di_a, di_b]), [gate_matrix, in_matrix], mine_last
    )
    order.set(d_mine)

    hop_second(in_pair)
    sums.run(third)
    order.set(sums.final["up"][0])
    rest.run(third)
    order.set(rest.sent)
    d_other = order.take(swap(order(d_sent)))
    grad_tokens, in_gains = tokens_back(d_mine, d_other, tokens, d_resid, gain_in)
    order.set(grad_tokens)
    small = pack_small(
        par_grads, head_grads, gain_grads, mid_gains, in_gains, spread, core_now, local, heads
    )
    order.set(small)
    all_came(in_pair)
    rest.run(third, "in")
    order.set(rest.sent)
    to_send = member_pieces(
        [
            (arrays[name], order(sums.final[name][0]), sums.final[name][1] // hidden, hidden)
            for name in ("gate", "up", "down")
        ],
        where, lines, height,
    )
    order.set(*to_send)
    came = to_send[:1] + [hop(order(to_send[k]), k) for k in range(1, GROUP)]
    small = sum_in_order([small, order(swap(small))], core_now, 2)
    order.set(small)
    small = sum_in_order([small] + order([hop(small, k) for k in range(1, GROUP)]), place_now, GROUP)
    order.set(small)
    bits = GROUP
    while bits < lines * GROUP:
        if 2 * bits < lines * GROUP:
            others = order([hop(small, k * bits) for k in range(1, 4)])
            small = sum_in_order([small] + others, (me // bits).reshape(1), 4)
            bits *= 4
        else:
            small = sum_in_order([small, order(hop(small, bits))], (me // bits).reshape(1), 2)
            bits *= 2
        order.set(small)
    rest.run(third)
    order.set(rest.sent)
    came = list(order.take(*came))
    g_egu, g_edown, g_sgu, g_sdown = unpack_experts(came, place_now, units, shared_units)
    order.set(g_edown)
    rest.run(third)
    order.set(rest.sent)
    g_out = out_outputs(order(rest.final["og"]), cut_gate)
    order.set(g_out)
    rest.run(third)
    order.set(rest.final["in"])
    g_zx, g_dt, joint_mine, joint_sent = inner_outputs(
        rest.final["og"], rest.final["in"], core_now, local, heads, cut_gate
    )
    joint = joint_mine + swap(joint_sent)
    g_router, g_bc = joint[:, heads : heads + EXPERTS], joint[:, LANES:]

    def of_heads(number):
        return jnp.concatenate(
            [
                small[7, (2 * number + which) * LANES : (2 * number + which) * LANES + heads]
                for which in range(2)
            ]
        )

    return (
        output, grad_tokens, small[6, :width_d], g_zx, g_dt, g_bc, small[:4],
        small[4], of_heads(0), of_heads(1), of_heads(2), small[5, :inner_all], g_out,
        small[6, width_d : 2 * width_d], g_router, g_sgu, g_sdown, g_egu, g_edown,
    )


def solution(mesh):
    both = P(("dp", "tensor"), None)
    rows = P("dp", None, "tensor")
    cols = P("tensor", "dp")
    return jax.shard_map(
        shards,
        mesh=mesh,
        in_specs=(
            both, P("dp", None), P(), rows, P("dp", "tensor"), both, P(), P(), P(), P(), P(), P(),
            cols, P(), both, rows, cols, P(None, "dp", None, "tensor"), P(None, "tensor", "dp"),
            both,
        ),
        out_specs=(
            both, both, P(), rows, P("dp", "tensor"), both, P(), P(), P(), P(), P(), P(),
            cols, P(), both, rows, cols, P(None, "dp", None, "tensor"), P(None, "tensor", "dp"),
        ),
        check_vma=False,
    )
```

```python
import functools

import jax
import jax.numpy as jnp
from jax import lax
from jax.experimental import pallas as pl
from jax.experimental.pallas import tpu as pltpu
from jax.sharding import PartitionSpec as P

F32 = jnp.float32
BF = jnp.bfloat16
EPS = 1e-05
H = 48
P_SIZE = 64
NS = 128
EXPERTS = 16
BL = 128
GROUP = 4
LANES = 128
VMEM = 60 * 1024 * 1024
SMALL = pl.CostEstimate(flops=1000, bytes_accessed=1000, transcendentals=0)
highest = lax.Precision.HIGHEST


def nn(left, right):
    return lax.dot_general(left, right, (((1,), (0,)), ((), ())), preferred_element_type=F32)


def nt(left, right):
    return lax.dot_general(left, right, (((1,), (1,)), ((), ())), preferred_element_type=F32)


def tn(left, right, kind=F32):
    return lax.dot_general(left, right, (((0,), (0,)), ((), ())), preferred_element_type=kind)


def hop(values, bits):
    count = lax.axis_size("dp")
    return lax.ppermute(values, "dp", [(i, i ^ bits) for i in range(count)])


def next_line(values):
    count = lax.axis_size("dp")
    return lax.ppermute(values, "dp", [(i, (i + GROUP) % count) for i in range(count)])


def swap(values):
    return lax.ppermute(values, "tensor", [(0, 1), (1, 0)])


def pick(values, index, axis=0):
    return lax.dynamic_index_in_dim(values, index, axis, keepdims=False)


def in_order(mine, theirs, core):
    return jnp.where(
        core == 0, jnp.concatenate([mine, theirs]), jnp.concatenate([theirs, mine])
    )


def tie(values, *others):
    flat, tree = jax.tree.flatten(values)
    held = lax.optimization_barrier((flat, others))
    return jax.tree.unflatten(tree, held[0])


class Order:
    def __init__(self):
        self.marks = self.last = ()

    def __call__(self, values):
        return tie(values, *self.marks)

    def set(self, *marks):
        self.marks, self.last = marks + self.last, marks

    def take(self, *values):
        values = self(values)
        self.set(*values)
        return values if len(values) > 1 else values[0]


def ring_on(blocks, order, low, high, lines):
    for _ in range(low, min(high, lines)):
        blocks.append(order(next_line(blocks[-1])))


def pieces_of(parts, targets, cut):
    inner, height, width = parts[0].shape
    starts = [0] * len(parts)
    if cut:
        starts[-1] = cut
    if height % 32 == 0:
        return parts, starts, targets
    if cut:
        parts = parts[:3] + [jnp.concatenate(parts[3:], axis=-1)]
    flat = jnp.concatenate(parts)
    total = flat.shape[0]
    source = jnp.zeros((total,), jnp.int32)
    source = source.at[targets[:total]].set(jnp.arange(total, dtype=jnp.int32))
    whole = flat[source].reshape(1, total * height, width)
    return [whole], [0], jnp.zeros((1,), jnp.int32)


def load_pieces(target_ref, part_refs, starts, held, base, sems):
    copies = []
    for ref, start in zip(part_refs, starts):
        inner, height, width = ref.shape
        for j in range(inner):
            row = pl.multiple_of(target_ref[len(copies)] * height, height)
            copies.append(
                pltpu.make_async_copy(
                    ref.at[j],
                    held.at[pl.ds(row, height), base + start : base + start + width],
                    sems.at[len(copies)],
                )
            )
    return copies


def run_copies(copies):
    for copy in copies:
        copy.start()
    for copy in copies:
        copy.wait()


def norm_rows(values):
    return lax.rsqrt(jnp.mean(values * values, axis=-1, keepdims=True) + EPS)


def sigmoid(values):
    return 1.0 / (1.0 + jnp.exp(-values))


def split_two(values):
    high = values.astype(BF)
    return high, (values - high.astype(F32)).astype(BF)


def spread_heads(values, spread):
    high, low = split_two(values)
    packed = high.astype(F32) + pltpu.roll(low.astype(F32), LANES // 2, 1)
    return nn(packed.astype(BF), spread)


def sum_heads(values, spread, heads_on):
    return jnp.where(heads_on, nt(values.astype(BF), spread), 0.0)


def gather_heads(values, spread, heads_on):
    high, low = split_two(values)
    return jnp.where(heads_on, nt(high, spread) + nt(low, spread), 0.0)


def conv_rows(ext, kern, low, high, offset):
    summed = kern[4:5, low:high]
    for j in range(4):
        summed = summed + kern[j : j + 1, low:high] * ext[offset + j : offset + j + BL, low:high]
    return summed


def step_terms(raw, head_par, heads_on):
    shifted = raw + head_par[0:1]
    soft = jnp.maximum(shifted, 0.0) + jnp.log1p(jnp.exp(-jnp.abs(shifted)))
    step = jnp.where(heads_on, soft, 0.0)
    return shifted, step, -step * head_par[1:2]


def front_body(zi_ref, kern_ref, head_ref, spread_ref, y_ref, state_ref, ext, state):
    width = y_ref.shape[1]
    first = pl.program_id(0) == 0

    @pl.when(first)
    def _():
        ext[0:8, :] = jnp.zeros((8, ext.shape[1]), F32)
        state[...] = jnp.zeros(state.shape, F32)

    @pl.when(jnp.logical_not(first))
    def _():
        ext[0:8, :] = ext[BL : BL + 8, :]

    ext[8 : BL + 8, :] = zi_ref[...]
    rows = lax.broadcasted_iota(jnp.int32, (BL, LANES), 0)
    cols = lax.broadcasted_iota(jnp.int32, (BL, LANES), 1)
    causal = cols <= rows
    heads_on = cols < width // P_SIZE
    spread = spread_ref[...]
    state_ref[0] = state[...]
    pre = conv_rows(ext, kern_ref, 0, width, 5)
    x = pre * sigmoid(pre)
    pre = conv_rows(ext, kern_ref, width + LANES, ext.shape[1], 5)
    maps = pre * sigmoid(pre)
    b, c = maps[:, :NS], maps[:, NS:]
    shifted, step, decay = step_terms(zi_ref[:, width : width + LANES], head_ref, heads_on)
    cum = jnp.dot(causal.astype(F32), decay, precision=highest, preferred_element_type=F32)
    cum_t = cum.T
    last = cum[BL - 1 : BL]
    scores = nt(c.astype(BF), b.astype(BF))
    u = x * spread_heads(step, spread)
    from_start = spread_heads(jnp.where(heads_on, jnp.exp(cum), 0.0), spread)
    to_end = spread_heads(jnp.where(heads_on, jnp.exp(last - cum), 0.0), spread)
    u_low = u.astype(BF)
    left = cols < P_SIZE
    within = []
    for pair in range(width // LANES):
        mats = []
        for head in (2 * pair, 2 * pair + 1):
            gap = cum[:, head : head + 1] - cum_t[head : head + 1, :]
            mats.append((jnp.where(causal, jnp.exp(gap), 0.0) * scores).astype(BF))
        cut = u_low[:, pair * LANES : (pair + 1) * LANES]
        zero = jnp.zeros_like(cut)
        stacked = jnp.concatenate([jnp.where(left, cut, zero), jnp.where(left, zero, cut)], axis=0)
        within.append(nn(jnp.concatenate(mats, axis=1), stacked))
    before = state[...]
    across = nn(c.astype(BF), before.astype(BF)) * from_start
    y_ref[...] = jnp.concatenate(within, axis=1) + across + kern_ref[5:6, :width] * x
    grown = nn(b.T.astype(BF), (u * to_end).astype(BF))
    state[...] = before * from_start[BL - 1 : BL] + grown


def front_scan(zi, kern, head_par, spread):
    length, width = zi.shape[0], spread.shape[1]
    steps = length // BL
    return pl.pallas_call(
        front_body,
        grid=(steps,),
        out_shape=(
            jax.ShapeDtypeStruct((length, width), F32),
            jax.ShapeDtypeStruct((steps, NS, width), F32),
        ),
        in_specs=[
            pl.BlockSpec((BL, zi.shape[1]), lambda i: (i, 0)),
            pl.BlockSpec(kern.shape, lambda i: (0, 0)),
            pl.BlockSpec(head_par.shape, lambda i: (0, 0)),
            pl.BlockSpec(spread.shape, lambda i: (0, 0)),
        ],
        out_specs=(
            pl.BlockSpec((BL, width), lambda i: (i, 0)),
            pl.BlockSpec((1, NS, width), lambda i: (i, 0, 0)),
        ),
        scratch_shapes=[pltpu.VMEM((BL + 8, zi.shape[1]), F32), pltpu.VMEM((NS, width), F32)],
        compiler_params=pltpu.CompilerParams(
            dimension_semantics=("arbitrary",), vmem_limit_bytes=VMEM
        ),
        cost_estimate=SMALL,
        name="front_scan",
    )(zi, kern, head_par, spread)


def back_body(
    dy_ref, zi_ref, prev_ref, state_ref, kern_ref, head_ref, spread_ref,
    dia_ref, dib_ref, par_ref, hg_ref, ext, ext_d, d_state,
):
    width = dy_ref.shape[1]
    wide = zi_ref.shape[1]
    cut_at = dia_ref.shape[1]
    number = pl.program_id(0)
    steps = pl.num_programs(0)

    @pl.when(number == 0)
    def _():
        ext_d[BL : BL + 8, :] = jnp.zeros((8, wide), F32)
        d_state[...] = jnp.zeros(d_state.shape, F32)
        par_ref[...] = jnp.zeros(par_ref.shape, F32)
        hg_ref[...] = jnp.zeros(hg_ref.shape, F32)

    @pl.when(number > 0)
    def _():
        ext_d[BL : BL + 8, :] = ext_d[0:8, :]

    ext[0:8, :] = jnp.where(number == steps - 1, 0.0, prev_ref[...])
    ext[8 : BL + 8, :] = zi_ref[...]
    rows = lax.broadcasted_iota(jnp.int32, (BL, LANES), 0)
    cols = lax.broadcasted_iota(jnp.int32, (BL, LANES), 1)
    upper = rows <= cols
    strict = rows < cols
    heads_on = cols < width // P_SIZE
    left = cols < P_SIZE
    spread = spread_ref[...]
    pre_x = conv_rows(ext, kern_ref, 0, width, 5)
    sig_x = sigmoid(pre_x)
    x = pre_x * sig_x
    pre_m = conv_rows(ext, kern_ref, width + LANES, wide, 5)
    sig_m = sigmoid(pre_m)
    maps = pre_m * sig_m
    b, c = maps[:, :NS], maps[:, NS:]
    b_low, c_low = b.astype(BF), c.astype(BF)
    shifted, step, decay = step_terms(zi_ref[:, width : width + LANES], head_ref, heads_on)
    cum = jnp.dot(
        (cols <= rows).astype(F32), decay, precision=highest, preferred_element_type=F32
    )
    cum_t = cum.T
    last = cum[BL - 1 : BL]
    step_wide = spread_heads(step, spread)
    from_start = spread_heads(jnp.where(heads_on, jnp.exp(cum), 0.0), spread)
    to_end = spread_heads(jnp.where(heads_on, jnp.exp(last - cum), 0.0), spread)
    whole = from_start[BL - 1 : BL]
    d_y = dy_ref[...]
    par_ref[5:6, :width] += jnp.sum(d_y * x, axis=0, keepdims=True)
    u = x * step_wide
    u_low, dy_low = u.astype(BF), d_y.astype(BF)
    scores_t = nt(b_low, c_low)
    d_scores_t = jnp.zeros((BL, BL), F32)
    du_parts = []
    gap_rows = jnp.zeros((BL, LANES), F32)
    gap_cols = []
    for pair in range(width // LANES):
        lanes = slice(pair * LANES, (pair + 1) * LANES)
        cut_u, cut_d = u_low[:, lanes], dy_low[:, lanes]
        zero = jnp.zeros_like(cut_u)
        stack_u = jnp.concatenate([jnp.where(left, cut_u, zero), jnp.where(left, zero, cut_u)], axis=0)
        stack_d = jnp.concatenate([jnp.where(left, cut_d, zero), jnp.where(left, zero, cut_d)], axis=0)
        d_weights = nt(stack_u, cut_d)
        mats = []
        for place, head in enumerate((2 * pair, 2 * pair + 1)):
            gap = cum_t[head : head + 1, :] - cum[:, head : head + 1]
            decays = jnp.where(upper, jnp.exp(gap), 0.0)
            weight = decays * scores_t
            mats.append(weight.astype(BF))
            d_weight = d_weights[place * BL : (place + 1) * BL]
            d_scores_t = d_scores_t + decays * d_weight
            moved = jnp.where(strict, weight * d_weight, 0.0)
            gap_rows = jnp.where(cols == head, jnp.sum(moved, axis=1, keepdims=True), gap_rows)
            gap_cols.append(jnp.sum(moved, axis=0, keepdims=True))
        du_parts.append(nn(jnp.concatenate(mats, axis=1), stack_d))
    gap_cols.append(jnp.zeros((LANES - width // P_SIZE, BL), F32))
    gap_cols = jnp.concatenate(gap_cols, axis=0).T
    before, d_after = state_ref[0], d_state[...]
    before_low, d_after_low = before.astype(BF), d_after.astype(BF)
    dy_start = d_y * from_start
    dy_start_low = dy_start.astype(BF)
    reach = sum_heads(dy_start * nn(c_low, before_low), spread, heads_on)
    u_end = u * to_end
    d_from_state = nn(b_low, d_after_low)
    kept = sum_heads(u_end * d_from_state, spread, heads_on)
    carried = jnp.sum(before * d_after, axis=0, keepdims=True) * whole
    carried = gather_heads(jnp.broadcast_to(carried, (8, width)), spread, heads_on[:8])[0:1]
    d_c = nt(dy_start_low, before_low) + nn(d_scores_t.T.astype(BF), b_low)
    d_b = nt(u_end.astype(BF), d_after_low) + nn(d_scores_t.astype(BF), c_low)
    d_state[...] = d_after * whole + nn(c.T.astype(BF), dy_start_low)
    d_u = jnp.concatenate(du_parts, axis=1) + to_end * d_from_state
    d_decay = (
        jnp.dot(
            upper.astype(F32), reach + gap_cols - gap_rows, precision=highest,
            preferred_element_type=F32,
        )
        + jnp.dot(
            (cols < rows).astype(F32), kept, precision=highest, preferred_element_type=F32
        )
        + carried
    )
    d_step = sum_heads(x * d_u, spread, heads_on)
    rate = head_ref[1:2]
    d_raw = jnp.where(heads_on, (d_step - rate * d_decay) * sigmoid(shifted), 0.0)
    hg_ref[0:1, :] += jnp.sum(d_raw, axis=0, keepdims=True)
    hg_ref[1:2, :] += jnp.sum(jnp.where(heads_on, d_decay * decay, 0.0), axis=0, keepdims=True)
    d_x = step_wide * d_u + kern_ref[5:6, :width] * d_y
    ext_d[0:BL, :width] = d_x * sig_x * (1.0 + pre_x * (1.0 - sig_x))
    ext_d[0:BL, width : width + LANES] = jnp.zeros((BL, LANES), F32)
    ext_d[0:BL, width + LANES :] = (
        jnp.concatenate([d_b, d_c], axis=1) * sig_m * (1.0 + pre_m * (1.0 - sig_m))
    )
    for low, high in ((0, cut_at), (cut_at, width), (width + LANES, wide)):
        d_act = ext_d[0:BL, low:high]
        d_in = jnp.zeros((BL, high - low), F32)
        for j in range(4):
            d_in = d_in + kern_ref[j : j + 1, low:high] * ext_d[3 - j : 3 - j + BL, low:high]
            par_ref[j : j + 1, low:high] += jnp.sum(
                d_act * ext[5 + j : 5 + j + BL, low:high], axis=0, keepdims=True
            )
        par_ref[4:5, low:high] += jnp.sum(d_act, axis=0, keepdims=True)
        if low < cut_at:
            dia_ref[...] = d_in.astype(BF)
        else:
            dib_ref[:, low - cut_at : high - cut_at] = d_in.astype(BF)
    dib_ref[:, width - cut_at : width - cut_at + LANES] = d_raw.astype(BF)


def back_scan(d_y, zi, states, kern, head_par, spread, cut_at):
    length, width = d_y.shape
    wide = zi.shape[1]
    steps = length // BL
    per = BL // 8

    def back(i):
        return (steps - 1 - i, 0)

    def fixed(i):
        return (0, 0)

    return pl.pallas_call(
        back_body,
        grid=(steps,),
        out_shape=(
            jax.ShapeDtypeStruct((length, cut_at), BF),
            jax.ShapeDtypeStruct((length, wide - cut_at), BF),
            jax.ShapeDtypeStruct((8, wide), F32),
            jax.ShapeDtypeStruct((8, LANES), F32),
        ),
        in_specs=[
            pl.BlockSpec((BL, width), back),
            pl.BlockSpec((BL, wide), back),
            pl.BlockSpec((8, wide), lambda i: (jnp.maximum((steps - 1 - i) * per - 1, 0), 0)),
            pl.BlockSpec((1, NS, width), lambda i: (steps - 1 - i, 0, 0)),
            pl.BlockSpec(kern.shape, fixed),
            pl.BlockSpec(head_par.shape, fixed),
            pl.BlockSpec(spread.shape, fixed),
        ],
        out_specs=(
            pl.BlockSpec((BL, cut_at), back),
            pl.BlockSpec((BL, wide - cut_at), back),
            pl.BlockSpec((8, wide), fixed),
            pl.BlockSpec((8, LANES), fixed),
        ),
        scratch_shapes=[
            pltpu.VMEM((BL + 8, wide), F32),
            pltpu.VMEM((BL + 8, wide), F32),
            pltpu.VMEM((NS, width), F32),
        ],
        compiler_params=pltpu.CompilerParams(
            dimension_semantics=("arbitrary",), vmem_limit_bytes=VMEM
        ),
        cost_estimate=SMALL,
        name="back_scan",
    )(d_y, zi, zi, states, kern, head_par, spread)


def small_call(body, outs, args, name, scalars=0):
    vmem, smem = pl.BlockSpec(memory_space=pltpu.VMEM), pl.BlockSpec(memory_space=pltpu.SMEM)
    return pl.pallas_call(
        body,
        out_shape=tuple(jax.ShapeDtypeStruct(shape, kind) for shape, kind in outs),
        in_specs=[smem] * scalars + [vmem] * (len(args) - scalars),
        out_specs=tuple(vmem for _ in outs),
        compiler_params=pltpu.CompilerParams(vmem_limit_bytes=VMEM),
        cost_estimate=SMALL,
        name=name,
    )(*args)


def stack_columns(blocks, start, width):
    height = blocks[0].shape[0]

    def body(*refs):
        for number, ref in enumerate(refs[:-1]):
            refs[-1][number] = ref[:, start : start + width]

    shape = (len(blocks), height, width)
    return small_call(body, [(shape, blocks[0].dtype)], blocks, "stack_columns")[0]


def stack_pairs(first, second):
    height, low = first[0].shape
    high = second[0].shape[1]

    def body(*refs):
        for number in range(len(first)):
            refs[-1][number, :, :low] = refs[number][...]
            refs[-1][number, :, low:] = refs[len(first) + number][...]

    shape = (len(first), height, low + high)
    return small_call(body, [(shape, first[0].dtype)], [*first, *second], "stack_pairs")[0]


def cut_columns(values, start, width):
    def body(values_ref, out_ref):
        out_ref[...] = values_ref[:, :, start : start + width]

    return small_call(
        body, [(values.shape[:2] + (width,), values.dtype)], [values], "cut_columns"
    )[0]


def cut_rows_of(values, start, rows):
    def body(values_ref, out_ref):
        out_ref[...] = values_ref[start : start + rows]

    return small_call(body, [((rows, values.shape[1]), values.dtype)], [values], "cut_rows")[0]


def pair_rows(pairs, core):
    def body(core_ref, *refs):
        for number in range(len(pairs)):
            mine_ref, other_ref = refs[2 * number : 2 * number + 2]
            out_ref = refs[2 * len(pairs) + number]
            out_ref[core_ref[0]] = mine_ref[...]
            out_ref[1 - core_ref[0]] = other_ref[...]

    outs = [((2,) + mine.shape, mine.dtype) for mine, _ in pairs]
    args = [core] + [item for pair in pairs for item in pair]
    done = small_call(body, outs, args, "pair_rows", 1)
    return [item.reshape(-1, item.shape[2]) for item in done]


def add_blocks(groups, height, count, kind, where, name):
    total = sum(width for width, _, _ in groups)
    flat = [(width, item) for width, items, _ in groups for item in items]
    overs = []
    for _, _, over in groups:
        if over is not None and not any(over[0] is array for array in overs):
            overs.append(over[0])

    if height % 32:
        columns = []
        for width, items, over in groups:
            term = 0.0
            for array, number, spot in items:
                part = array[:, number * width : (number + 1) * width].reshape(-1, height, width)
                picked = [pick(part, spot(i, where)) for i in range(count)]
                term = term + jnp.concatenate(picked).astype(F32)
            if over is not None:
                term = term + over[0][:, over[1] : over[1] + width].astype(F32)
            columns.append(term)
        return jnp.concatenate(columns, axis=1).astype(kind)

    def body(where_ref, *refs):
        item_refs = refs[: len(flat)]
        over_refs = refs[len(flat) : len(flat) + len(overs)]
        out_ref, sems = refs[len(flat) + len(overs)], refs[-1]
        helds = refs[len(flat) + len(overs) + 1 : -1]
        copies = []
        for row, (ref, held, (width, (_, number, spot))) in enumerate(zip(item_refs, helds, flat)):
            for i in range(count):
                start = pl.multiple_of(spot(i, where_ref) * height, height)
                copies.append(
                    pltpu.make_async_copy(
                        ref.at[pl.ds(start, height), number * width : (number + 1) * width],
                        held.at[i * height : (i + 1) * height],
                        sems.at[row, i],
                    )
                )
        run_copies(copies)
        at = start = 0
        for width, items, over in groups:
            term = helds[at][...]
            if len(items) > 1 or over is not None:
                term = term.astype(F32)
            for held in helds[at + 1 : at + len(items)]:
                term = term + held[...].astype(F32)
            if over is not None:
                (number,) = [i for i, array in enumerate(overs) if array is over[0]]
                term = term + over_refs[number][:, over[1] : over[1] + width].astype(F32)
            out_ref[:, start : start + width] = term.astype(kind)
            at += len(items)
            start += width

    vmem, any_ref = pl.BlockSpec(memory_space=pltpu.VMEM), pl.BlockSpec(memory_space=pl.ANY)
    return pl.pallas_call(
        body,
        out_shape=jax.ShapeDtypeStruct((count * height, total), kind),
        in_specs=[pl.BlockSpec(memory_space=pltpu.SMEM)]
        + [any_ref] * len(flat)
        + [vmem] * len(overs),
        out_specs=vmem,
        scratch_shapes=[
            pltpu.VMEM((count * height, width), item[0].dtype) for width, item in flat
        ]
        + [pltpu.SemaphoreType.DMA((len(flat), count))],
        compiler_params=pltpu.CompilerParams(vmem_limit_bytes=VMEM),
        cost_estimate=SMALL,
        name=name,
    )(where, *[item[0] for _, item in flat], *overs)


class Plane:
    def __init__(self, values, bits, where, lines):
        self.values, self.bits, self.where, self.lines = values, bits, where, lines
        self.height = values[0][0].shape[0] // (lines * GROUP)
        self.came = self.came_last = None

    def _spot(self, i, first, second):
        x, y = (first, second) if self.bits == 1 else (second, first)
        return i * GROUP + y * 2 + x

    def _own(self, where, axis):
        return lax.rem(where[0], 2) if axis == 1 else where[0] // 2

    def start(self, order):
        def spot(i, where):
            return self._spot(i // 2, 1 - self._own(where, self.bits), i % 2)

        groups = [
            (width, [(order(array), number, spot)], None) for array, number, width in self.values
        ]
        return add_blocks(groups, self.height, 2 * self.lines, BF, self.where, "plane_start")

    def _groups(self, keep, line_at, last):
        def which(where):
            own = self._own(where, 3 - self.bits)
            return own if keep else 1 - own

        def in_came(i, where):
            return 2 * line_at(i, where) + which(where)

        def in_values(i, where):
            return self._spot(line_at(i, where), self._own(where, self.bits), which(where))

        width = sum(item[2] for item in self.values)
        groups = []
        start = 0
        for array, number, wide in self.values:
            items = [(array, number, in_values), (self.came, start, in_came)]
            if last:
                items.append((self.came_last, start, line_at))
            groups.append((wide, items, None))
            start += 1
        return groups

    def turn(self):
        return add_blocks(
            self._groups(False, lambda i, where: i, False), self.height, self.lines, BF,
            self.where, "plane_turn",
        )

    def groups(self, line_at):
        return self._groups(True, line_at, True)


class LineSums:
    def __init__(self, parts, order, lines, height, where, apart=()):
        self.parts, self.order, self.lines, self.apart = parts, order, lines, apart
        self.height, self.where = height, where
        self.steps, self.final, self.names = {}, {}, []
        self.sent = None

    def _step(self, names, overs, kind):
        groups = []
        for name in names:
            back = self.steps[name] + 1

            def line_at(i, spots, back=back):
                return lax.rem(spots[1] - back + 2 * self.lines, self.lines)

            over = overs.get(name)
            start = 0
            for width, items, _ in self.parts[name](line_at):
                groups.append((width, items, None if over is None else (over[0], over[1] + start)))
                start += width
        return add_blocks(groups, self.height, 1, kind, self.where, "line_step")

    def _send(self, names, overs):
        self.names = names
        self.sent = self._step(names, overs, BF) if names else None

    def start(self, *names):
        for name in names:
            self.steps[name] = 0
        self._send(list(names), {})

    def run(self, count, *new):
        for number in range(count):
            joining = list(new) if number + 1 == count else []
            overs = {}
            if self.names:
                came = self.order(next_line(self.sent))
                start = 0
                for name in self.names:
                    overs[name] = (came, start)
                    start += sum(width for width, _, _ in self.parts[name](None))
                    self.steps[name] += 1
                    if self.steps[name] + 1 == self.lines:
                        if name in self.apart:
                            self.final[name] = overs[name]
                        else:
                            self.final[name] = self._step([name], overs, F32)
            staying = [name for name in self.names if name not in self.final]
            for name in joining:
                self.steps[name] = 0
            if staying or joining or self.names:
                self._send(staying + joining, overs)


def member_pieces(parts, where, lines, height):
    def member(k, spots):
        bit_0 = lax.rem(spots[0] + k % 2, 2)
        return bit_0 + 2 * lax.rem(spots[0] // 2 + k // 2, 2)

    total = sum(item[3] for item in parts)
    if height % 32:
        done = []
        for k in range(GROUP):
            columns = []
            for array, came, number, width in parts:
                block = pick(array[:, :width].reshape(lines, GROUP, height, width), where[1])
                other = came[:, number * width : (number + 1) * width]
                block = block.astype(F32) + other.reshape(GROUP, height, width).astype(F32)
                columns.append(pick(block, member(k, where)))
            done.append(jnp.concatenate(columns, axis=1).astype(BF))
        return done

    def body(where_ref, *refs):
        count = len(parts)
        array_refs, came_refs = refs[:count], refs[count : 2 * count]
        out_refs = refs[2 * count : 2 * count + GROUP]
        helds, sems = refs[2 * count + GROUP : -1], refs[-1]
        rows = GROUP * height
        start = pl.multiple_of(where_ref[1] * rows, rows)
        copies = []
        for i, (_, _, number, width) in enumerate(parts):
            copies += [
                pltpu.make_async_copy(
                    array_refs[i].at[pl.ds(start, rows), :width], helds[2 * i], sems.at[2 * i]
                ),
                pltpu.make_async_copy(
                    came_refs[i].at[:, number * width : (number + 1) * width],
                    helds[2 * i + 1], sems.at[2 * i + 1],
                ),
            ]
        run_copies(copies)
        for k, out_ref in enumerate(out_refs):
            spot = pl.ds(pl.multiple_of(member(k, where_ref) * height, height), height)
            at = 0
            for i, (_, _, _, width) in enumerate(parts):
                term = helds[2 * i][spot, :].astype(F32) + helds[2 * i + 1][spot, :].astype(F32)
                out_ref[:, at : at + width] = term.astype(BF)
                at += width

    vmem, any_ref = pl.BlockSpec(memory_space=pltpu.VMEM), pl.BlockSpec(memory_space=pl.ANY)
    held = [pltpu.VMEM((GROUP * height, width), BF) for *_, width in parts for _ in range(2)]
    return list(
        pl.pallas_call(
            body,
            out_shape=(jax.ShapeDtypeStruct((height, total), BF),) * GROUP,
            in_specs=[pl.BlockSpec(memory_space=pltpu.SMEM)] + [any_ref] * (2 * len(parts)),
            out_specs=(vmem,) * GROUP,
            scratch_shapes=held + [pltpu.SemaphoreType.DMA((2 * len(parts),))],
            compiler_params=pltpu.CompilerParams(vmem_limit_bytes=VMEM),
            cost_estimate=SMALL,
            name="member_pieces",
        )(where, *[item[0] for item in parts], *[item[1] for item in parts])
    )


def sum_in_order(pieces, place, count):
    rows, width = pieces[0].shape

    def body(place_ref, *refs):
        out_ref, held = refs[-2:]
        for k in range(count):
            spot = 0
            bit = 1
            while bit < count:
                own = lax.rem(place_ref[0] // bit, 2)
                spot = spot + bit * (1 - own if k & bit else own)
                bit *= 2
            held[spot] = refs[k][...]
        total = held[0]
        for number in range(1, count):
            total = total + held[number]
        out_ref[...] = total

    vmem = pl.BlockSpec(memory_space=pltpu.VMEM)
    return pl.pallas_call(
        body,
        out_shape=jax.ShapeDtypeStruct((rows, width), F32),
        in_specs=[pl.BlockSpec(memory_space=pltpu.SMEM)] + [vmem] * count,
        out_specs=vmem,
        scratch_shapes=[pltpu.VMEM((count, rows, width), F32)],
        compiler_params=pltpu.CompilerParams(vmem_limit_bytes=VMEM),
        cost_estimate=SMALL,
        name="sum_in_order",
    )(place, *pieces)


def gathered_call(body, tile, row_args, fixed_args, matrices, shift, outs, name):
    depth = sum(part.shape[0] * part.shape[1] for part in matrices[0][0][:4])
    widths = [parts[0].shape[2] for parts, _, _ in matrices]
    counts = [len(parts) for parts, _, _ in matrices]
    targets = matrices[0][2]
    rows = row_args[0].shape[0]
    steps = rows // tile
    row_count, fixed_count = len(row_args), len(fixed_args)

    def whole(*refs):
        order_ref = refs[0]
        at = 2
        row_refs = refs[at : at + row_count]
        at += row_count
        fixed_refs = refs[at : at + fixed_count]
        at += fixed_count
        part_refs = refs[at : at + sum(counts)]
        at += sum(counts)
        out_refs = refs[at : at + len(outs)]
        held, sems = refs[-2], refs[-1]

        @pl.when(pl.program_id(0) == 0)
        def _():
            copies = []
            used = base = 0
            for number, (count, width) in enumerate(zip(counts, widths)):
                copies += load_pieces(
                    order_ref, part_refs[used : used + count], matrices[number][1], held, base,
                    sems.at[number],
                )
                used += count
                base += width
            run_copies(copies)

        body(row_refs, fixed_refs, held, out_refs, pl.program_id(0))

    def rows_map(i, order_ref, shift_ref):
        return (lax.rem(i + shift_ref[0], steps), 0)

    def fixed_map(i, order_ref, shift_ref):
        return (0, 0)

    def low_map(i, order_ref, shift_ref):
        return (jnp.minimum(i, steps // 2 - 1), 0)

    def high_map(i, order_ref, shift_ref):
        return (jnp.maximum(i - steps // 2, 0), 0)

    maps = {"rows": rows_map, "low": low_map, "high": high_map}

    def out_spec(shape, kind):
        if kind == "one":
            return pl.BlockSpec(shape, fixed_map)
        return pl.BlockSpec((tile, shape[1]), maps[kind])

    return pl.pallas_call(
        whole,
        grid_spec=pltpu.PrefetchScalarGridSpec(
            num_scalar_prefetch=2,
            grid=(steps,),
            in_specs=[pl.BlockSpec((tile, arg.shape[1]), rows_map) for arg in row_args]
            + [pl.BlockSpec(arg.shape, fixed_map) for arg in fixed_args]
            + [pl.BlockSpec(memory_space=pl.ANY)] * sum(counts),
            out_specs=tuple(out_spec(shape, kind) for shape, _, kind in outs),
            scratch_shapes=[
                pltpu.VMEM((depth, sum(widths)), BF),
                pltpu.SemaphoreType.DMA((len(matrices), targets.shape[0])),
            ],
        ),
        out_shape=tuple(jax.ShapeDtypeStruct(shape, kind) for shape, kind, _ in outs),
        compiler_params=pltpu.CompilerParams(
            dimension_semantics=("arbitrary",), vmem_limit_bytes=VMEM
        ),
        cost_estimate=SMALL,
        name=name,
    )(targets, shift, *row_args, *fixed_args, *[part for parts, _, _ in matrices for part in parts])


NO_SHIFT = (0,)


def inner_product(normed, matrix, small):
    rows, depth = normed.shape
    width = matrix[0][0].shape[2]

    def body(row_refs, fixed_refs, held, out_refs, number):
        out_refs[0][...] = nn(row_refs[0][...], held[...])

        @pl.when(number == 0)
        def _():
            out_refs[1][...] = held[:, small : small + LANES]

    return gathered_call(
        body, 256, [normed], [], [matrix], jnp.array(NO_SHIFT, jnp.int32),
        [((rows, width), F32, "rows"), ((depth, LANES), BF, "one")], "inner_product",
    )


def gate_product(normed, y, matrix):
    rows, width = y.shape

    def body(row_refs, fixed_refs, held, out_refs, number):
        gate = nn(row_refs[0][...], held[...])
        out_refs[0][...] = gate
        gated = row_refs[1][...] * gate * sigmoid(gate)
        total = jnp.sum(gated * gated, axis=1, keepdims=True)
        out_refs[1][...] = jnp.broadcast_to(total, out_refs[1].shape)

    return gathered_call(
        body, 256, [normed, y], [], [matrix], jnp.array(NO_SHIFT, jnp.int32),
        [((rows, width), F32, "rows"), ((rows, LANES), F32, "rows")], "gate_product",
    )


def row_scales(squares_ref, others_ref, width):
    return lax.rsqrt((squares_ref[:, 0:1] + others_ref[:, 0:1]) / width + EPS)


def split_rows(value, number, steps, low_ref, high_ref):
    @pl.when(number < steps // 2)
    def _():
        low_ref[...] = value.astype(BF)

    @pl.when(number >= steps // 2)
    def _():
        high_ref[...] = value


def mixed_product(y, gate, squares, others, kern, matrix, shift, inner_all):
    rows, width = y.shape
    depth = sum(part.shape[0] * part.shape[1] for part in matrix[0][:4])
    tile = 256

    def body(row_refs, fixed_refs, held, out_refs, number):
        gate_now = row_refs[1][...]
        scale = row_scales(row_refs[2], row_refs[3], inner_all)
        scaled = row_refs[0][...] * gate_now * sigmoid(gate_now) * scale
        scaled = (scaled * fixed_refs[0][6:7, :width]).astype(BF)
        out_refs[0][...] = scaled
        mixed = nt(scaled, held[...])
        split_rows(mixed, number, rows // tile, out_refs[1], out_refs[2])

    return gathered_call(
        body, tile, [y, gate, squares, others], [kern], [matrix], shift,
        [
            ((rows, width), BF, "rows"), ((rows // 2, depth), BF, "low"),
            ((rows // 2, depth), F32, "high"),
        ],
        "mixed_product",
    )


def gate_back(d_mix, y, gate, squares, others, pulls, kern, matrix, cut_at, inner_all):
    rows, width = y.shape

    def body(row_refs, fixed_refs, held, out_refs, number):
        d_scaled = nn(row_refs[0][...], held[...])
        y_now, gate_now = row_refs[1][...], row_refs[2][...]
        scale = row_scales(row_refs[3], row_refs[4], inner_all)
        pull = scale * scale * row_refs[5][:, 0:1] / inner_all
        sig = sigmoid(gate_now)
        silu = gate_now * sig
        gated = y_now * silu
        scaled_in = d_scaled * scale
        d_gated = scaled_in * fixed_refs[0][6:7, :width] - gated * pull

        @pl.when(number == 0)
        def _():
            out_refs[3][...] = jnp.zeros(out_refs[3].shape, F32)

        out_refs[3][0:1, :] += jnp.sum(scaled_in * gated, axis=0, keepdims=True)
        out_refs[0][...] = d_gated * silu
        d_gate = (d_gated * y_now * sig * (1.0 + gate_now * (1.0 - sig))).astype(BF)
        out_refs[1][...] = d_gate[:, :cut_at]
        out_refs[2][...] = d_gate[:, cut_at:]

    return gathered_call(
        body, 256, [d_mix, y, gate, squares, others, pulls], [kern], [matrix],
        jnp.array(NO_SHIFT, jnp.int32),
        [
            ((rows, width), F32, "rows"), ((rows, cut_at), BF, "rows"),
            ((rows, width - cut_at), BF, "rows"), ((8, width), F32, "one"),
        ],
        "gate_back",
    )


def normed_back(grads, matrices, shift):
    rows = grads[0].shape[0]
    widths = [grad.shape[1] for grad in grads]
    depth = sum(part.shape[0] * part.shape[1] for part in matrices[0][0][:4])
    tile = 256

    def body(row_refs, fixed_refs, held, out_refs, number):
        total = None
        start = 0
        for ref, width in zip(row_refs, widths):
            term = nt(ref[...], held[:, start : start + width])
            total = term if total is None else total + term
            start += width
        split_rows(total, number, rows // tile, out_refs[0], out_refs[1])

    return gathered_call(
        body, tile, grads, [], matrices, shift,
        [((rows // 2, depth), BF, "low"), ((rows // 2, depth), F32, "high")], "normed_back",
    )


def rows_call(body, tile, row_args, fixed_args, outs, name):
    arrays = [arg if isinstance(arg, tuple) else (arg, None) for arg in row_args]
    rows = arrays[0][0].shape[-2]

    def spec(array, number):
        if number is None:
            return pl.BlockSpec((tile, array.shape[1]), lambda i: (i, 0))
        return pl.BlockSpec((None, tile, array.shape[2]), lambda i: (number, i, 0))

    return pl.pallas_call(
        body,
        grid=(rows // tile,),
        out_shape=tuple(jax.ShapeDtypeStruct(shape, kind) for shape, kind, _ in outs),
        in_specs=[spec(*item) for item in arrays]
        + [pl.BlockSpec(arg.shape, lambda i: (0, 0)) for arg in fixed_args],
        out_specs=tuple(
            pl.BlockSpec(shape, lambda i: (0, 0))
            if one
            else pl.BlockSpec((tile, shape[1]), lambda i: (i, 0))
            for shape, _, one in outs
        ),
        compiler_params=pltpu.CompilerParams(
            dimension_semantics=("arbitrary",), vmem_limit_bytes=VMEM
        ),
        cost_estimate=SMALL,
        name=name,
    )(*[array for array, _ in arrays], *fixed_args)


def columns_call(body, row_args, outs, name):
    arrays = [arg if isinstance(arg, tuple) else (arg, None) for arg in row_args]
    width = arrays[0][0].shape[-1]
    tile = width // 2

    def spec(array, number):
        if number is None:
            return pl.BlockSpec((array.shape[0], tile), lambda i: (0, i))
        return pl.BlockSpec((None, array.shape[1], tile), lambda i: (number, 0, i))

    return pl.pallas_call(
        body,
        grid=(width // tile,),
        out_shape=tuple(jax.ShapeDtypeStruct(shape, BF) for shape in outs),
        in_specs=[spec(*item) for item in arrays],
        out_specs=tuple(pl.BlockSpec((shape[0], tile), lambda i: (0, i)) for shape in outs),
        compiler_params=pltpu.CompilerParams(
            dimension_semantics=("arbitrary",), vmem_limit_bytes=VMEM
        ),
        cost_estimate=SMALL,
        name=name,
    )(*[array for array, _ in arrays])


def normed_rows(tokens, others, gain, core):
    rows, width = tokens.shape
    tile = 128

    def body(core_ref, mine_ref, other_ref, gain_ref, out_ref):
        for ref, spot in ((mine_ref, core_ref[0]), (other_ref, 1 - core_ref[0])):
            values = ref[...].astype(F32)
            out_ref[spot] = (values * norm_rows(values) * gain_ref[...]).astype(BF)

    by_rows = pl.BlockSpec((tile, width), lambda i: (i, 0))
    return pl.pallas_call(
        body,
        grid=(rows // tile,),
        out_shape=jax.ShapeDtypeStruct((2, rows, width), BF),
        in_specs=[
            pl.BlockSpec(memory_space=pltpu.SMEM), by_rows, by_rows,
            pl.BlockSpec((1, width), lambda i: (0, 0)),
        ],
        out_specs=pl.BlockSpec((2, tile, width), lambda i: (0, i, 0)),
        compiler_params=pltpu.CompilerParams(
            dimension_semantics=("arbitrary",), vmem_limit_bytes=VMEM
        ),
        cost_estimate=SMALL,
        name="normed_rows",
    )(core, tokens, others, gain).reshape(2 * rows, width)


def marked_rows(grad_out, routes, core, first_lane):
    rows, width = grad_out.shape
    tile = 256

    def body(core_ref, grad_ref, routes_ref, out_ref):
        out_ref[:, :width] = grad_ref[...]
        lane = lax.broadcasted_iota(jnp.int32, (tile, LANES), 1)
        start = pl.multiple_of(core_ref[0] * rows + pl.program_id(0) * tile, tile)
        named = routes_ref[pl.ds(start, tile), :]
        marks = jnp.zeros(lane.shape, F32)
        for number in range(routes_ref.shape[1]):
            marks = jnp.where(lane == named[:, number : number + 1] + first_lane, 1.0, marks)
        out_ref[:, width:] = marks.astype(BF)

    return pl.pallas_call(
        body,
        grid=(rows // tile,),
        out_shape=jax.ShapeDtypeStruct((rows, width + LANES), BF),
        in_specs=[
            pl.BlockSpec(memory_space=pltpu.SMEM),
            pl.BlockSpec((tile, width), lambda i: (i, 0)),
            pl.BlockSpec(routes.shape, lambda i: (0, 0)),
        ],
        out_specs=pl.BlockSpec((tile, width + LANES), lambda i: (i, 0)),
        compiler_params=pltpu.CompilerParams(
            dimension_semantics=("arbitrary",), vmem_limit_bytes=VMEM
        ),
        cost_estimate=SMALL,
        name="marked_rows",
    )(core, grad_out, routes)


def prepare_params(conv_w, conv_b, norm_gain, d_skip, dt_bias, a_log, core, local, heads):
    wide = conv_w.shape[1]
    both = norm_gain.shape[1]

    def body(core_ref, w_ref, b_ref, gain_ref, skip_ref, bias_ref, log_ref, kern_ref, head_ref, spread_ref):
        row = lax.broadcasted_iota(jnp.int32, (LANES, local), 0)
        column = lax.broadcasted_iota(jnp.int32, (LANES, local), 1)
        head = jnp.where(row >= LANES // 2, row - LANES // 2, row)
        low = head * P_SIZE
        spread = jnp.where((column >= low) & (column < low + P_SIZE), 1.0, 0.0).astype(BF)
        spread_ref[...] = spread
        first = core_ref[0] == 0

        def mine(ref):
            return jnp.where(first, ref[:, :heads], ref[:, heads : 2 * heads])

        kern_ref[...] = jnp.zeros(kern_ref.shape, F32)
        spot = pl.ds(pl.multiple_of(core_ref[0] * local, LANES), local)
        kern_ref[0:4, :local] = w_ref[:, spot]
        kern_ref[0:4, local + LANES :] = w_ref[:, both:]
        kern_ref[4:5, :local] = b_ref[:, spot]
        kern_ref[4:5, local + LANES :] = b_ref[:, both:]
        head_ref[...] = jnp.zeros(head_ref.shape, F32)
        head_ref[2:3, :heads] = mine(skip_ref)
        kern_ref[5:6, :local] = spread_heads(head_ref[...], spread)[2:3]
        kern_ref[6:7, :local] = gain_ref[:, spot]
        head_ref[0:1, :heads] = mine(bias_ref)
        head_ref[1:2, :heads] = jnp.exp(mine(log_ref))

    return small_call(
        body,
        [((8, local + LANES + wide - both), F32), ((8, LANES), F32), ((LANES, local), BF)],
        [core, conv_w, conv_b, norm_gain, d_skip, dt_bias, a_log], "prepare_params", 1,
    )


def mid_rows_of(mixed, others, tokens, gain):
    rows, width = tokens.shape

    def body(mixed_ref, other_ref, tokens_ref, gain_ref, resid_ref, mid_ref):
        resid = tokens_ref[...].astype(F32) + mixed_ref[...] + other_ref[...].astype(F32)
        resid_ref[...] = resid
        mid_ref[...] = (resid * norm_rows(resid) * gain_ref[...]).astype(BF)

    return rows_call(
        body, 256, [mixed, others, tokens], [gain],
        [((rows, width), F32, False), ((rows, width), BF, False)], "mid_rows",
    )


def across_sum(mine, came, number):
    _, rows, width = mine.shape
    cut = rows // 2

    def body(mine_ref, came_ref, low_ref, high_ref):
        total = (mine_ref[...].astype(F32) + came_ref[...].astype(F32)).astype(BF)
        low_ref[...] = total[:cut]
        high_ref[...] = total[cut:]

    return columns_call(
        body, [(mine, number), (came, number)], [(cut, width)] * 2, "across_sum"
    )


def side_sums(mine, came, over_x, over_y):
    _, rows, width = mine.shape
    cut = rows // 2

    def body(mine_x, came_x, mine_y, came_y, over_x_ref, over_y_ref, x_ref, y_ref):
        to_x = mine_x[...].astype(F32) + came_x[...].astype(F32)
        x_ref[:cut] = to_x[:cut].astype(BF)
        x_ref[cut:] = (to_x[cut:] + over_y_ref[...].astype(F32)).astype(BF)
        to_y = mine_y[...].astype(F32) + came_y[...].astype(F32)
        y_ref[:cut] = (to_y[:cut] + over_x_ref[...].astype(F32)).astype(BF)
        y_ref[cut:] = to_y[cut:].astype(BF)

    return columns_call(
        body, [(mine, 0), (came, 0), (mine, 1), (came, 1), over_x, over_y],
        [(rows, width)] * 2, "side_sums",
    )


def own_sum(mine_ref, came_ref, x_ref, y_ref):
    return (
        mine_ref[...].astype(F32) + came_ref[...].astype(F32)
        + x_ref[...].astype(F32) + y_ref[...].astype(F32)
    )


def norm_back(d_rows, values, gain, grad_ref):
    scale = norm_rows(values)

    @pl.when(pl.program_id(0) == 0)
    def _():
        grad_ref[...] = jnp.zeros(grad_ref.shape, F32)

    grad_ref[0:1, :] += jnp.sum(d_rows * values * scale, axis=0, keepdims=True)
    pulled = d_rows * gain
    mean = jnp.mean(values * pulled, axis=-1, keepdims=True)
    return scale * pulled - values * (scale * scale * scale) * mean


def resid_back(mine, came, from_x, from_y, resid, tokens, grad_out, gain):
    rows, width = tokens.shape

    def body(
        mine_ref, came_ref, x_ref, y_ref, resid_ref, tokens_ref, grad_ref, gain_ref,
        d_resid_ref, d_mix_ref, pulls_ref, gain_grad_ref,
    ):
        resid_now = resid_ref[...]
        d_mid = own_sum(mine_ref, came_ref, x_ref, y_ref)
        d_extra = norm_back(d_mid, resid_now, gain_ref[...], gain_grad_ref)
        d_resid = grad_ref[...].astype(F32) + d_extra
        d_resid_ref[...] = d_resid
        d_mix = d_resid.astype(BF)
        d_mix_ref[...] = d_mix
        mixed = resid_now - tokens_ref[...].astype(F32)
        pull = jnp.sum(d_mix.astype(F32) * mixed, axis=1, keepdims=True)
        pulls_ref[...] = jnp.broadcast_to(pull, pulls_ref.shape)

    return rows_call(
        body, 256, [(mine, 0), (came, 0), from_x, from_y, resid, tokens, grad_out], [gain],
        [
            ((rows, width), F32, False), ((rows, width), BF, False),
            ((rows, LANES), F32, False), ((8, width), F32, True),
        ],
        "resid_back",
    )


def output_rows(mine, came, from_x, from_y, resid):
    def body(mine_ref, came_ref, x_ref, y_ref, resid_ref, out_ref):
        out_ref[...] = (resid_ref[...] + own_sum(mine_ref, came_ref, x_ref, y_ref)).astype(BF)

    return rows_call(
        body, 256, [(mine, 0), (came, 0), from_x, from_y, resid], [], [(resid.shape, BF, False)],
        "output_rows",
    )[0]


def tokens_back(mine, came, tokens, d_resid, gain):
    rows, width = tokens.shape

    def body(mine_ref, came_ref, tokens_ref, d_resid_ref, gain_ref, out_ref, gain_grad_ref):
        d_rows = mine_ref[...] + came_ref[...].astype(F32)
        d_extra = norm_back(d_rows, tokens_ref[...].astype(F32), gain_ref[...], gain_grad_ref)
        out_ref[...] = (d_resid_ref[...] + d_extra).astype(BF)

    return rows_call(
        body, 256, [mine, came, tokens, d_resid], [gain],
        [((rows, width), BF, False), ((8, width), F32, True)], "tokens_back",
    )


def pack_small(par_grads, head_grads, gain_grads, mid_gains, in_gains, spread, core, local, heads):
    width_d = in_gains.shape[1]
    both = 2 * local
    rest = par_grads.shape[1] - local - LANES

    def body(core_ref, par_ref, head_ref, gain_ref, mid_ref, in_ref, spread_ref, out_ref):
        out_ref[...] = jnp.zeros(out_ref.shape, F32)
        spot = pl.ds(pl.multiple_of(core_ref[0] * local, LANES), local)
        out_ref[0:5, spot] = par_ref[0:5, :local]
        out_ref[0:5, both:] = par_ref[0:5, local + LANES :]
        out_ref[5:6, spot] = gain_ref[0:1, :]
        out_ref[6:7, :width_d] = in_ref[0:1, :]
        out_ref[6:7, width_d : 2 * width_d] = mid_ref[0:1, :]
        lane = lax.broadcasted_iota(jnp.int32, (8, LANES), 1)
        skip = gather_heads(par_ref[:, :local], spread_ref[...], lane < heads)
        for number, row in enumerate((head_ref[0:1], head_ref[1:2], skip[5:6])):
            start = pl.multiple_of((2 * number + core_ref[0]) * LANES, LANES)
            out_ref[7:8, pl.ds(start, LANES)] = row

    return small_call(
        body, [((8, both + rest), F32)],
        [core, par_grads, head_grads, gain_grads, mid_gains, in_gains, spread], "pack_small", 1,
    )[0]


def out_outputs(og_sums, cut):
    height = og_sums.shape[0]

    def body(sums_ref, out_ref):
        out_ref[:cut, :] = sums_ref[:, :cut].T
        out_ref[cut:, :] = sums_ref[:, 2 * cut : 3 * cut].T

    return small_call(body, [((2 * cut, height), F32)], [og_sums], "out_outputs")[0]


def inner_outputs(og_sums, in_sums, core, local, heads, cut):
    height = in_sums.shape[0]
    half = height // 2
    if height % 32:
        gate = jnp.concatenate([og_sums[:, cut : 2 * cut], og_sums[:, 3 * cut :]], axis=1)
        joint = in_sums[:, local:].reshape(2, half, -1)
        return (
            jnp.stack([gate, in_sums[:, :local]], axis=1), in_sums[:, local : local + heads],
            pick(joint, core[0]), pick(joint, 1 - core[0]),
        )

    def body(core_ref, og_ref, in_ref, zx_ref, dt_ref, mine_ref, sent_ref):
        zx_ref[:, 0, :cut] = og_ref[:, cut : 2 * cut]
        zx_ref[:, 0, cut:] = og_ref[:, 3 * cut :]
        zx_ref[:, 1, :] = in_ref[:, :local]
        dt_ref[...] = in_ref[:, local : local + heads]
        for ref, spot in ((mine_ref, core_ref[0]), (sent_ref, 1 - core_ref[0])):
            ref[...] = in_ref[pl.ds(pl.multiple_of(spot * half, half), half), local:]

    rest = in_sums.shape[1] - local
    return small_call(
        body,
        [
            ((height, 2, local), F32), ((height, heads), F32), ((half, rest), F32),
            ((half, rest), F32),
        ],
        [core, og_sums, in_sums], "inner_outputs", 1,
    )


def unpack_experts(came, place, units, shared_units):
    height, width = came[0].shape
    hidden = width // 3
    own = EXPERTS // GROUP

    def body(place_ref, *refs):
        came_refs, (gu_ref, down_ref, sgu_ref, sdown_ref) = refs[:GROUP], refs[GROUP:]
        for k in range(GROUP):
            bit_0 = lax.rem(place_ref[0] + k % 2, 2)
            bit_1 = lax.rem(place_ref[0] // 2 + k // 2, 2)
            member = bit_0 + 2 * bit_1
            for e in range(own):
                expert = member * own + e
                for j in range(2):
                    start = j * hidden + e * units
                    gu_ref[expert, :, j, :] = came_refs[k][:, start : start + units].astype(F32)
                start = 2 * hidden + e * units
                down_ref[expert] = came_refs[k][:, start : start + units].astype(F32).T
            spot = pl.ds(pl.multiple_of(member * shared_units, shared_units), shared_units)
            for j in range(2):
                start = j * hidden + own * units
                sgu_ref[:, j, spot] = came_refs[k][:, start : start + shared_units].astype(F32)
            start = 2 * hidden + own * units
            sdown_ref[spot, :] = came_refs[k][:, start : start + shared_units].astype(F32).T

    return pl.pallas_call(
        body,
        out_shape=(
            jax.ShapeDtypeStruct((EXPERTS, height, 2, units), F32),
            jax.ShapeDtypeStruct((EXPERTS, units, height), F32),
            jax.ShapeDtypeStruct((height, 2, GROUP * shared_units), F32),
            jax.ShapeDtypeStruct((GROUP * shared_units, height), F32),
        ),
        in_specs=[pl.BlockSpec(memory_space=pltpu.SMEM)]
        + [pl.BlockSpec(memory_space=pltpu.VMEM)] * GROUP,
        out_specs=(pl.BlockSpec(memory_space=pltpu.VMEM),) * 4,
        compiler_params=pltpu.CompilerParams(vmem_limit_bytes=VMEM),
        cost_estimate=SMALL,
        name="unpack_experts",
    )(place, *came)


def expert_body(plan, *refs):
    own, units, shared, counts, part_count, aliased = plan
    hidden = own * units + shared
    refs = list(refs)

    def take(number):
        out = refs[:number]
        del refs[:number]
        return out

    order_ref, base_ref = take(2)
    x_pieces = [take(number) for number in counts]
    ym_pieces = [take(number) for number in counts]
    count = len(counts)
    (router_ref,) = take(1)
    part_refs = take(part_count)
    take(aliased)
    x_out, dy_out, gate_ref, up_ref, down_ref = take(5)
    out_mine, out_other, dx_mine, dx_other = take(4)
    w, sems, x_held, ym_held, row_sems = refs
    step = pl.program_id(0)
    width = router_ref.shape[0]

    def fetch(number):
        slot = number % 2
        copies = []
        for which, (parts, target) in enumerate(
            ((x_pieces[number], x_held), (ym_pieces[number], ym_held))
        ):
            start = 0
            for half, ref in enumerate(parts):
                rows = ref.shape[0]
                copies.append(
                    pltpu.make_async_copy(
                        ref, target.at[slot, start : start + rows], row_sems.at[which, slot, half]
                    )
                )
                start += rows
        return copies

    @pl.when(step == 0)
    def _():
        loads = load_pieces(order_ref, part_refs, [0] * part_count, w, 0, sems)
        for copy in fetch(0) + loads:
            copy.start()
        for copy in loads:
            copy.wait()

    for number in range(count):

        @pl.when(step == number)
        def _():
            if number + 1 < count:
                for copy in fetch(number + 1):
                    copy.start()
            for copy in fetch(number):
                copy.wait()

    slot = lax.rem(step, 2)
    x_now, ym_now = x_held.at[slot], ym_held.at[slot]
    x_out[...] = x_now[...]
    dy_out[...] = ym_now[:, :width]
    tile = x_now.shape[0]
    lane = lax.broadcasted_iota(jnp.int32, (tile, LANES), 1)
    routed = ym_now[:, width:].astype(F32) > 0.5
    logits = nn(x_now[...], router_ref[...])
    top = jnp.max(jnp.where(routed, logits, -1e30), axis=1, keepdims=True)
    powers = jnp.where(routed, jnp.exp(jnp.where(routed, logits - top, 0.0)), 0.0)
    gates = powers / jnp.sum(powers, axis=1, keepdims=True)
    d_gates = jnp.zeros((tile, LANES), F32)
    parts = [(e * units, units, e) for e in range(own)] + [(own * units, shared, None)]
    for start, size, expert in parts:
        cols = [slice(k * hidden + start, k * hidden + start + size) for k in range(3)]
        pre = nn(x_now[...], w[:, cols[0]])
        up = nn(x_now[...], w[:, cols[1]])
        d_act = nn(ym_now[:, :width], w[:, cols[2]])
        sig = sigmoid(pre)
        silu = pre * sig
        act = (silu * up).astype(BF).astype(F32)
        if expert is not None:
            here = lane == base_ref[0] + expert
            gate = jnp.sum(jnp.where(here, gates, 0.0), axis=1, keepdims=True)
            d_gate = jnp.sum(act * d_act, axis=1, keepdims=True)
            d_gates = jnp.where(here, d_gate, d_gates)
            d_act = d_act * gate
            act = act * gate
        gate_ref[:, cols[0]] = (d_act * up * sig * (1.0 + pre * (1.0 - sig))).astype(BF)
        up_ref[:, cols[0]] = (d_act * silu).astype(BF)
        down_ref[:, start : start + size] = act.astype(BF)
    mean = jnp.sum(gates * d_gates, axis=1, keepdims=True)
    d_logits = (gates * (d_gates - mean)).astype(BF)
    up_ref[:, hidden:] = d_logits
    cut = 256

    def results(out_ref, dx_ref):
        for number in range(width // cut):
            rows = slice(number * cut, (number + 1) * cut)
            out_ref[0, :, rows] = nt(down_ref[...], w[rows, 2 * hidden :]).astype(BF)
            d_x = nt(gate_ref[...], w[rows, :hidden])
            d_x = d_x + nt(up_ref[:, :hidden], w[rows, hidden : 2 * hidden])
            dx_ref[0, :, rows] = (d_x + nt(d_logits, router_ref[rows, :])).astype(BF)

    @pl.when(slot == 0)
    def _():
        results(out_mine, dx_mine)

    @pl.when(slot == 1)
    def _():
        results(out_other, dx_other)


def expert_rows(members, x_pieces, ym_pieces, held, base, router, parts, targets, units, shared):
    low, count = members[0], len(members)
    width = router.shape[0]
    x_pieces = [item if isinstance(item, tuple) else (item,) for item in x_pieces]
    ym_pieces = [item if isinstance(item, tuple) else (item,) for item in ym_pieces]
    tile = sum(part.shape[0] for part in x_pieces[0])
    counts = [len(item) for item in x_pieces]
    rows = 2 * GROUP * tile
    steps = 2 * count
    own = EXPERTS // GROUP
    hidden = own * units + shared

    def like(columns):
        spec = pl.BlockSpec((tile, columns), lambda i: (i + 2 * low, 0))
        return jax.ShapeDtypeStruct((rows, columns), BF), spec

    result = (
        jax.ShapeDtypeStruct((count, tile, width), BF),
        pl.BlockSpec((1, tile, width), lambda i: (i // 2, 0, 0)),
    )
    outs = [like(columns) for columns in (width, width, hidden, hidden + LANES, hidden)]
    outs += [result] * 4
    any_ref = pl.BlockSpec(memory_space=pl.ANY)
    flat = [part for item in x_pieces + ym_pieces for part in item]
    args = [targets, base, *flat, router, *parts, *held]
    specs = [pl.BlockSpec(memory_space=pltpu.SMEM)] * 2 + [any_ref] * len(flat)
    specs += [pl.BlockSpec(router.shape, lambda i: (0, 0))]
    specs += [any_ref] * (len(parts) + len(held))
    aliases = {len(args) - len(held) + i: i for i in range(len(held))}
    done = pl.pallas_call(
        functools.partial(
            expert_body, (own, units, shared, counts, len(parts), len(held))
        ),
        grid=(steps,),
        out_shape=tuple(shape for shape, _ in outs),
        in_specs=specs,
        out_specs=tuple(spec for _, spec in outs),
        scratch_shapes=[
            pltpu.VMEM((width, 3 * hidden), BF), pltpu.SemaphoreType.DMA((targets.shape[0],)),
            pltpu.VMEM((2, tile, width), BF), pltpu.VMEM((2, tile, width + LANES), BF),
            pltpu.SemaphoreType.DMA((2, 2, 2)),
        ],
        input_output_aliases=aliases,
        compiler_params=pltpu.CompilerParams(
            dimension_semantics=("arbitrary",), vmem_limit_bytes=VMEM
        ),
        cost_estimate=SMALL,
        name="expert_rows",
    )(*args)
    return list(done[:5]), list(done[5:])


def shards(
    tokens, routes, gain_in, w_zx, w_dt, w_bc, conv_w, conv_b, dt_bias, a_log, d_skip, norm_gain,
    w_out, gain_mid, router, shared_gu, shared_down, expert_gu, expert_down, grad_out,
):
    core = lax.axis_index("tensor")
    me = lax.axis_index("dp")
    lines = lax.axis_size("dp") // GROUP
    line, place = me // GROUP, lax.rem(me, GROUP)
    piece, width_d = tokens.shape
    local = w_zx.shape[2]
    heads = w_dt.shape[1]
    units = expert_gu.shape[3]
    own = EXPERTS // GROUP
    inner_all = norm_gain.shape[0]
    height = w_zx.shape[0]
    cut_in, cut_gate = 2 * local // 3, local // 2
    third = (lines - 1 + 2) // 3
    place_now = place.reshape(1)
    where = jnp.stack([place, line]).astype(jnp.int32)
    base = (heads + own * place).reshape(1)
    tiles = 4
    mine_last = (tiles // 2 * (1 - core)).reshape(1).astype(jnp.int32)

    lines_back = lax.rem(line - jnp.arange(lines, dtype=jnp.int32) + lines, lines)
    members = place ^ jnp.arange(GROUP, dtype=jnp.int32)
    pieces = jnp.concatenate([members, members[3:]])
    mixer_targets = (pieces[:, None] + GROUP * lines_back[None, :]).reshape(-1)
    expert_targets = (members[None, :] + GROUP * lines_back[:, None]).reshape(-1)
    order = Order()

    core_now = core.reshape(1)
    gain_in, gain_mid, conv_b, norm_gain = gain_in[None], gain_mid[None], conv_b[None], norm_gain[None]
    d_skip, dt_bias, a_log = d_skip[None], dt_bias[None], a_log[None]
    joint = jnp.concatenate([w_bc, router], axis=1)
    joint_came = swap(joint)
    ring_a = [w_zx[:, 1, :cut_in]]
    tokens_other = swap(tokens)
    order.set(ring_a[0], joint)
    joint = in_order(joint, order(joint_came), core)
    bc_cols, router_cols = joint[:, : 2 * NS], joint[:, 2 * NS :]
    pad = jnp.zeros((height, LANES - heads - EXPERTS), BF)
    ring_b = [jnp.concatenate([w_zx[:, 1, cut_in:], w_dt, router_cols, pad, bc_cols], axis=1)]
    order.set(ring_b[0])
    ring_on(ring_a, order, 1, 1 + third, lines)
    order.set(ring_a[-1])
    shared_units = shared_gu.shape[2] // GROUP
    hidden = own * units + shared_units
    gu = order(expert_gu).reshape(GROUP, own, height, 2, units).transpose(0, 2, 3, 1, 4)
    gu = gu.reshape(GROUP, height, 2, own * units)
    order.set(gu)
    ring_on(ring_b, order, 1, 1 + third, lines)
    ring_on(ring_a, order, 1 + third, 1 + 2 * third, lines)
    order.set(ring_a[-1], ring_b[-1])
    down = order(expert_down).reshape(GROUP, own, units, height).transpose(0, 3, 1, 2)
    down = down.reshape(GROUP, height, own * units)
    sgu = order(shared_gu).reshape(height, 2, GROUP, shared_units).transpose(2, 0, 1, 3)
    sdown = order(shared_down).reshape(GROUP, shared_units, height).transpose(0, 2, 1)
    order.set(
        down, sgu, sdown, gain_in, gain_mid, where, base, mine_last, place_now, core_now,
        mixer_targets, expert_targets,
    )
    ring_on(ring_b, order, 1 + third, 1 + 2 * third, lines)
    ring_on(ring_a, order, 1 + 2 * third, lines, lines)
    order.set(ring_a[-1], ring_b[-1])
    gu, sgu, down, sdown = order((gu, sgu, down, sdown))
    packed = jnp.concatenate([gu[:, :, 0], sgu[:, :, 0], gu[:, :, 1], sgu[:, :, 1], down, sdown], axis=2)
    to_send = [pick(packed, members[k]) for k in range(GROUP)]
    order.set(*to_send)
    came = to_send[:1] + [hop(to_send[k], k) for k in range(1, GROUP)]
    go_block = order(jnp.concatenate([w_zx[:, 0], w_out.T], axis=1))
    order.set(go_block)
    ring_on(ring_b, order, 1 + 2 * third, lines, lines)
    order.set(ring_a[-1], ring_b[-1])

    def matrix(parts, cut_at):
        return pieces_of(parts, mixer_targets, cut_at)

    def along_both(stacked):
        return [stacked, hop(stacked, 1), hop(stacked, 2)]

    def across_halves(parts, cut_at):
        width = parts[0].shape[2]
        low, high = cut_columns(parts[1], 0, cut_at), cut_columns(parts[2], cut_at, width - cut_at)
        order.set(low, high)
        return parts + [hop(low, 2), hop(high, 1)]

    go_ring = [order(go_block)]
    tokens_other = order.take(tokens_other)
    in_stack = stack_pairs(ring_a, ring_b)
    order.set(in_stack)
    ring_on(go_ring, order, 1, 1 + third, lines)
    order.set(go_ring[-1])
    came = order.take(*came)
    ring_on(go_ring, order, 1 + third, 1 + 2 * third, lines)
    order.set(go_ring[-1])
    in_w = along_both(order(in_stack))
    expert_ring = [stack_columns(order(came), 0, 3 * hidden)]
    marked = marked_rows(order(grad_out), routes, core_now, heads)
    normed = normed_rows(order(tokens), tokens_other, gain_in, core_now)
    kern, head_par, spread = prepare_params(
        order(conv_w), conv_b, norm_gain, d_skip, dt_bias, a_log, core_now, local, heads
    )
    order.set(normed, marked, expert_ring[0], kern)
    ring_on(go_ring, order, 1 + 2 * third, lines, lines)
    order.set(go_ring[-1])
    expert_ring[0] = order(expert_ring[0])
    in_w = list(order.take(*in_w))
    in_w = across_halves(in_w, cut_in)
    marked_other = order.take(swap(order(marked)))
    gate_stack = stack_columns(order(go_ring), 0, local)
    in_w = order.take(*in_w, gate_stack)
    gate_stack, in_w = in_w[-1], list(in_w[:-1])

    gate_w = along_both(gate_stack)
    in_matrix = matrix(in_w, cut_in)
    zi, router_w = inner_product(order(normed), in_matrix, local)
    order.set(zi)
    ring_on(expert_ring, order, 1, 1 + third, lines)
    order.set(expert_ring[-1])
    y, states = front_scan(order(zi), kern, head_par, spread)
    order.set(y)
    gate_w = list(order.take(*gate_w))
    gate_w = across_halves(gate_w, cut_gate)
    out_stack = stack_columns(order(go_ring), local, width_d)
    order.set(out_stack)
    gate_w = list(order.take(*gate_w))
    out_w = along_both(order(out_stack))
    gate_matrix = matrix(gate_w, cut_gate)
    gate, squares = gate_product(order(normed), y, gate_matrix)
    order.set(gate)
    squares_other = order.take(swap(squares))
    out_w = list(order.take(*out_w))
    ring_on(expert_ring, order, 1 + third, 1 + 2 * third, lines)
    order.set(expert_ring[-1])
    out_w = across_halves(out_w, cut_gate)
    out_w = list(order.take(*out_w))
    marked_sent = order(marked)
    marked_x, marked_y = hop(marked_sent, 1), hop(marked_sent, 2)
    out_matrix = matrix(out_w, cut_gate)
    scaled, mixed_sent, mixed_mine = mixed_product(
        order(y), gate, squares, squares_other, kern, out_matrix, mine_last, inner_all
    )
    order.set(mixed_mine)
    marked_x, marked_y = order.take(marked_x, marked_y)
    half_rows = piece // 2

    def halves_of(from_x, from_y):
        return cut_rows_of(from_x, 0, half_rows), cut_rows_of(from_y, half_rows, half_rows)

    def across(halves):
        return hop(halves[0], 2), hop(halves[1], 1)

    marked_halves = halves_of(marked_x, marked_y)
    order.set(*marked_halves)
    ring_on(expert_ring, order, 1 + 2 * third, lines, lines)
    order.set(expert_ring[-1])
    mixed_came = order.take(swap(order(mixed_sent)))
    resid, mid = mid_rows_of(mixed_mine, mixed_came, tokens, gain_mid)
    order.set(mid)

    mid_x, mid_y = hop(mid, 1), hop(mid, 2)
    mid_other = order.take(swap(mid))
    marked_swap_x, marked_swap_y = swap(order(marked_x)), swap(order(marked_y))
    parts, _, expert_order = pieces_of(expert_ring, expert_targets, 0)
    common = (base, router_w, parts, expert_order, units, shared_units)
    kept, result_0 = expert_rows(
        [0], [order(mid), mid_other], [marked, marked_other], [], *common
    )
    order.set(result_0[0])
    mid_x, mid_y, marked_swap_x, marked_swap_y = order.take(
        mid_x, mid_y, marked_swap_x, marked_swap_y
    )
    mid_halves = halves_of(mid_x, mid_y)
    order.set(*mid_halves)
    mid_swap_x, mid_swap_y = order.take(swap(mid_x), swap(mid_y))
    mid_d, marked_d = across(order(mid_halves)), across(order(marked_halves))
    kept, result = expert_rows(
        [1, 2], order([mid_x, mid_swap_x, mid_y, mid_swap_y]),
        [marked_x, marked_swap_x, marked_y, marked_swap_y], kept, *common,
    )
    order.set(result[0])
    mid_d = order.take(*mid_d)
    marked_d = order.take(*marked_d)
    mid_d_other = order.take(*[swap(item) for item in mid_d])
    marked_d_other = order.take(*[swap(item) for item in marked_d])
    d_others, d_other_0 = swap(order(result[3])), swap(order(result_0[3]))
    kept, result_3 = expert_rows(
        [3], [order(mid_d), mid_d_other], [marked_d, marked_d_other], kept, *common
    )
    order.set(result_3[0])
    x_all, dy_all, gate_acts, up_acts, down = kept
    d_others, d_other_0 = order.take(d_others, d_other_0)
    d_other_3 = order.take(swap(result_3[3]))
    over_low, over_high = across_sum(result_3[2], d_other_3, 0)
    order.set(over_low)
    d_over = hop(over_low, 1), hop(over_high, 2)
    out_others = swap(order(result_3[1])), swap(order(result[1])), swap(order(result_0[1]))

    grad_down = tn(order(dy_all), down, BF)
    order.set(grad_down)
    d_over = order.take(*d_over)
    out_other_3, out_others, out_other_0 = order.take(*out_others)
    to_x, to_y = side_sums(result[2], d_others, *d_over)
    order.set(to_x)
    arrays = {}

    def whole_block(name, width):
        return lambda line_at: [(width, [(arrays[name], 0, line_at)], None)]

    sums = LineSums(
        {name: whole_block(name, hidden) for name in ("gate", "up", "down")},
        order, lines, GROUP * height, where, ("gate", "up", "down"),
    )
    arrays["down"] = grad_down
    sums.start("down")
    d_came = hop(to_x, 1), hop(to_y, 2)
    out_over = across_sum(result_3[0], order(out_other_3), 0)
    order.set(out_over[0], sums.sent)
    out_over = hop(out_over[0], 1), hop(out_over[1], 2)
    arrays["gate"] = tn(order(x_all), gate_acts, BF)
    order.set(arrays["gate"])
    sums.run(third, "gate")
    order.set(sums.sent)
    arrays["up"] = tn(order(x_all), up_acts, BF)
    order.set(arrays["up"])
    d_came = order.take(*d_came)
    out_over = order.take(*out_over)
    out_sums = side_sums(result[0], out_others, *out_over)
    order.set(out_sums[0])
    out_came = hop(out_sums[0], 1), hop(out_sums[1], 2)

    d_resid, d_mix_mine, pulls, mid_gains = resid_back(
        result_0[2], d_other_0, *d_came, order(resid), tokens, grad_out, gain_mid
    )
    order.set(d_mix_mine)
    sums.run(third, "up")
    order.set(sums.sent)
    d_mix_came, pulls_came = order.take(swap(d_mix_mine), swap(pulls))
    d_mix, pulls = pair_rows([(d_mix_mine, order(d_mix_came)), (pulls, pulls_came)], core_now)
    order.set(d_mix)
    d_y, dz_a, dz_b, gain_grads = gate_back(
        order(d_mix), y, gate, squares, squares_other, pulls, kern, out_matrix, cut_gate, inner_all
    )
    order.set(d_y)

    def hop_first(pair, *before):
        sent = [item.start(order) for item in pair]
        order.set(*sent)
        for other in before:
            all_came(other)
        for item, values in zip(pair, sent):
            item.came = hop(order(values), item.bits)

    def hop_second(pair):
        for item in pair:
            item.came = order(item.came)
        sent = [item.turn() for item in pair]
        order.set(*sent)
        for item, values in zip(pair, sent):
            item.came_last = hop(values, 3 - item.bits)

    def all_came(pair):
        for item in pair:
            item.came_last = order(item.came_last)
        order.set(*[item.came_last for item in pair])

    grad_out_w = tn(order(d_mix), scaled, BF)
    normed_now = order(normed)
    grad_gate_a, grad_gate_b = tn(normed_now, dz_a, BF), tn(normed_now, dz_b, BF)
    order.set(grad_gate_a, grad_gate_b, grad_out_w)
    out_came = order.take(*out_came)
    og_pair = [
        Plane([(grad_out_w, 0, cut_gate), (grad_gate_a, 0, cut_gate)], 1, where, lines),
        Plane([(grad_out_w, 1, cut_gate), (grad_gate_b, 0, cut_gate)], 2, where, lines),
    ]
    hop_first(og_pair)
    output = output_rows(order(result_0[0]), out_other_0, *out_came, resid)
    order.set(output)
    sums.run(third)
    order.set(sums.sent)
    di_a, di_b, par_grads, head_grads = back_scan(
        order(d_y), zi, states, kern, head_par, spread, cut_in
    )
    order.set(di_a)
    hop_second(og_pair)
    grad_in_a = tn(order(normed), di_a, BF)
    start = local - cut_in
    grad_router = jnp.pad(
        order(arrays["up"][:, hidden:]).astype(F32),
        ((0, 0), (start, di_b.shape[1] - start - LANES)),
    )
    grad_in_b = (tn(order(normed), di_b) + grad_router).astype(BF)
    order.set(grad_in_a, grad_in_b)
    sums.run(third)
    order.set(sums.sent)
    in_pair = [
        Plane([(grad_in_a, 0, cut_in)], 1, where, lines),
        Plane([(grad_in_b, 0, grad_in_b.shape[1])], 2, where, lines),
    ]
    hop_first(in_pair, og_pair)

    def pair_groups(pair):
        return lambda line_at: [group for item in pair for group in item.groups(line_at)]

    rest = LineSums(
        {"og": pair_groups(og_pair), "in": pair_groups(in_pair)}, order, lines, height, where
    )
    rest.start("og")
    order.set(rest.sent)
    d_sent, d_mine = normed_back(
        order([dz_a, dz_b, di_a, di_b]), [gate_matrix, in_matrix], mine_last
    )
    order.set(d_mine)

    hop_second(in_pair)
    sums.run(third)
    order.set(sums.final["up"][0])
    rest.run(third)
    order.set(rest.sent)
    d_other = order.take(swap(order(d_sent)))
    grad_tokens, in_gains = tokens_back(d_mine, d_other, tokens, d_resid, gain_in)
    order.set(grad_tokens)
    small = pack_small(
        par_grads, head_grads, gain_grads, mid_gains, in_gains, spread, core_now, local, heads
    )
    order.set(small)
    all_came(in_pair)
    rest.run(third, "in")
    order.set(rest.sent)
    to_send = member_pieces(
        [
            (arrays[name], order(sums.final[name][0]), sums.final[name][1] // hidden, hidden)
            for name in ("gate", "up", "down")
        ],
        where, lines, height,
    )
    order.set(*to_send)
    came = to_send[:1] + [hop(order(to_send[k]), k) for k in range(1, GROUP)]
    small = sum_in_order([small, order(swap(small))], core_now, 2)
    order.set(small)
    small = sum_in_order([small] + order([hop(small, k) for k in range(1, GROUP)]), place_now, GROUP)
    order.set(small)
    bits = GROUP
    while bits < lines * GROUP:
        if 2 * bits < lines * GROUP:
            others = order([hop(small, k * bits) for k in range(1, 4)])
            small = sum_in_order([small] + others, (me // bits).reshape(1), 4)
            bits *= 4
        else:
            small = sum_in_order([small, order(hop(small, bits))], (me // bits).reshape(1), 2)
            bits *= 2
        order.set(small)
    rest.run(third)
    order.set(rest.sent)
    came = list(order.take(*came))
    g_egu, g_edown, g_sgu, g_sdown = unpack_experts(came, place_now, units, shared_units)
    order.set(g_edown)
    rest.run(third)
    order.set(rest.sent)
    g_out = out_outputs(order(rest.final["og"]), cut_gate)
    order.set(g_out)
    rest.run(third)
    order.set(rest.final["in"])
    g_zx, g_dt, joint_mine, joint_sent = inner_outputs(
        rest.final["og"], rest.final["in"], core_now, local, heads, cut_gate
    )
    joint = joint_mine + swap(joint_sent)
    g_router, g_bc = joint[:, heads : heads + EXPERTS], joint[:, LANES:]

    def of_heads(number):
        return jnp.concatenate(
            [
                small[7, (2 * number + which) * LANES : (2 * number + which) * LANES + heads]
                for which in range(2)
            ]
        )

    return (
        output, grad_tokens, small[6, :width_d], g_zx, g_dt, g_bc, small[:4],
        small[4], of_heads(0), of_heads(1), of_heads(2), small[5, :inner_all], g_out,
        small[6, width_d : 2 * width_d], g_router, g_sgu, g_sdown, g_egu, g_edown,
    )


def solution(mesh):
    both = P(("dp", "tensor"), None)
    rows = P("dp", None, "tensor")
    cols = P("tensor", "dp")
    return jax.shard_map(
        shards,
        mesh=mesh,
        in_specs=(
            both, P("dp", None), P(), rows, P("dp", "tensor"), both, P(), P(), P(), P(), P(), P(),
            cols, P(), both, rows, cols, P(None, "dp", None, "tensor"), P(None, "tensor", "dp"),
            both,
        ),
        out_specs=(
            both, both, P(), rows, P("dp", "tensor"), both, P(), P(), P(), P(), P(), P(),
            cols, P(), both, rows, cols, P(None, "dp", None, "tensor"), P(None, "tensor", "dp"),
        ),
        check_vma=False,
    )
```
